32 devices in a mesh: dp: 4 (over y, core), stream: 2 (over x), tensor: 4 (over z).
Axes of the slice: x: 2, y: 2, z: 4, core: 2. Of those that a mesh axis runs over, the one named last changes fastest.
Arguments:
- hidden_in: bfloat16 [2, 4096, 768], P('stream', 'dp'), may hold values from -6 to 6
- lengths: int32 [128], P('dp'), may hold values from 5 to 32
- image_features: bfloat16 [128, 257, 1408], P('dp'), may hold values from -6 to 6
- self_q: bfloat16 [768, 768], P(None, 'tensor'), may hold values from -0.21875 to 0.21875
- self_k: bfloat16 [768, 768], P(None, 'tensor'), may hold values from -0.21875 to 0.21875
- self_v: bfloat16 [768, 768], P(None, 'tensor'), may hold values from -0.21875 to 0.21875
- self_out: bfloat16 [768, 768], P(None, 'tensor'), may hold values from -0.625 to 0.625
- ln1_gain: float32 [768], replicated, may hold values from 0.1 to 1.9
- ln1_bias: float32 [768], replicated, may hold values from -0.5 to 0.5
- cross_q: bfloat16 [768, 768], P(None, 'tensor'), may hold values from -0.21875 to 0.21875
- cross_k: bfloat16 [1408, 768], P(None, 'tensor'), may hold values from -0.15625 to 0.15625
- cross_v: bfloat16 [1408, 768], P(None, 'tensor'), may hold values from -0.15625 to 0.15625
- cross_out: bfloat16 [768, 768], P(None, 'tensor'), may hold values from -0.875 to 0.875
- ln2_gain: float32 [768], replicated, may hold values from 0.1 to 1.9
- ln2_bias: float32 [768], replicated, may hold values from -0.5 to 0.5
- ffn_up: bfloat16 [2, 768, 3072], P('stream', None, 'tensor'), may hold values from -0.21875 to 0.21875
- ffn_down: bfloat16 [2, 768, 3072], P('stream', None, 'tensor'), may hold values from -0.109375 to 0.109375
- ln3_gain: float32 [2, 768], P('stream'), may hold values from 0.1 to 1.9
- ln3_bias: float32 [2, 768], P('stream'), may hold values from -0.5 to 0.5
- cotangent: bfloat16 [2, 4096, 768], P('stream', 'dp'), may hold values from -6 to 6
Outputs:
- hidden_out: bfloat16 [2, 4096, 768], P('stream', 'dp')
- grad_input: bfloat16 [2, 4096, 768], P('stream', 'dp')
- grad_self_q: float32 [768, 768], P(('dp', 'stream'), 'tensor')
- grad_self_k: float32 [768, 768], P(('dp', 'stream'), 'tensor')
- grad_self_v: float32 [768, 768], P(('dp', 'stream'), 'tensor')
- grad_self_out: float32 [768, 768], P(('dp', 'stream'), 'tensor')
- grad_ln1_gain: float32 [768], P(('dp', 'stream'))
- grad_ln1_bias: float32 [768], P(('dp', 'stream'))
- grad_cross_q: float32 [768, 768], P(('dp', 'stream'), 'tensor')
- grad_cross_k: float32 [1408, 768], P(('dp', 'stream'), 'tensor')
- grad_cross_v: float32 [1408, 768], P(('dp', 'stream'), 'tensor')
- grad_cross_out: float32 [768, 768], P(('dp', 'stream'), 'tensor')
- grad_ln2_gain: float32 [768], P(('dp', 'stream'))
- grad_ln2_bias: float32 [768], P(('dp', 'stream'))
- grad_ffn_up: float32 [2, 768, 3072], P('stream', 'dp', 'tensor')
- grad_ffn_down: float32 [2, 768, 3072], P('stream', 'dp', 'tensor')
- grad_ln3_gain: float32 [2, 768], P('stream', 'dp')
- grad_ln3_bias: float32 [2, 768], P('stream', 'dp')
The draws below stay inside these ranges and needn't reach their ends.
Inputs may be any that keep to these rules, and one draw needn't show every extreme that they name: lengths[i] is item i's caption length; its text slots from position lengths[i] on are padding.
All inputs are finite; a program needn't handle non-finite values.
Results may differ from the reference program's by a relative error of at most 0.02.
The reference program's roundings to bfloat16 on the way count: a program that leaves them out, or rounds other values in their place, can miss the bound.
Values may be sent and summed in bfloat16 or wider, within the bound.
No kernel may reach another device: no remote copies, remote signals or barrier semaphores. Data moves between devices by JAX's collectives and lax.ppermute only.
A program may use at most 256 MiB of HBM per device.

```python
import math
import jax
import jax.numpy as jnp
from jax import lax

D = 768
H = 12
HD = 64
FF = 3072
IMG_D = 1408
QN = 32
TXT = 32
IMG_T = 257
ITEMS = 128
ROWS = 4096


def with_ends(result, own_key, least, top_value):
    place = [jax.random.randint(jax.random.fold_in(own_key, axis), (), 0, length) for axis, length in enumerate(result.shape)]
    widest = result.shape.index(max(result.shape))
    next_to = place[:widest] + [(place[widest] + 1) % result.shape[widest]] + place[widest + 1:]
    return result.at[tuple(place)].set(least).at[tuple(next_to)].set(top_value)


def with_spikes(result, key, source, target, blocks, factor):
    def block_of(position):
        return (jnp.arange(result.shape[position]) // (result.shape[position] // blocks)).reshape((-1,) + (1,) * (result.ndim - 1 - position))

    one_side = jax.random.permutation(key, blocks)[block_of(target)]
    other_side = (block_of(target) + blocks // 2) % blocks
    return jnp.where((block_of(source) == one_side) | (block_of(source) == other_side), factor * result, result)


def block_scale(rng, shape, cuts, least, top_value):
    def one(axis_at, parts):
        draws = jax.random.uniform(jax.random.fold_in(jax.random.fold_in(rng, 6), axis_at), (parts,), jnp.float32, least / len(cuts), top_value / len(cuts))
        return jnp.repeat(jnp.exp(draws), shape[axis_at] // parts).reshape((-1,) + (1,) * (len(shape) - axis_at - 1))

    level = one(*cuts[0])
    for cut in cuts[1:]:
        level = level * one(*cut)
    return level


def normal_values(key, shape, width, reach, cuts=(), kind=jnp.bfloat16):
    drawn = width * jax.random.normal(key, shape, jnp.float32)
    if cuts:
        drawn = drawn * block_scale(key, shape, cuts, -0.22, 0.18)
    return jnp.clip(drawn, -reach, reach).astype(kind)


def bell_draw_with(key, extent, scale, most, cuts, heavy, held_as=jnp.bfloat16):
    result = scale * jax.random.normal(key, extent, jnp.float32)
    if cuts:
        result = result * block_scale(key, extent, cuts, -0.22, 0.18)
    return jnp.clip(with_spikes(result, jax.random.fold_in(key, 3), *heavy), -most, most).astype(held_as)


def setup_inputs(seed: int = 0) -> dict:
    streams_of = jax.random.split(jax.random.key(seed), 21)
    hidden_in = bell_draw_with(streams_of[0], (2, ROWS, D), 1.0, 6.0, ((0, 2), (1, 4)), (1, 2, 4, 2.0))
    lengths = with_ends(jax.random.randint(streams_of[1], (ITEMS,), 5, TXT + 1), jax.random.fold_in(streams_of[1], 1), 5, TXT).astype(jnp.int32)
    image_features = normal_values(streams_of[2], (ITEMS, IMG_T, IMG_D), 1.0, 6.0, ((0, 4),))
    self_q = normal_values(streams_of[3], (D, D), D ** -0.5, 0.21875, ((1, 4),))
    self_k = normal_values(streams_of[4], (D, D), D ** -0.5, 0.21875, ((1, 4),))
    self_v = normal_values(streams_of[5], (D, D), D ** -0.5, 0.21875, ((1, 4),))
    self_out = normal_values(streams_of[6], (D, D), (D // 8) ** -0.5, 0.625, ((1, 4),))
    ln1_gain = jnp.clip(1.0 + 0.18 * jax.random.normal(streams_of[7], (D,), jnp.float32), 0.1, 1.9)
    ln1_bias = jnp.clip(jax.random.uniform(streams_of[8], (D,), jnp.float32, -0.5, 0.5), -0.5, 0.5)
    cross_q = normal_values(streams_of[9], (D, D), D ** -0.5, 0.21875, ((1, 4),))
    cross_k = normal_values(streams_of[10], (IMG_D, D), IMG_D ** -0.5, 0.15625, ((1, 4),))
    cross_v = normal_values(streams_of[11], (IMG_D, D), IMG_D ** -0.5, 0.15625, ((1, 4),))
    cross_out = normal_values(streams_of[12], (D, D), (D // 16) ** -0.5, 0.875, ((1, 4),))
    ln2_gain = jnp.clip(1.0 + 0.18 * jax.random.normal(streams_of[13], (D,), jnp.float32), 0.1, 1.9)
    ln2_bias = jnp.clip(jax.random.uniform(streams_of[14], (D,), jnp.float32, -0.5, 0.5), -0.5, 0.5)
    ffn_up = normal_values(streams_of[15], (2, D, FF), D ** -0.5, 0.21875, ((0, 2), (2, 4)))
    ffn_down = normal_values(streams_of[16], (2, D, FF), FF ** -0.5, 0.109375, ((0, 2), (2, 4)))
    ln3_gain = jnp.clip(1.0 + 0.18 * jax.random.normal(streams_of[17], (2, D), jnp.float32), 0.1, 1.9)
    ln3_bias = jnp.clip(jax.random.uniform(streams_of[18], (2, D), jnp.float32, -0.5, 0.5) * block_scale(streams_of[18], (2, D), ((0, 2),), -0.4, 0.0), -0.5, 0.5)
    cotangent = normal_values(streams_of[19], (2, ROWS, D), 1.0, 6.0, ((0, 2), (1, 4)))
    return dict(hidden_in=hidden_in, lengths=lengths, image_features=image_features, self_q=self_q, self_k=self_k, self_v=self_v, self_out=self_out, ln1_gain=ln1_gain, ln1_bias=ln1_bias, cross_q=cross_q, cross_k=cross_k, cross_v=cross_v, cross_out=cross_out, ln2_gain=ln2_gain, ln2_bias=ln2_bias, ffn_up=ffn_up, ffn_down=ffn_down, ln3_gain=ln3_gain, ln3_bias=ln3_bias, cotangent=cotangent)


NORM_EPSILON = 1e-06
HIGHEST = lax.Precision.HIGHEST

@jax.custom_vjp
def low(v):
    return lax.optimization_barrier(v.astype(jnp.bfloat16)).astype(jnp.float32)

@jax.custom_vjp
def low_back(v):
    return v

def low_keep(v):
    return (low(v), None)

def low_pass(kept, grad):
    return (grad,)

def back_keep(v):
    return (v, None)

def back_low(kept, grad):
    return (low(grad),)
low.defvjp(low_keep, low_pass)
low_back.defvjp(back_keep, back_low)

def round_both(value):
    return low(low_back(value))

def project(value, matrix):
    return jnp.matmul(value, matrix, precision=HIGHEST)

def project_back(value, matrix):
    return jnp.matmul(value, matrix.T, precision=HIGHEST)

def layer_norm(value, gain, bias):
    center = value - lax.optimization_barrier(jnp.mean(value, axis=-1, keepdims=True))
    spread = lax.optimization_barrier(jnp.mean(center * center, axis=-1, keepdims=True))
    return center * lax.rsqrt(spread + NORM_EPSILON) * gain + bias

def attend(queries, keys, values, key_valid):
    scores = low_back(jnp.einsum('gqhe,gkhe->ghqk', queries, keys, precision=HIGHEST) * 0.125)
    if key_valid is not None:
        scores = jnp.where(key_valid[:, None, None, :], scores, -1e+30)
    row_peak = lax.optimization_barrier(jnp.max(scores, axis=-1, keepdims=True))
    weights = jnp.exp(scores - row_peak)
    softmax_out = weights / lax.optimization_barrier(jnp.sum(weights, axis=-1, keepdims=True))
    return round_both(jnp.einsum('ghqk,gkhe->gqhe', low(softmax_out), values, precision=HIGHEST))

def group_forward(params, hidden, image, spans):
    self_q, self_k, self_v, self_out, ln1_gain, ln1_bias, cross_q, cross_k, cross_v, cross_out, ln2_gain, ln2_bias, ffn_up, ffn_down, ln3_gain, ln3_bias = params
    group_size = spans.shape[0]
    split_heads = (2, group_size, QN, H, HD)
    queries = round_both(project(hidden, self_q)).reshape(split_heads)
    keys_all = round_both(project(hidden, self_k)).reshape(split_heads)
    values_all = round_both(project(hidden, self_v)).reshape(split_heads)
    keys_item = jnp.concatenate([keys_all[0], keys_all[1]], axis=1)
    values_item = jnp.concatenate([values_all[0], values_all[1]], axis=1)
    text_valid = lax.broadcasted_iota(jnp.int32, (group_size, TXT), 1) < spans[:, None].astype(jnp.int32)
    key_valid = jnp.concatenate([jnp.ones((group_size, QN), jnp.bool_), text_valid], axis=1)
    mixture = jnp.stack([attend(queries[0], keys_item, values_item, key_valid), attend(queries[1], keys_item, values_item, key_valid)]).reshape(2, group_size * QN, D)
    first = layer_norm(hidden + low_back(project_back(mixture, self_out)), ln1_gain, ln1_bias)
    cross_queries = round_both(project(low(first[0]), cross_q)).reshape(group_size, QN, H, HD)
    flat_image = image.reshape(group_size * IMG_T, IMG_D)
    image_keys = round_both(project(flat_image, cross_k)).reshape(group_size, IMG_T, H, HD)
    image_values = round_both(project(flat_image, cross_v)).reshape(group_size, IMG_T, H, HD)
    cross_mix = attend(cross_queries, image_keys, image_values, None).reshape(group_size * QN, D)
    second_query = layer_norm(first[0] + low_back(project_back(cross_mix, cross_out)), ln2_gain, ln2_bias)
    second = jnp.stack([second_query, first[1]])
    up_proj = low_back(jnp.einsum('srd,sdf->srf', low(second), ffn_up, precision=HIGHEST))
    activated = low(jax.nn.gelu(up_proj, approximate=False))
    down_proj = low_back(jnp.einsum('srf,sdf->srd', activated, ffn_down, precision=HIGHEST))
    return layer_norm(second + down_proj, ln3_gain[:, None, :], ln3_bias[:, None, :])

def reference(hidden_in, lengths, image_features, self_q, self_k, self_v, self_out, ln1_gain, ln1_bias, cross_q, cross_k, cross_v, cross_out, ln2_gain, ln2_bias, ffn_up, ffn_down, ln3_gain, ln3_bias, cotangent):
    group_size = math.gcd(ITEMS, 16)
    group_count = ITEMS // group_size
    params = tuple((matrix.astype(jnp.float32) for matrix in (self_q, self_k, self_v, self_out, ln1_gain, ln1_bias, cross_q, cross_k, cross_v, cross_out, ln2_gain, ln2_bias, ffn_up, ffn_down, ln3_gain, ln3_bias)))

    def split_rows(value):
        return value.astype(jnp.float32).reshape(2, group_count, group_size * QN, D).transpose(1, 0, 2, 3)

    def join_rows(value):
        return value.transpose(1, 0, 2, 3).reshape(2, ITEMS * QN, D)
    image_groups = image_features.reshape(group_count, group_size, IMG_T, IMG_D)
    span_groups = lengths.reshape(group_count, group_size)
    stepper = jax.checkpoint(group_forward)

    def whole_forward(weights, hidden):
        return lax.map(lambda pieces: stepper(weights, pieces[0], pieces[1].astype(jnp.float32), pieces[2]), (hidden, image_groups, span_groups))
    forward_out, pullback = jax.vjp(whole_forward, params, split_rows(hidden_in))
    grad_params, grad_hidden = pullback(split_rows(cotangent))
    grad_sq, grad_sk, grad_sv, grad_so, grad_g1, grad_b1, grad_cq, grad_ck, grad_cv, grad_co, grad_g2, grad_b2, grad_up, grad_down, grad_g3, grad_b3 = grad_params
    hidden_out = join_rows(forward_out).astype(jnp.bfloat16)
    grad_input = join_rows(grad_hidden).astype(jnp.bfloat16)
    return (hidden_out, grad_input, grad_sq, grad_sk, grad_sv, grad_so, grad_g1, grad_b1, grad_cq, grad_ck, grad_cv, grad_co, grad_g2, grad_b2, grad_up, grad_down, grad_g3, grad_b3)
```

```python
import functools

import jax
import jax.numpy as jnp
from jax import lax
from jax.experimental import pallas as pl
from jax.experimental.pallas import tpu as pltpu
from jax.sharding import Mesh, PartitionSpec as P

HD = 64
QUAD = 256
EPSILON = 1e-06
BF = jnp.bfloat16
F32 = jnp.float32
DP = ("node", "core")
SWAP = [(0, 1), (1, 0)]
SCALE = 0.125
NEG = -1e30


def nn(a, b):
    return lax.dot_general(a, b, (((1,), (0,)), ((), ())), preferred_element_type=F32)


def nt(a, b):
    return lax.dot_general(a, b, (((1,), (1,)), ((), ())), preferred_element_type=F32)


def tn(a, b):
    return lax.dot_general(a, b, (((0,), (0,)), ((), ())), preferred_element_type=F32)


def norm_stats(v):
    center = v - jnp.mean(v, axis=-1, keepdims=True)
    inverse = lax.rsqrt(jnp.mean(center * center, axis=-1, keepdims=True) + EPSILON)
    return center * inverse, inverse


def norm_back(e, normed, inverse, gain):
    scaled = e * gain
    out = inverse * (
        scaled
        - jnp.mean(scaled, axis=-1, keepdims=True)
        - normed * jnp.mean(scaled * normed, axis=-1, keepdims=True)
    )
    return out, jnp.sum(e * normed, axis=0, keepdims=True), jnp.sum(e, axis=0, keepdims=True)


def spread_heads(x):
    lane = lax.broadcasted_iota(jnp.int32, x.shape, 1) // HD
    zero = jnp.zeros_like(x)
    return jnp.concatenate([jnp.where(lane == j, x, zero) for j in range(QUAD // HD)], axis=0)


def collect_heads(x):
    rows = x.shape[0] * HD // QUAD
    lane = lax.broadcasted_iota(jnp.int32, (rows, QUAD), 1) // HD
    out = x[:rows]
    for j in range(1, QUAD // HD):
        out = jnp.where(lane == j, x[j * rows : (j + 1) * rows], out)
    return out


def softmax_keys(parts):
    peak = functools.reduce(jnp.maximum, [jnp.max(p, axis=0, keepdims=True) for p in parts])
    weights = [jnp.exp(p - peak) for p in parts]
    total = sum(jnp.sum(w, axis=0, keepdims=True) for w in weights)
    inverse = 1.0 / total
    return [w * inverse for w in weights]


def score_back(probs, grads):
    total = sum(jnp.sum(p * g, axis=0, keepdims=True) for p, g in zip(probs, grads))
    return [(p * (g - total)).astype(BF) for p, g in zip(probs, grads)]


def stack_rows(ref):
    value = ref[...]
    return value.reshape(-1, value.shape[-1])


def fetch(info, pieces, full, sems, where):
    node, core, stream, me = info[0], info[1], info[2], info[3]
    count = pieces[0].shape[0]
    copies = []
    for b, piece in enumerate(pieces):
        n = 1 - node if b & 1 else node
        s = 1 - stream if b & 2 else stream
        c = 1 - core if b & 4 else core
        for k in range(count):
            src = lax.rem(me - k + count, count)
            copies.append(pltpu.make_async_copy(piece.at[k], where(full, n, c, s, src), sems.at[b, k]))
    for copy in copies:
        copy.start()
    return copies


def place_self(full, n, c, s, t):
    return full.at[n * 2 + c, t, s]


def place_cross(full, n, c, s, t):
    return full.at[n, t, c * 2 + s]


def self_forward(
    info, spans, *refs, items, tokens
):
    pieces = refs[:8]
    (h_own, h_oth, gain, bias, q_own, k_own, v_own, q_oth, k_oth, v_oth, mix, first_sum, first, full, sems) = refs[8:]
    stream = info[2]
    copies = fetch(info, pieces, full, sems, place_self)
    for copy in copies:
        copy.wait()
    ho, hx = h_own[...], h_oth[...]
    for at, (own, oth) in enumerate(((q_own, q_oth), (k_own, k_oth), (v_own, v_oth))):
        weight = stack_rows(full.at[at])
        own[...] = nt(ho, weight).astype(BF)
        oth[...] = nt(hx, weight).astype(BF)

    width = ho.shape[1]

    def item(i, carry):
        rows = pl.ds(pl.multiple_of(i * tokens, tokens), tokens)
        valid = valid_keys(spans[i], stream, tokens, 4 * tokens)
        for u in range(width // QUAD):
            lanes = slice(u * QUAD, (u + 1) * QUAD)
            keys = jnp.concatenate([k_own[rows, lanes], k_oth[rows, lanes]], axis=0)
            values = jnp.concatenate([v_own[rows, lanes], v_oth[rows, lanes]], axis=0)
            scores = nt(keys, spread_heads(q_own[rows, lanes])) * SCALE
            (probs,) = softmax_keys([jnp.where(valid, scores, NEG)])
            mix[rows, lanes] = collect_heads(tn(probs.astype(BF), values)).astype(BF)
        return carry

    lax.fori_loop(0, items, item, 0)
    total = ho.astype(F32) + nn(mix[...], stack_rows(full.at[3]))
    first_sum[...] = total
    normed, _ = norm_stats(total)
    first[...] = normed * gain[...] + bias[...]


def valid_keys(span, stream, tokens, columns):
    row = lax.broadcasted_iota(jnp.int32, (2 * tokens, columns), 0)
    own_limit = jnp.where(stream == 0, tokens, span)
    oth_limit = jnp.where(stream == 0, span, tokens)
    return ((row < tokens) & (row < own_limit)) | ((row >= tokens) & (row - tokens < oth_limit))


def image_forward(info, *refs):
    pieces = refs[:8]
    x, x_last, keys, values, keys_last, values_last, full, sems = refs[8:]

    @pl.when(info[2] == 0)
    def _():
        @pl.when(pl.program_id(0) == 0)
        def _():
            copies = fetch(info, pieces, full, sems, place_cross)
            for copy in copies:
                copy.wait()
            keys_last[...] = nt(x_last[...], stack_rows(full.at[0])).astype(BF)
            values_last[...] = nt(x_last[...], stack_rows(full.at[1])).astype(BF)

        keys[...] = nt(x[...], stack_rows(full.at[0])).astype(BF)
        values[...] = nt(x[...], stack_rows(full.at[1])).astype(BF)


def last_row(i, shape):
    return lax.broadcasted_iota(jnp.int32, shape, 0) == i


def cross_forward(info, *refs, items, tokens, patches):
    pieces = refs[:8]
    (first, keys, values, keys_last, values_last, gain, bias, cross_q, cross_mix, second_sum, second, full, sems) = refs[8:]
    is_query = info[2] == 0

    @pl.when(jnp.logical_not(is_query))
    def _():
        second[...] = first[...]
        second_sum[...] = first[...]

    @pl.when(is_query)
    def _():
        copies = fetch(info, pieces, full, sems, place_cross)
        for copy in copies:
            copy.wait()
        base = first[...]
        width = base.shape[1]
        cross_q[...] = nt(base.astype(BF), stack_rows(full.at[0])).astype(BF)

        def item(i, carry):
            rows = pl.ds(pl.multiple_of(i * tokens, tokens), tokens)
            patch_rows = pl.ds(pl.multiple_of(i * patches, patches), patches)
            for u in range(width // QUAD):
                lanes = slice(u * QUAD, (u + 1) * QUAD)
                queries = spread_heads(cross_q[rows, lanes])
                scores = nt(keys[patch_rows, lanes], queries) * SCALE
                tail = nt(keys_last[:, lanes], queries) * SCALE
                tail = jnp.where(last_row(i, tail.shape), tail, NEG)
                probs, probs_tail = softmax_keys([scores, tail])
                out = tn(probs.astype(BF), values[patch_rows, lanes]) + tn(probs_tail.astype(BF), values_last[:, lanes])
                cross_mix[rows, lanes] = collect_heads(out).astype(BF)
            return carry

        lax.fori_loop(0, items, item, 0)
        total = base + nn(cross_mix[...], stack_rows(full.at[1]))
        second_sum[...] = total
        normed, _ = norm_stats(total)
        second[...] = normed * gain[...] + bias[...]


def ffn_both(second, weights, cot, gain, bias, out, grad_second, grads, vectors, full, ups, acts, sems):
    blocks, width = full.shape[0], second.shape[1]
    copies = [pltpu.make_async_copy(weights.at[:, t], full.at[t], sems.at[t]) for t in range(blocks)]
    for copy in copies:
        copy.start()
    x = second[...]
    low = x.astype(BF)
    total = x
    for t in range(blocks):
        copies[t].wait()
        both = stack_rows(full.at[t])
        up = nn(low, both[:width])
        act = (up * (0.5 * (1.0 + lax.erf(up * 0.7071067811865476)))).astype(BF)
        ups[t] = up
        acts[t] = act
        total = total + nt(act, both[width:])
    normed, inverse = norm_stats(total)
    out[...] = (normed * gain[...] + bias[...]).astype(BF)
    grad_third, grad_gain, grad_bias = norm_back(cot[...].astype(F32), normed, inverse, gain[...])
    vectors[...] = jnp.zeros_like(vectors)
    vectors[0:1] = grad_gain
    vectors[1:2] = grad_bias
    third_low = grad_third.astype(BF)
    shape = (grads.shape[0], grads.shape[3], grads.shape[4])
    back = grad_third
    for t in range(blocks):
        both = stack_rows(full.at[t])
        up = ups[t]
        grads[:, t, 1] = tn(third_low, acts[t]).astype(BF).reshape(shape)
        slope = 0.5 * (1.0 + lax.erf(up * 0.7071067811865476)) + up * (
            jnp.exp(-0.5 * up * up) * 0.3989422804014327
        )
        grad_up = (slope * nn(third_low, both[width:])).astype(BF)
        grads[:, t, 0] = tn(low, grad_up).astype(BF).reshape(shape)
        back = back + nt(grad_up, both[:width])
    grad_second[...] = back


def cross_backward(info, *refs, items, tokens, patches):
    pieces = refs[:8]
    (
        grad_second, second_sum, first, first_sum, cross_q, cross_mix, keys, values, keys_last, values_last, gain2, gain1,
        grads, grad_keys, grad_values, grad_keys_last, grad_values_last, grad_first_sum, first_grad_low, vectors,
        full, grad_mix, grad_q, sems,
    ) = refs[8:]
    is_query = info[2] == 0
    vectors[...] = jnp.zeros_like(vectors)

    def finish(grad_first):
        normed, inverse = norm_stats(first_sum[...])
        out, grad_gain, grad_bias = norm_back(grad_first, normed, inverse, gain1[...])
        vectors[0:1] = grad_gain
        vectors[1:2] = grad_bias
        grad_first_sum[...] = out
        first_grad_low[...] = out.astype(BF)

    @pl.when(jnp.logical_not(is_query))
    def _():
        grads[...] = jnp.zeros_like(grads)
        finish(grad_second[...])

    @pl.when(is_query)
    def _():
        copies = fetch(info, pieces, full, sems, place_cross)
        normed, inverse = norm_stats(second_sum[...])
        grad_cross, grad_gain, grad_bias = norm_back(grad_second[...], normed, inverse, gain2[...])
        vectors[2:3] = grad_gain
        vectors[3:4] = grad_bias
        low = grad_cross.astype(BF)
        width = low.shape[1]
        grads[1] = tn(low, cross_mix[...]).astype(BF)
        for copy in copies:
            copy.wait()
        grad_mix[...] = nt(low, stack_rows(full.at[1])).astype(BF)
        grad_keys_last[...] = jnp.zeros_like(grad_keys_last)
        grad_values_last[...] = jnp.zeros_like(grad_values_last)

        def item(i, carry):
            rows = pl.ds(pl.multiple_of(i * tokens, tokens), tokens)
            patch_rows = pl.ds(pl.multiple_of(i * patches, patches), patches)
            for u in range(width // QUAD):
                lanes = slice(u * QUAD, (u + 1) * QUAD)
                key, value = keys[patch_rows, lanes], values[patch_rows, lanes]
                key_last, value_last = keys_last[:, lanes], values_last[:, lanes]
                queries = spread_heads(cross_q[rows, lanes])
                pulls = spread_heads(grad_mix[rows, lanes])
                scores = nt(key, queries) * SCALE
                tail = nt(key_last, queries) * SCALE
                is_last = last_row(i, tail.shape)
                probs = softmax_keys([scores, jnp.where(is_last, tail, NEG)])
                back, back_tail = score_back(probs, [nt(value, pulls), nt(value_last, pulls)])
                grad_keys[patch_rows, lanes] = (nn(back, queries) * SCALE).astype(BF)
                grad_values[patch_rows, lanes] = nn(probs[0].astype(BF), pulls).astype(BF)
                grad_keys_last[:, lanes] += nn(back_tail, queries) * SCALE
                grad_values_last[:, lanes] += nn(probs[1].astype(BF), pulls)
                grad_q[rows, lanes] = (collect_heads(tn(back, key) + tn(back_tail, key_last)) * SCALE).astype(BF)
            return carry

        lax.fori_loop(0, items, item, 0)
        grad_cross_q = grad_q[...]
        grads[0] = tn(first[...].astype(BF), grad_cross_q).astype(BF)
        finish(grad_cross + nn(grad_cross_q, stack_rows(full.at[0])))


def image_backward(info, x, x_last, grad_kv, grad_last, out):
    is_query = info[2] == 0

    @pl.when(is_query)
    def _():
        out[...] = (tn(x[...], grad_kv[...]) + tn(x_last[...], grad_last[...].astype(BF))).astype(BF)

    @pl.when(jnp.logical_not(is_query))
    def _():
        out[...] = jnp.zeros_like(out)


def self_backward(info, spans, *refs, items, tokens):
    pieces = refs[:8]
    (
        h_own, low_own, low_oth, q_own, k_own, v_own, q_oth, k_oth, v_oth, mix, grad_first_sum,
        grads, grad_input, full, pull_own, pull_oth, grad_q, grad_k, grad_v, sems,
    ) = refs[8:]
    stream = info[2]
    copies = fetch(info, pieces, full, sems, place_self)
    for copy in copies:
        copy.wait()
    out_weight = stack_rows(full.at[3])
    pull_own[...] = nt(low_own[...], out_weight).astype(BF)
    pull_oth[...] = nt(low_oth[...], out_weight).astype(BF)
    width = h_own.shape[1]

    def item(i, carry):
        rows = pl.ds(pl.multiple_of(i * tokens, tokens), tokens)
        valid = valid_keys(spans[i], stream, tokens, 8 * tokens)
        for u in range(width // QUAD):
            lanes = slice(u * QUAD, (u + 1) * QUAD)
            keys = jnp.concatenate([k_own[rows, lanes], k_oth[rows, lanes]], axis=0)
            values = jnp.concatenate([v_own[rows, lanes], v_oth[rows, lanes]], axis=0)
            queries = jnp.concatenate([spread_heads(q_own[rows, lanes]), spread_heads(q_oth[rows, lanes])], axis=0)
            pulls = jnp.concatenate([spread_heads(pull_own[rows, lanes]), spread_heads(pull_oth[rows, lanes])], axis=0)
            scores = nt(keys, queries) * SCALE
            probs = softmax_keys([jnp.where(valid, scores, NEG)])
            (back,) = score_back(probs, [nt(values, pulls)])
            own_probs = probs[0].astype(BF)
            grad_k[rows, lanes] = (nn(back[:tokens], queries) * SCALE).astype(BF)
            grad_v[rows, lanes] = nn(own_probs[:tokens], pulls).astype(BF)
            grad_q[rows, lanes] = (collect_heads(tn(back[:, : 4 * tokens], keys)) * SCALE).astype(BF)
        return carry

    lax.fori_loop(0, items, item, 0)
    hidden = h_own[...]
    total = grad_first_sum[...]
    blocks, per = grads.shape[0], width // grads.shape[0]

    def write(at, value):
        value = value.astype(BF)
        for b in range(blocks):
            grads[b, at * per : (at + 1) * per, :] = value[b * per : (b + 1) * per]

    for at, ref in enumerate((grad_q, grad_k, grad_v)):
        value = ref[...]
        write(at, tn(hidden, value))
        total = total + nn(value, stack_rows(full.at[at]))
    write(3, tn(low_own[...], mix[...]))
    grad_input[...] = total.astype(BF)


VMEM = pl.BlockSpec(memory_space=pltpu.VMEM)
SMEM = pl.BlockSpec(memory_space=pltpu.SMEM)
ANY = pl.BlockSpec(memory_space=pl.ANY)


def shape(dims, kind):
    return jax.ShapeDtypeStruct(tuple(dims), kind)


def call(kernel, out_shapes, specs, scratch, flops, moved, **more):
    return pl.pallas_call(
        kernel,
        out_shape=out_shapes,
        in_specs=specs,
        out_specs=more.pop("out_specs", [VMEM] * len(out_shapes)),
        scratch_shapes=scratch,
        compiler_params=pltpu.CompilerParams(vmem_limit_bytes=56 * 1024 * 1024),
        cost_estimate=pl.CostEstimate(flops=int(flops), bytes_accessed=int(moved), transcendentals=0),
        **more,
    )


def pick(array, index, axis):
    return lax.dynamic_index_in_dim(array, index, axis, keepdims=False)


def around_tensor(block):
    count = lax.axis_size("tensor")
    parts = [block]
    for k in range(1, count):
        parts.append(lax.ppermute(block, "tensor", [(i, (i + k) % count) for i in range(count)]))
    return jnp.stack(parts)


def gather_pieces(pieces, one_way):
    nodes = lax.axis_size("node")
    core, stream = lax.axis_index("core"), lax.axis_index("stream")
    pieces = pick(pick(pieces, core, 1), stream, 1)
    if nodes == 2:
        node = lax.axis_index("node")
        base = around_tensor(pick(pieces, node, 0))
        there = lax.ppermute(base, "node", SWAP)
    else:
        base = around_tensor(pieces[0])
        there = around_tensor(pieces[1])
    four = [base, there]
    route = [(1, 0)] if one_way else SWAP
    four += [lax.ppermute(v, "stream", route) for v in four]
    return four + [lax.ppermute(v, "core", SWAP) for v in four]


def halve(array, axis_name, axis):
    me = lax.axis_index(axis_name)
    arrived = lax.ppermute(pick(array, 1 - me, axis), axis_name, SWAP)
    return (pick(array, me, axis).astype(F32) + arrived.astype(F32)).astype(BF)


def scatter_rows(grads):
    grads = halve(grads, "core", 1)
    grads = halve(grads, "stream", 1)
    if lax.axis_size("node") == 2:
        grads = halve(grads, "node", 0)
    else:
        grads = lax.psum_scatter(grads, "node", scatter_dimension=0, tiled=False)
    count, me = lax.axis_size("tensor"), lax.axis_index("tensor")
    rows, columns = grads.shape
    grads = grads.reshape(rows, count, columns // count).transpose(1, 0, 2)
    total = pick(grads, me, 0).astype(F32)
    for k in range(1, count):
        sent = pick(grads, lax.rem(me + k, count), 0)
        total += lax.ppermute(sent, "tensor", [(i, (i + k) % count) for i in range(count)]).astype(F32)
    return total


def shards(
    hidden_in, lengths, image_features, self_q, self_k, self_v, self_out, ln1_gain, ln1_bias,
    cross_q, cross_k, cross_v, cross_out, ln2_gain, ln2_bias, ffn_up, ffn_down, ln3_gain, ln3_bias, cotangent,
):
    nodes, streams, count = lax.axis_size("node"), lax.axis_size("stream"), lax.axis_size("tensor")
    node, core = lax.axis_index("node"), lax.axis_index("core")
    stream, me = lax.axis_index("stream"), lax.axis_index("tensor")
    devices = nodes * 2
    rows_all, width = hidden_in.shape[1:]
    local = self_q.shape[1]
    image_tokens, image_width = image_features.shape[1:]
    patches = image_tokens - 1
    items = lengths.shape[0] // count
    rows = rows_all // count
    tokens = rows // items
    info = jnp.stack([node if nodes == 2 else jnp.int32(0), core, stream, me]).astype(jnp.int32)

    self_pieces = jnp.stack([self_q.T, self_k.T, self_v.T, self_out.T]).reshape(2, 2, 2, local // 2, width)
    small_pieces = jnp.stack([cross_q.T, cross_out.T]).reshape(2, 2, 2, local // 4, width)
    image_pieces = jnp.stack([cross_k.T, cross_v.T]).reshape(2, 2, 2, local // 4, image_width)
    self_full = gather_pieces(self_pieces, False)
    image_full = gather_pieces(image_pieces, True)
    small_full = gather_pieces(small_pieces, True)
    ffn_rows = jnp.concatenate([ffn_up[0], ffn_down[0]], axis=0).reshape(devices, 2 * width // devices, ffn_up.shape[2])
    ffn_own = pick(ffn_rows, node * 2 + core, 0)
    ffn_full = lax.all_gather(ffn_own, ("node", "core", "tensor"), tiled=False)
    ffn_full = ffn_full.reshape((devices, count) + ffn_own.shape)

    h_own = lax.dynamic_slice_in_dim(hidden_in[0], me * rows, rows, 0)
    h_oth = lax.ppermute(h_own, "stream", SWAP)
    spans = lax.dynamic_slice_in_dim(lengths, me * items, items, 0)
    cot = lax.dynamic_slice_in_dim(cotangent[0], me * rows, rows, 0)
    image = lax.dynamic_slice_in_dim(image_features, me * items, items, 0)
    x = image[:, :patches].reshape(items * patches, image_width)
    x_last = image[:, patches]

    flops = 2 * rows * width * width
    wide = width * width * 2
    act_low, act = shape((rows, width), BF), shape((rows, width), F32)
    image_kv, image_kv_last = shape((items * patches, width), BF), shape((items, width), BF)
    dma = pltpu.SemaphoreType.DMA
    self_scratch = pltpu.VMEM((4, count, 2, local // 2, width), BF)
    small_scratch = pltpu.VMEM((2, count, 4, local // 4, width), BF)
    image_scratch = pltpu.VMEM((2, count, 4, local // 4, image_width), BF)
    row = lambda v: v.reshape(1, width)

    q_own, k_own, v_own, q_oth, k_oth, v_oth, mix, first_sum, first = call(
        functools.partial(self_forward, items=items, tokens=tokens),
        [act_low] * 7 + [act] * 2,
        [SMEM, SMEM] + [ANY] * 8 + [VMEM] * 4,
        [self_scratch, dma((8, count))],
        8 * flops, 4 * wide,
        name="self_forward",
    )(info, spans, *self_full, h_own, h_oth, row(ln1_gain), row(ln1_bias))

    image_flops = 4 * items * patches * width * image_width
    image_keys, image_values, keys_last, values_last = call(
        image_forward,
        [image_kv] * 2 + [image_kv_last] * 2,
        [SMEM] + [ANY] * 8 + [pl.BlockSpec((patches, image_width), lambda i: (i, 0)), pl.BlockSpec((items, image_width), lambda i: (0, 0))],
        [image_scratch, dma((8, count))],
        image_flops, 20e6,
        grid=(items,),
        out_specs=[pl.BlockSpec((patches, width), lambda i: (i, 0))] * 2 + [pl.BlockSpec((items, width), lambda i: (0, 0))] * 2,
        name="image_forward",
    )(info, *image_full, x, x_last)

    cross_queries, cross_mix, second_sum, second = call(
        functools.partial(cross_forward, items=items, tokens=tokens, patches=patches),
        [act_low] * 2 + [act] * 2,
        [SMEM] + [ANY] * 8 + [VMEM] * 7,
        [small_scratch, dma((8, count))],
        8 * flops, 12e6,
        name="cross_forward",
    )(info, *small_full, first, image_keys, image_values, keys_last, values_last, row(ln2_gain), row(ln2_bias))

    output, grad_second, ffn_grads, vectors3 = call(
        ffn_both,
        [act_low, act, shape((devices, count, 2, width // devices, width), BF), shape((8, width), F32)],
        [VMEM, ANY] + [VMEM] * 3,
        [
            pltpu.VMEM((count,) + (devices, 2 * width // devices, width), BF),
            pltpu.VMEM((count, rows, width), F32),
            pltpu.VMEM((count, rows, width), BF),
            dma((count,)),
        ],
        24 * flops, 20e6,
        name="ffn_both",
    )(second, ffn_full, cot, ln3_gain, ln3_bias)

    small_grads, grad_keys, grad_values, grad_keys_last, grad_values_last, grad_first_sum, low_own, vectors12 = call(
        functools.partial(cross_backward, items=items, tokens=tokens, patches=patches),
        [
            shape((2, width, width), BF), image_kv, image_kv, shape((items, width), F32), shape((items, width), F32),
            act, act_low, shape((8, width), F32),
        ],
        [SMEM] + [ANY] * 8 + [VMEM] * 12,
        [small_scratch, pltpu.VMEM((rows, width), BF), pltpu.VMEM((rows, width), BF), dma((8, count))],
        16 * flops, 24e6,
        name="cross_backward",
    )(
        info, *small_full, grad_second, second_sum, first, first_sum, cross_queries, cross_mix, image_keys, image_values,
        keys_last, values_last, row(ln2_gain), row(ln1_gain),
    )
    low_oth = lax.ppermute(low_own, "stream", SWAP)

    image_grads = [
        call(
            image_backward,
            [shape((image_width, width), BF)],
            [
                SMEM,
                pl.BlockSpec((items * patches, image_width), lambda i: (0, 0)),
                pl.BlockSpec((items, image_width), lambda i: (0, 0)),
                pl.BlockSpec((items * patches, QUAD), lambda i: (0, i)),
                pl.BlockSpec((items, QUAD), lambda i: (0, i)),
            ],
            [],
            image_flops / 2, 12e6,
            grid=(width // QUAD,),
            out_specs=[pl.BlockSpec((image_width, QUAD), lambda i: (0, i))],
            name="image_backward",
        )(info, x, x_last, grad, grad_last)[0]
        for grad, grad_last in ((grad_keys, grad_keys_last), (grad_values, grad_values_last))
    ]

    blocks = devices * streams
    per = width // blocks
    tail = 16
    self_grads, grad_input = call(
        functools.partial(self_backward, items=items, tokens=tokens),
        [shape((blocks, 4 * per + tail, width), BF), act_low],
        [SMEM, SMEM] + [ANY] * 8 + [VMEM] * 11,
        [self_scratch] + [pltpu.VMEM((rows, width), BF)] * 5 + [dma((8, count))],
        16 * flops, 12e6,
        name="self_backward",
    )(info, spans, *self_full, h_own, low_own, low_oth, q_own, k_own, v_own, q_oth, k_oth, v_oth, mix, grad_first_sum)

    ffn_sum = lax.psum_scatter(
        ffn_grads.reshape((devices * count,) + ffn_grads.shape[2:]), ("node", "core", "tensor"), scatter_dimension=0, tiled=False
    )
    ffn_sum = ffn_sum.astype(F32)
    split = lambda v, m: v.reshape(m, nodes, 2, streams, -1, width).transpose(1, 2, 3, 0, 4, 5)
    image_sum = scatter_rows(split(jnp.stack(image_grads), 2).reshape(nodes, 2, streams, -1, width))
    small_sum = scatter_rows(split(small_grads, 2).reshape(nodes, 2, streams, -1, width))

    shared = vectors12[:4].reshape(4, blocks, per).transpose(1, 0, 2)
    shared = jnp.pad(shared, ((0, 0), (0, 0), (0, width // count - per)))
    wide_per = width // devices
    halves = vectors3[:2].reshape(2, devices, wide_per).transpose(1, 0, 2)
    halves = jnp.stack([jnp.where(stream == s, halves, 0.0) for s in range(streams)], axis=1)
    halves = jnp.pad(halves.reshape(blocks, 2, wide_per), ((0, 0), (0, 0), (0, width // count - wide_per)))
    extra = jnp.pad(jnp.concatenate([shared, halves], axis=1), ((0, 0), (0, tail - 6), (0, 0)))
    extra = jnp.tile(extra, (1, 1, count)).astype(BF)
    self_grads = lax.dynamic_update_slice(self_grads, extra, (0, 4 * per, 0))
    self_sum = scatter_rows(self_grads.reshape(nodes, 2, streams, 4 * per + tail, width))

    every = lambda v: lax.all_gather(v, "tensor", tiled=True)[None]
    image_per = image_width // blocks
    vector = lambda r, n: self_sum[4 * per + r, :n]
    return (
        every(output),
        every(grad_input),
        self_sum[:per],
        self_sum[per : 2 * per],
        self_sum[2 * per : 3 * per],
        self_sum[3 * per : 4 * per],
        vector(0, per),
        vector(1, per),
        small_sum[:per],
        image_sum[:image_per],
        image_sum[image_per:],
        small_sum[per:],
        vector(2, per),
        vector(3, per),
        ffn_sum[0][None],
        ffn_sum[1][None],
        vector(4, wide_per)[None],
        vector(5, wide_per)[None],
    )


def solution(mesh):
    sizes = mesh.devices.shape
    fine = Mesh(mesh.devices.reshape(sizes[0] // 2, 2, *sizes[1:]), ("node", "core", "stream", "tensor"))
    weight = P(None, "tensor")
    in_specs = (
        P("stream", DP, None), P(DP), P(DP, None, None), weight, weight, weight, weight, P(), P(),
        weight, weight, weight, weight, P(), P(), P("stream", None, "tensor"), P("stream", None, "tensor"),
        P("stream", None), P("stream", None), P("stream", DP, None),
    )
    over = ("node", "core", "stream")
    square, flat = P(over, "tensor"), P(over)
    out_specs = (
        P("stream", DP, None), P("stream", DP, None), square, square, square, square, flat, flat,
        square, square, square, square, flat, flat, P("stream", DP, "tensor"), P("stream", DP, "tensor"),
        P("stream", DP), P("stream", DP),
    )
    return jax.shard_map(shards, mesh=fine, in_specs=in_specs, out_specs=out_specs, check_vma=False)
```

```python
import functools

import jax
import jax.numpy as jnp
from jax import lax
from jax.experimental import pallas as pl
from jax.experimental.pallas import tpu as pltpu
from jax.sharding import Mesh, PartitionSpec as P

HD = 64
QUAD = 256
EPSILON = 1e-06
BF = jnp.bfloat16
F32 = jnp.float32
DP = ("node", "core")
SWAP = [(0, 1), (1, 0)]
SCALE = 0.125
NEG = -1e30


def nn(a, b):
    return lax.dot_general(a, b, (((1,), (0,)), ((), ())), preferred_element_type=F32)


def nt(a, b):
    return lax.dot_general(a, b, (((1,), (1,)), ((), ())), preferred_element_type=F32)


def tn(a, b):
    return lax.dot_general(a, b, (((0,), (0,)), ((), ())), preferred_element_type=F32)


def norm_stats(v):
    center = v - jnp.mean(v, axis=-1, keepdims=True)
    inverse = lax.rsqrt(jnp.mean(center * center, axis=-1, keepdims=True) + EPSILON)
    return center * inverse, inverse


def norm_back(e, normed, inverse, gain):
    scaled = e * gain
    out = inverse * (
        scaled
        - jnp.mean(scaled, axis=-1, keepdims=True)
        - normed * jnp.mean(scaled * normed, axis=-1, keepdims=True)
    )
    return out, jnp.sum(e * normed, axis=0, keepdims=True), jnp.sum(e, axis=0, keepdims=True)


def spread_heads(x):
    lane = lax.broadcasted_iota(jnp.int32, x.shape, 1) // HD
    zero = jnp.zeros_like(x)
    return jnp.concatenate([jnp.where(lane == j, x, zero) for j in range(QUAD // HD)], axis=0)


def collect_heads(x):
    rows = x.shape[0] * HD // QUAD
    lane = lax.broadcasted_iota(jnp.int32, (rows, QUAD), 1) // HD
    out = x[:rows]
    for j in range(1, QUAD // HD):
        out = jnp.where(lane == j, x[j * rows : (j + 1) * rows], out)
    return out


def softmax_keys(parts):
    peak = functools.reduce(jnp.maximum, [jnp.max(p, axis=0, keepdims=True) for p in parts])
    weights = [jnp.exp(p - peak) for p in parts]
    total = sum(jnp.sum(w, axis=0, keepdims=True) for w in weights)
    inverse = 1.0 / total
    return [w * inverse for w in weights]


def score_back(probs, grads):
    total = sum(jnp.sum(p * g, axis=0, keepdims=True) for p, g in zip(probs, grads))
    return [(p * (g - total)).astype(BF) for p, g in zip(probs, grads)]


def stack_rows(ref):
    value = ref[...]
    return value.reshape(-1, value.shape[-1])


def doubling(count):
    order, bit = [0], count // 2
    while bit:
        order = order + [mask | bit for mask in order]
        bit //= 2
    return order


def fetch(info, pieces, full, sems, where, take=None):
    node, core, stream, me = info[0], info[1], info[2], info[3]
    count = pieces[0].shape[0]
    copies = []
    for b, piece in enumerate(pieces):
        n = 1 - node if b & 1 else node
        s = 1 - stream if b & 2 else stream
        c = 1 - core if b & 4 else core
        for k, mask in enumerate(doubling(count)):
            src = jnp.bitwise_xor(me, mask)
            block = piece.at[k] if take is None else piece.at[k, take]
            copies.append(pltpu.make_async_copy(block, where(full, n, c, s, src), sems.at[b, k]))
    for copy in copies:
        copy.start()
    return copies


def place_self(full, n, c, s, t):
    return full.at[n * 2 + c, t, s]


def place_cross(full, n, c, s, t):
    return full.at[n, t, c * 2 + s]


def forward(info, spans, *refs, items, tokens, patches):
    pieces = refs[:8]
    (
        h_own, h_oth, keys, values, keys_last, values_last, gain1, bias1, gain2, bias2,
        q_own, k_own, v_own, q_oth, k_oth, v_oth, mix, first_sum, first, cross_q, cross_mix, second_sum, second,
        full, small, sems, small_sems,
    ) = refs[8:]
    stream = info[2]
    copies = fetch(info, pieces, full, sems, place_self, pl.ds(0, full.shape[3]))
    later = fetch(info, pieces, small, small_sems, place_cross, pl.ds(full.shape[3], small.shape[3]))
    for copy in copies:
        copy.wait()
    ho, hx = h_own[...], h_oth[...]
    for at, (own, oth) in enumerate(((q_own, q_oth), (k_own, k_oth), (v_own, v_oth))):
        weight = stack_rows(full.at[at])
        own[...] = nt(ho, weight).astype(BF)
        oth[...] = nt(hx, weight).astype(BF)
    width = ho.shape[1]

    def item(i, carry):
        rows = pl.ds(pl.multiple_of(i * tokens, tokens), tokens)
        valid = valid_keys(spans[i], stream, tokens, 4 * tokens)
        for u in range(width // QUAD):
            lanes = slice(u * QUAD, (u + 1) * QUAD)
            near = jnp.concatenate([k_own[rows, lanes], k_oth[rows, lanes]], axis=0)
            mixed = jnp.concatenate([v_own[rows, lanes], v_oth[rows, lanes]], axis=0)
            scores = nt(near, spread_heads(q_own[rows, lanes])) * SCALE
            (probs,) = softmax_keys([jnp.where(valid, scores, NEG)])
            mix[rows, lanes] = collect_heads(tn(probs.astype(BF), mixed)).astype(BF)
        return carry

    lax.fori_loop(0, items, item, 0)
    total = ho.astype(F32) + nn(mix[...], stack_rows(full.at[3]))
    first_sum[...] = total
    normed, _ = norm_stats(total)
    base = normed * gain1[...] + bias1[...]
    first[...] = base
    for copy in later:
        copy.wait()

    @pl.when(stream != 0)
    def _():
        second[...] = base
        second_sum[...] = base

    @pl.when(stream == 0)
    def _():
        cross_q[...] = nt(base.astype(BF), stack_rows(small.at[0])).astype(BF)

        def cross_item(i, carry):
            rows = pl.ds(pl.multiple_of(i * tokens, tokens), tokens)
            patch_rows = pl.ds(pl.multiple_of(i * patches, patches), patches)
            for u in range(width // QUAD):
                lanes = slice(u * QUAD, (u + 1) * QUAD)
                queries = spread_heads(cross_q[rows, lanes])
                scores = nt(keys[patch_rows, lanes], queries) * SCALE
                tail = nt(keys_last[:, lanes], queries) * SCALE
                tail = jnp.where(last_row(i, tail.shape), tail, NEG)
                probs, probs_tail = softmax_keys([scores, tail])
                out = tn(probs.astype(BF), values[patch_rows, lanes]) + tn(probs_tail.astype(BF), values_last[:, lanes])
                cross_mix[rows, lanes] = collect_heads(out).astype(BF)
            return carry

        lax.fori_loop(0, items, cross_item, 0)
        total = base + nn(cross_mix[...], stack_rows(small.at[1]))
        second_sum[...] = total
        normed, _ = norm_stats(total)
        second[...] = normed * gain2[...] + bias2[...]


def valid_keys(span, stream, tokens, columns):
    row = lax.broadcasted_iota(jnp.int32, (2 * tokens, columns), 0)
    own_limit = jnp.where(stream == 0, tokens, span)
    oth_limit = jnp.where(stream == 0, span, tokens)
    return ((row < tokens) & (row < own_limit)) | ((row >= tokens) & (row - tokens < oth_limit))


def image_forward(info, *refs):
    pieces = refs[:8]
    x, x_last, keys, values, keys_last, values_last, full, sems = refs[8:]

    @pl.when(info[2] == 0)
    def _():
        @pl.when(pl.program_id(0) == 0)
        def _():
            copies = fetch(info, pieces, full, sems, place_cross)
            for copy in copies:
                copy.wait()
            keys_last[...] = nt(x_last[...], stack_rows(full.at[0])).astype(BF)
            values_last[...] = nt(x_last[...], stack_rows(full.at[1])).astype(BF)

        keys[...] = nt(x[...], stack_rows(full.at[0])).astype(BF)
        values[...] = nt(x[...], stack_rows(full.at[1])).astype(BF)


def last_row(i, shape):
    return lax.broadcasted_iota(jnp.int32, shape, 0) == i


def ffn_both(info, *refs, pieces, chunks):
    weights = [refs[q * pieces : (q + 1) * pieces] for q in range(chunks)]
    (
        second, cot, gain, bias, out, grad_second, vectors, keep_down, send_down, keep_up, send_up,
        full, ups, acts, stage, sems, out_sems,
    ) = refs[pieces * chunks :]
    node, core, me = info[0], info[1], info[3]
    blocks, width = full.shape[0], second.shape[1]
    nodes = keep_up.shape[0]
    copies = []
    for k, mask in enumerate(doubling(blocks)):
        src = jnp.bitwise_xor(me, mask)
        group = []
        for b in range(pieces):
            if pieces == 4:
                share = (1 - node if b & 1 else node) * 2 + (1 - core if b & 2 else core)
            else:
                share = 1 - core if b & 1 else core
            start = 0
            for q in range(chunks):
                size = weights[q][b].shape[1]
                place = full.at[src, share, pl.ds(start, size)]
                group.append(pltpu.make_async_copy(weights[q][b].at[k], place, sems.at[k, b, q]))
                start += size
        for copy in group:
            copy.start()
        copies.append(group)

    written = []

    def emit(slot, value, keep, send, t):
        stage[slot] = value.astype(BF).reshape(stage.shape[1:])
        for n in range(nodes):
            for half, target in enumerate((keep, send)):
                part = n * 2 + (1 - core if half else core)
                copy = pltpu.make_async_copy(stage.at[slot, part], target.at[n, t], out_sems.at[slot, n * 2 + half])
                copy.start()
                written.append(copy)

    x = second[...]
    low = x.astype(BF)
    total = x
    for k, mask in enumerate(doubling(blocks)):
        for copy in copies[k]:
            copy.wait()
        both = stack_rows(full.at[jnp.bitwise_xor(me, mask)])
        up = nn(low, both[:width])
        ups[k] = up
        act = (up * (0.5 * (1.0 + lax.erf(up * 0.7071067811865476)))).astype(BF)
        acts[k] = act
        total = total + nt(act, both[width:])
    normed, inverse = norm_stats(total)
    out[...] = (normed * gain[...] + bias[...]).astype(BF)
    grad_third, grad_gain, grad_bias = norm_back(cot[...].astype(F32), normed, inverse, gain[...])
    vectors[...] = jnp.zeros_like(vectors)
    vectors[0:1] = grad_gain
    vectors[1:2] = grad_bias
    third_low = grad_third.astype(BF)
    for k, mask in enumerate(doubling(blocks)):
        emit(k, tn(third_low, acts[k]), keep_down, send_down, jnp.bitwise_xor(me, mask))
    back = grad_third
    for k, mask in enumerate(doubling(blocks)):
        both = stack_rows(full.at[jnp.bitwise_xor(me, mask)])
        up = ups[k]
        slope = 0.5 * (1.0 + lax.erf(up * 0.7071067811865476)) + up * (
            jnp.exp(-0.5 * up * up) * 0.3989422804014327
        )
        grad_up = (slope * nn(third_low, both[width:])).astype(BF)
        emit(blocks + k, tn(low, grad_up), keep_up, send_up, jnp.bitwise_xor(me, mask))
        back = back + nt(grad_up, both[:width])
    grad_second[...] = back
    for copy in written:
        copy.wait()


def cross_backward(info, *refs, items, tokens, patches):
    pieces = refs[:8]
    (
        grad_second, second_sum, first, first_sum, mix, cross_q, cross_mix, keys, values, keys_last, values_last, gain2, gain1,
        grad_keys, grad_values, grad_keys_last, grad_values_last, grad_first_sum, first_grad_low, vectors, keep, send,
        full, grad_mix, grad_q, stage, sems, out_sems,
    ) = refs[8:]
    is_query = info[2] == 0
    vectors[...] = jnp.zeros_like(vectors)
    blocks = stage.shape[0]
    per = stage.shape[1] // 3

    def write(at, value):
        value = value.astype(BF)
        for b in range(blocks):
            stage[b, at * per : (at + 1) * per, :] = value[b * per : (b + 1) * per]

    def finish(grad_first):
        normed, inverse = norm_stats(first_sum[...])
        out, grad_gain, grad_bias = norm_back(grad_first, normed, inverse, gain1[...])
        vectors[0:1] = grad_gain
        vectors[1:2] = grad_bias
        grad_first_sum[...] = out
        first_grad_low[...] = out.astype(BF)
        write(2, tn(out.astype(BF), mix[...]))

    @pl.when(jnp.logical_not(is_query))
    def _():
        stage[:, : 2 * per, :] = jnp.zeros_like(stage[:, : 2 * per, :])
        finish(grad_second[...])

    @pl.when(is_query)
    def _():
        copies = fetch(info, pieces, full, sems, place_cross, pl.ds(2 * full.shape[3], full.shape[3]))
        normed, inverse = norm_stats(second_sum[...])
        grad_cross, grad_gain, grad_bias = norm_back(grad_second[...], normed, inverse, gain2[...])
        vectors[2:3] = grad_gain
        vectors[3:4] = grad_bias
        low = grad_cross.astype(BF)
        width = low.shape[1]
        write(1, tn(low, cross_mix[...]))
        for copy in copies:
            copy.wait()
        grad_mix[...] = nt(low, stack_rows(full.at[1])).astype(BF)
        grad_keys_last[...] = jnp.zeros_like(grad_keys_last)
        grad_values_last[...] = jnp.zeros_like(grad_values_last)

        def item(i, carry):
            rows = pl.ds(pl.multiple_of(i * tokens, tokens), tokens)
            patch_rows = pl.ds(pl.multiple_of(i * patches, patches), patches)
            for u in range(width // QUAD):
                lanes = slice(u * QUAD, (u + 1) * QUAD)
                key, value = keys[patch_rows, lanes], values[patch_rows, lanes]
                key_last, value_last = keys_last[:, lanes], values_last[:, lanes]
                queries = spread_heads(cross_q[rows, lanes])
                pulls = spread_heads(grad_mix[rows, lanes])
                scores = nt(key, queries) * SCALE
                tail = nt(key_last, queries) * SCALE
                is_last = last_row(i, tail.shape)
                probs = softmax_keys([scores, jnp.where(is_last, tail, NEG)])
                back, back_tail = score_back(probs, [nt(value, pulls), nt(value_last, pulls)])
                grad_keys[patch_rows, lanes] = (nn(back, queries) * SCALE).astype(BF)
                grad_values[patch_rows, lanes] = nn(probs[0].astype(BF), pulls).astype(BF)
                grad_keys_last[:, lanes] += nn(back_tail, queries) * SCALE
                grad_values_last[:, lanes] += nn(probs[1].astype(BF), pulls)
                grad_q[rows, lanes] = (collect_heads(tn(back, key) + tn(back_tail, key_last)) * SCALE).astype(BF)
            return carry

        lax.fori_loop(0, items, item, 0)
        grad_cross_q = grad_q[...]
        write(0, tn(first[...].astype(BF), grad_cross_q))
        finish(grad_cross + nn(grad_cross_q, stack_rows(full.at[0])))

    for copy in send_blocks(stage, keep, send, info[1], out_sems, True):
        copy.wait()


def send_blocks(stage, keep, send, core, sems, swapped):
    nodes, streams = keep.shape[:2][:: -1 if swapped else 1]
    copies = []
    for n in range(nodes):
        for s in range(streams):
            for half, target in enumerate((keep, send)):
                part = (n * 2 + (1 - core if half else core)) * streams + s
                copies.append(pltpu.make_async_copy(
                    stage.at[part], target.at[(s, n) if swapped else (n, s)], sems.at[half, n * streams + s]
                ))
    for copy in copies:
        copy.start()
    return copies


def image_backward(
    info, x, x_last, grad_keys, keys_last, grad_values, values_last, keep, send, stage, sems
):
    blocks, width = stage.shape[0], stage.shape[2]
    image = stage.shape[1] // 2

    @pl.when(info[2] == 0)
    def _():
        for m, (grad, last) in enumerate(((grad_keys, keys_last), (grad_values, values_last))):
            for u in range(width // QUAD):
                lanes = slice(u * QUAD, (u + 1) * QUAD)
                value = (tn(x[...], grad[:, lanes]) + tn(x_last[...], last[:, lanes].astype(BF))).astype(BF)
                for b in range(blocks):
                    stage[b, m * image : (m + 1) * image, lanes] = value[b * image : (b + 1) * image]

    @pl.when(info[2] != 0)
    def _():
        stage[...] = jnp.zeros_like(stage)

    for copy in send_blocks(stage, keep, send, info[1], sems, True):
        copy.wait()


def self_backward(info, spans, *refs, items, tokens):
    pieces = refs[:8]
    (
        h_own, low_own, low_oth, q_own, k_own, v_own, q_oth, k_oth, v_oth, grad_first_sum, extra,
        grad_input, keep, send, grads, full, pull_own, pull_oth, grad_q, grad_k, grad_v, sems, out_sems,
    ) = refs[8:]
    stream = info[2]
    copies = fetch(info, pieces, full, sems, place_self, pl.ds(0, full.shape[3]))
    for copy in copies:
        copy.wait()
    out_weight = stack_rows(full.at[3])
    pull_own[...] = nt(low_own[...], out_weight).astype(BF)
    pull_oth[...] = nt(low_oth[...], out_weight).astype(BF)
    width = h_own.shape[1]

    def item(i, carry):
        rows = pl.ds(pl.multiple_of(i * tokens, tokens), tokens)
        valid = valid_keys(spans[i], stream, tokens, 8 * tokens)
        for u in range(width // QUAD):
            lanes = slice(u * QUAD, (u + 1) * QUAD)
            keys = jnp.concatenate([k_own[rows, lanes], k_oth[rows, lanes]], axis=0)
            values = jnp.concatenate([v_own[rows, lanes], v_oth[rows, lanes]], axis=0)
            queries = jnp.concatenate([spread_heads(q_own[rows, lanes]), spread_heads(q_oth[rows, lanes])], axis=0)
            pulls = jnp.concatenate([spread_heads(pull_own[rows, lanes]), spread_heads(pull_oth[rows, lanes])], axis=0)
            scores = nt(keys, queries) * SCALE
            probs = softmax_keys([jnp.where(valid, scores, NEG)])
            (back,) = score_back(probs, [nt(values, pulls)])
            own_probs = probs[0].astype(BF)
            grad_k[rows, lanes] = (nn(back[:tokens], queries) * SCALE).astype(BF)
            grad_v[rows, lanes] = nn(own_probs[:tokens], pulls).astype(BF)
            grad_q[rows, lanes] = (collect_heads(tn(back[:, : 4 * tokens], keys)) * SCALE).astype(BF)
        return carry

    lax.fori_loop(0, items, item, 0)
    hidden = h_own[...]
    total = grad_first_sum[...]
    blocks, per = grads.shape[0], width // grads.shape[0]

    def write(at, value):
        value = value.astype(BF)
        for b in range(blocks):
            grads[b, at * per : (at + 1) * per, :] = value[b * per : (b + 1) * per]

    for at, ref in enumerate((grad_q, grad_k, grad_v)):
        value = ref[...]
        write(at, tn(hidden, value))
        total = total + nn(value, stack_rows(full.at[at]))
    grads[:, 3 * per :, :] = extra[...]
    grad_input[...] = total.astype(BF)
    for copy in send_blocks(grads, keep, send, info[1], out_sems, True):
        copy.wait()


VMEM = pl.BlockSpec(memory_space=pltpu.VMEM)
SMEM = pl.BlockSpec(memory_space=pltpu.SMEM)
ANY = pl.BlockSpec(memory_space=pl.ANY)


def shape(dims, kind):
    return jax.ShapeDtypeStruct(tuple(dims), kind)


def call(kernel, out_shapes, specs, scratch, micros, after=(), **more):
    count = len(specs)

    def body(*refs):
        kernel(*refs[:count], *refs[count + len(after) :])

    run = pl.pallas_call(
        body,
        out_shape=out_shapes,
        in_specs=specs + [ANY] * len(after),
        out_specs=more.pop("out_specs", [VMEM] * len(out_shapes)),
        scratch_shapes=scratch,
        compiler_params=pltpu.CompilerParams(vmem_limit_bytes=56 * 1024 * 1024),
        cost_estimate=pl.CostEstimate(flops=int(micros * 1.15e9), bytes_accessed=int(micros * 3.6e6), transcendentals=0),
        **more,
    )
    return lambda *operands: run(*operands, *after)


def pick(array, index, axis):
    return lax.dynamic_index_in_dim(array, index, axis, keepdims=False)


def add(a, b):
    return (a.astype(F32) + b.astype(F32)).astype(BF)


def swap(block, axis, bit=1):
    return lax.ppermute(block, axis, [(i, i ^ bit) for i in range(lax.axis_size(axis))])


def tie(value, *others):
    return jax.tree.map(lambda v: lax.optimization_barrier((v,) + others)[0], value)


def tensor_order(gathered, other, bit):
    upper = jnp.bitwise_and(lax.axis_index("tensor"), bit) != 0
    low, high = jnp.where(upper, other, gathered), jnp.where(upper, gathered, other)
    return jnp.stack([low, high], axis=1).reshape((-1,) + gathered.shape[1:])


def own_piece(pieces):
    pieces = pick(pick(pieces, lax.axis_index("core"), 1), lax.axis_index("stream"), 1)
    if lax.axis_size("node") == 2:
        return [pick(pieces, lax.axis_index("node"), 0)]
    return [pieces[0], pieces[1]]


def halve(pair, axis_name, axis, bit=1):
    keep, arrived = pair
    me = jnp.bitwise_and(lax.axis_index(axis_name) // bit, 1)
    sent = add(pick(keep, 1 - me, axis), pick(arrived, 1 - me, axis))
    kept = add(pick(keep, me, axis), pick(arrived, me, axis))
    return kept, swap(sent, axis_name, bit)


def over_nodes(pair):
    if lax.axis_size("node") == 2:
        return halve(pair, "node", 0)
    total = lax.psum_scatter(add(*pair), "node", scatter_dimension=0, tiled=False)
    return total, jnp.zeros_like(total)


def tensor_step(pair, bit):
    pair = [v.reshape((v.shape[0] // 2, 2) + v.shape[1:]) for v in pair]
    return halve(pair, "tensor", 1, bit)


def finish(pair):
    return (pair[0].astype(F32) + pair[1].astype(F32))[0]


def by_tensor(pair):
    count = lax.axis_size("tensor")
    rows, columns = pair[0].shape
    return [v.reshape(rows, count, columns // count).transpose(1, 0, 2) for v in pair]


def shards(
    hidden_in, lengths, image_features, self_q, self_k, self_v, self_out, ln1_gain, ln1_bias,
    cross_q, cross_k, cross_v, cross_out, ln2_gain, ln2_bias, ffn_up, ffn_down, ln3_gain, ln3_bias, cotangent,
):
    nodes, streams, count = lax.axis_size("node"), lax.axis_size("stream"), lax.axis_size("tensor")
    node, core = lax.axis_index("node"), lax.axis_index("core")
    stream, me = lax.axis_index("stream"), lax.axis_index("tensor")
    devices = nodes * 2
    rows_all, width = hidden_in.shape[1:]
    local = self_q.shape[1]
    image_tokens, image_width = image_features.shape[1:]
    patches = image_tokens - 1
    items = lengths.shape[0] // count
    rows = rows_all // count
    tokens = rows // items
    info = jnp.stack([node if nodes == 2 else jnp.int32(0), core, stream, me]).astype(jnp.int32)

    self_pieces = jnp.stack([self_q.T, self_k.T, self_v.T, self_out.T]).reshape(2, 2, 2, local // 2, width)
    small_pieces = jnp.stack([cross_q.T, cross_out.T]).reshape(2, 2, 2, local // 4, width)
    image_pieces = jnp.stack([cross_k.T, cross_v.T]).reshape(2, 2, 2, local // 4, image_width)
    h_own = lax.dynamic_slice_in_dim(hidden_in[0], me * rows, rows, 0)
    h_oth = lax.ppermute(h_own, "stream", SWAP)
    spans = lax.dynamic_slice_in_dim(lengths, me * items, items, 0)
    cot = lax.dynamic_slice_in_dim(cotangent[0], me * rows, rows, 0)
    image = lax.dynamic_slice_in_dim(image_features, me * items, items, 0)
    x = image[:, :patches].reshape(items * patches, image_width)
    x_last = image[:, patches]

    z = lambda vs, bit: [swap(v, "tensor", bit) for v in vs]
    join = lambda a, b: [jnp.concatenate([v, w]) for v, w in zip(a, b)]
    nodes_too = lambda vs: vs + [swap(vs[0], "node")] if nodes == 2 else vs
    cores_too = lambda vs: vs + [swap(v, "core") for v in vs]
    one_way = lambda v: lax.ppermute(v, "stream", [(1, 0)])
    image_0 = [v[None] for v in own_piece(image_pieces)]
    self_0 = [v[None] for v in own_piece(jnp.concatenate([self_pieces, small_pieces], axis=3))]
    ffn_share = 4 if nodes == 2 else 2
    ffn_rows = jnp.concatenate([ffn_up[0], ffn_down[0]], axis=0).reshape(ffn_share, 1, 2 * width // ffn_share, -1)
    ffn_own = pick(ffn_rows, node * 2 + core if nodes == 2 else core, 0)
    cut = ffn_own.shape[1] // 3
    ffn_0 = [[ffn_own[:, :cut]], [ffn_own[:, cut:]]]

    image_1 = z(image_0, 2)
    image_2 = join(tie(image_0, x, h_oth), image_1)
    image_3 = z(image_2, 1)
    self_1 = z(tie(self_0, *image_1), 2)
    image_4 = join(image_2, image_3)
    image_near = nodes_too(image_4)
    image_side = [one_way(image_near[0])]
    self_2 = join(tie(self_0, *image_4), self_1)
    self_3 = z(self_2, 1)
    first_1 = z(tie(ffn_0[0], *self_1, *image_4), 2)
    image_side.append(one_way(tie(image_near[1], image_side[0])))
    self_4 = join(self_2, self_3)
    self_near = nodes_too(tie(self_4, image_near[1]))
    first_2 = join(tie(ffn_0[0], image_near[1], image_side[0]), first_1)
    first_3 = z(first_2, 1)
    second_1 = z(tie(ffn_0[1], image_near[1], *first_1), 2)
    image_full = cores_too(image_near + image_side)
    first_4 = join(first_2, first_3)
    first_near = nodes_too(tie(first_4, self_near[1]))
    self_side = [swap(tie(self_near[0], image_side[1]), "stream")]
    second_2 = join(tie(ffn_0[1], *first_4), second_1)
    second_3 = z(second_2, 1)

    act_low, act = shape((rows, width), BF), shape((rows, width), F32)
    image_kv, image_kv_last = shape((items * patches, width), BF), shape((items, width), BF)
    dma = pltpu.SemaphoreType.DMA
    self_scratch = pltpu.VMEM((4, count, 2, local // 2, width), BF)
    small_scratch = pltpu.VMEM((2, count, 4, local // 4, width), BF)
    image_scratch = pltpu.VMEM((2, count, 4, local // 4, image_width), BF)
    row = lambda v: v.reshape(1, width)

    image_keys, image_values, keys_last, values_last = call(
        image_forward,
        [image_kv] * 2 + [image_kv_last] * 2,
        [SMEM] + [ANY] * 8 + [pl.BlockSpec((patches, image_width), lambda i: (i, 0)), pl.BlockSpec((items, image_width), lambda i: (0, 0))],
        [image_scratch, dma((8, count))],
        3,
        after=(*first_4, *second_2),
        grid=(items,),
        out_specs=[pl.BlockSpec((patches, width), lambda i: (i, 0))] * 2 + [pl.BlockSpec((items, width), lambda i: (0, 0))] * 2,
        name="image_forward",
    )(info, *image_full, x, x_last)

    self_side.append(swap(tie(self_near[1], image_keys, self_side[0], first_near[-1], second_3[0]), "stream"))
    second_4 = join(tie(second_2, image_keys), second_3)
    second_near = nodes_too(second_4)
    self_full = cores_too(self_near + self_side)

    (
        q_own, k_own, v_own, q_oth, k_oth, v_oth, mix, first_sum, first, cross_queries, cross_mix, second_sum, second,
    ) = call(
        functools.partial(forward, items=items, tokens=tokens, patches=patches),
        [act_low] * 7 + [act] * 2 + [act_low] * 2 + [act] * 2,
        [SMEM, SMEM] + [ANY] * 8 + [VMEM] * 10,
        [self_scratch, small_scratch, dma((8, count)), dma((8, count))],
        5,
        after=tuple(second_4),
        name="forward",
    )(
        info, spans, *self_full, h_own, h_oth, image_keys, image_values, keys_last, values_last,
        row(ln1_gain), row(ln1_bias), row(ln2_gain), row(ln2_bias),
    )

    ffn_full = cores_too(first_near) + second_near
    ffn_full += [swap(v, "core") for v in second_near[:-1] + [tie(second_near[-1], second)]]
    chunks, ffn_pieces = 2, len(ffn_full) // 2
    half_grads = [shape((nodes, count, width // devices, width), BF)] * 2
    output, grad_second, vectors3, keep_down, send_down, keep_up, send_up = call(
        functools.partial(ffn_both, pieces=ffn_pieces, chunks=chunks),
        [act_low, act, shape((8, width), F32)] + half_grads * 2,
        [SMEM] + [ANY] * (chunks * ffn_pieces) + [VMEM] * 4,
        [
            pltpu.VMEM((count, ffn_share, 2 * width // ffn_share, width), BF),
            pltpu.VMEM((count, rows, width), F32),
            pltpu.VMEM((count, rows, width), BF),
            pltpu.VMEM((2 * count, devices, width // devices, width), BF),
            dma((count, ffn_pieces, chunks)),
            dma((2 * count, 2 * nodes)),
        ],
        5,
        out_specs=[VMEM] * 3 + [ANY] * 4,
        name="ffn_both",
    )(info, *ffn_full, second, cot, ln3_gain, ln3_bias)
    down_core = keep_down, swap(send_down, "core")
    up_core = keep_up, swap(send_up, "core")
    output_1 = swap(output[None], "tensor", 2)
    down_nodes = over_nodes(down_core)
    blocks = devices * streams
    per, image_per, wide_per = width // blocks, image_width // blocks, width // devices
    tail = 16
    halves_of = lambda r: [shape((streams, nodes, r, width), BF)] * 2

    grad_keys, grad_values, grad_keys_last, grad_values_last, grad_first_sum, low_own, vectors12, keep_square, send_square = call(
        functools.partial(cross_backward, items=items, tokens=tokens, patches=patches),
        [
            image_kv, image_kv, shape((items, width), F32), shape((items, width), F32), act, act_low, shape((8, width), F32),
            *halves_of(3 * per),
        ],
        [SMEM] + [ANY] * 8 + [VMEM] * 13,
        [
            small_scratch, pltpu.VMEM((rows, width), BF), pltpu.VMEM((rows, width), BF),
            pltpu.VMEM((blocks, 3 * per, width), BF), dma((8, count)), dma((2, nodes * streams)),
        ],
        5,
        after=(down_nodes[0],),
        out_specs=[VMEM] * 7 + [ANY] * 2,
        name="cross_backward",
    )(
        info, *self_full, grad_second, second_sum, first, first_sum, mix, cross_queries, cross_mix, image_keys, image_values,
        keys_last, values_last, row(ln2_gain), row(ln1_gain),
    )
    shared = vectors12[:4].reshape(4, blocks, per).transpose(1, 0, 2)
    shared = jnp.pad(shared, ((0, 0), (0, 0), (0, width // count - per)))
    halves = vectors3[:2].reshape(2, devices, wide_per).transpose(1, 0, 2)
    halves = jnp.stack([jnp.where(stream == s, halves, 0.0) for s in range(streams)], axis=1)
    halves = jnp.pad(halves.reshape(blocks, 2, wide_per), ((0, 0), (0, 0), (0, width // count - wide_per)))
    extra = jnp.pad(jnp.concatenate([shared, halves], axis=1), ((0, 0), (0, tail - 6), (0, 0)))
    extra = jnp.tile(extra, (1, 1, count)).astype(BF)

    square_core = keep_square, swap(tie(send_square, output_1, down_nodes[1], up_core[1]), "core")
    output_2 = tensor_order(tie(output[None], low_own), output_1, 2)
    output_3 = swap(output_2, "tensor", 1)
    low_oth = swap(low_own, "stream")
    up_nodes = over_nodes(tie(up_core, low_own))
    down_half = tensor_step(tie(down_nodes, low_own), 1)
    square_stream = halve(square_core, "stream", 0)
    keep_image, send_image = call(
        image_backward,
        halves_of(2 * image_per),
        [SMEM] + [VMEM] * 6,
        [pltpu.VMEM((blocks, 2 * image_per, width), BF), dma((2, nodes * streams))],
        5,
        after=(output_2, up_nodes[0], down_half[0], square_stream[0], extra),
        out_specs=[ANY] * 2,
        name="image_backward",
    )(info, x, x_last, grad_keys, grad_keys_last, grad_values, grad_values_last)

    ended = low_oth, up_nodes[1], down_half[1], output_3, square_stream[1]
    image_core = keep_image, swap(tie(send_image, *ended), "core")
    output_4 = tensor_order(tie(output_2, keep_image), output_3, 1)
    up_half = tensor_step(tie(up_nodes, keep_image), 1)
    down_quarter = tensor_step(tie(down_half, keep_image), 2)
    square_nodes = over_nodes(tie(square_stream, keep_image))
    image_stream = halve(image_core, "stream", 0)
    grad_input, keep_self, send_self = call(
        functools.partial(self_backward, items=items, tokens=tokens),
        [act_low] + halves_of(3 * per + tail),
        [SMEM, SMEM] + [ANY] * 8 + [VMEM] * 11,
        [pltpu.VMEM((blocks, 3 * per + tail, width), BF), self_scratch]
        + [pltpu.VMEM((rows, width), BF)] * 5
        + [dma((8, count)), dma((2, nodes * streams))],
        3,
        out_specs=[VMEM] + [ANY] * 2,
        after=(output_4, up_half[0], down_quarter[0], square_nodes[0], image_stream[0]),
        name="self_backward",
    )(info, spans, *self_full, h_own, low_own, low_oth, q_own, k_own, v_own, q_oth, k_oth, v_oth, grad_first_sum, extra)

    ended = up_half[1], down_quarter[1], square_nodes[1], image_stream[1]
    self_core = keep_self, swap(tie(send_self, *ended), "core")
    self_stream = halve(self_core, "stream", 0)
    step = self_stream[0]
    grad_1 = swap(tie(grad_input[None], step), "tensor", 2)
    image_nodes = over_nodes(tie(image_stream, step))
    square_half = tensor_step(by_tensor(tie(square_nodes, step)), 1)
    self_nodes = over_nodes(self_stream)
    step = self_nodes[0]
    up_quarter = tensor_step(tie(up_half, step), 2)
    image_half = tensor_step(by_tensor(tie(image_nodes, step)), 1)
    self_half = tensor_step(by_tensor(self_nodes), 1)
    step = self_half[0]
    down_sum = finish(tie(down_quarter, step))
    grad_2 = tensor_order(tie(grad_input[None], step), grad_1, 2)
    grad_3 = swap(grad_2, "tensor", 1)
    square_quarter = tensor_step(tie(square_half, step), 2)
    image_quarter = tensor_step(tie(image_half, step), 2)
    self_quarter = tensor_step(self_half, 2)
    step = self_quarter[0]
    up_sum = finish(tie(up_quarter, step))
    square_sum = finish(tie(square_quarter, step))
    image_sum = finish(tie(image_quarter, step))
    self_sum = finish(self_quarter)
    grad_input = tensor_order(tie(grad_2, self_sum), grad_3, 1)

    vector = lambda r, n: self_sum[3 * per + r, :n]
    part = lambda v, at, n: v[at : at + n]
    return (
        output_4.reshape(1, rows_all, width),
        grad_input.reshape(1, rows_all, width),
        part(self_sum, 0, per),
        part(self_sum, per, per),
        part(self_sum, 2 * per, per),
        part(square_sum, 2 * per, per),
        vector(0, per),
        vector(1, per),
        part(square_sum, 0, per),
        part(image_sum, 0, image_per),
        part(image_sum, image_per, image_per),
        part(square_sum, per, per),
        vector(2, per),
        vector(3, per),
        up_sum[None],
        down_sum[None],
        vector(4, wide_per)[None],
        vector(5, wide_per)[None],
    )


def solution(mesh):
    sizes = mesh.devices.shape
    fine = Mesh(mesh.devices.reshape(sizes[0] // 2, 2, *sizes[1:]), ("node", "core", "stream", "tensor"))
    weight = P(None, "tensor")
    in_specs = (
        P("stream", DP, None), P(DP), P(DP, None, None), weight, weight, weight, weight, P(), P(),
        weight, weight, weight, weight, P(), P(), P("stream", None, "tensor"), P("stream", None, "tensor"),
        P("stream", None), P("stream", None), P("stream", DP, None),
    )
    over = ("node", "core", "stream")
    square, flat = P(over, "tensor"), P(over)
    out_specs = (
        P("stream", DP, None), P("stream", DP, None), square, square, square, square, flat, flat,
        square, square, square, square, flat, flat, P("stream", DP, "tensor"), P("stream", DP, "tensor"),
        P("stream", DP), P("stream", DP),
    )
    return jax.shard_map(shards, mesh=fine, in_specs=in_specs, out_specs=out_specs, check_vma=False)
```

```python
import functools

import jax
import jax.numpy as jnp
from jax import lax
from jax.experimental import pallas as pl
from jax.experimental.pallas import tpu as pltpu
from jax.sharding import Mesh, PartitionSpec as P

HD = 64
QUAD = 256
EPSILON = 1e-06
BF = jnp.bfloat16
F32 = jnp.float32
DP = ("node", "core")
SWAP = [(0, 1), (1, 0)]
SCALE = 0.125
NEG = -1e30


def nn(a, b):
    return lax.dot_general(a, b, (((1,), (0,)), ((), ())), preferred_element_type=F32)


def nt(a, b):
    return lax.dot_general(a, b, (((1,), (1,)), ((), ())), preferred_element_type=F32)


def tn(a, b):
    return lax.dot_general(a, b, (((0,), (0,)), ((), ())), preferred_element_type=F32)


def norm_stats(v):
    center = v - jnp.mean(v, axis=-1, keepdims=True)
    inverse = lax.rsqrt(jnp.mean(center * center, axis=-1, keepdims=True) + EPSILON)
    return center * inverse, inverse


def norm_back(e, normed, inverse, gain):
    scaled = e * gain
    out = inverse * (
        scaled
        - jnp.mean(scaled, axis=-1, keepdims=True)
        - normed * jnp.mean(scaled * normed, axis=-1, keepdims=True)
    )
    return out, jnp.sum(e * normed, axis=0, keepdims=True), jnp.sum(e, axis=0, keepdims=True)


def spread_heads(x):
    lane = lax.broadcasted_iota(jnp.int32, x.shape, 1) // HD
    zero = jnp.zeros_like(x)
    return jnp.concatenate([jnp.where(lane == j, x, zero) for j in range(QUAD // HD)], axis=0)


def collect_heads(x):
    rows = x.shape[0] * HD // QUAD
    lane = lax.broadcasted_iota(jnp.int32, (rows, QUAD), 1) // HD
    out = x[:rows]
    for j in range(1, QUAD // HD):
        out = jnp.where(lane == j, x[j * rows : (j + 1) * rows], out)
    return out


def softmax_keys(parts):
    peak = functools.reduce(jnp.maximum, [jnp.max(p, axis=0, keepdims=True) for p in parts])
    weights = [jnp.exp(p - peak) for p in parts]
    total = sum(jnp.sum(w, axis=0, keepdims=True) for w in weights)
    inverse = 1.0 / total
    return [w * inverse for w in weights]


def score_back(probs, grads):
    total = sum(jnp.sum(p * g, axis=0, keepdims=True) for p, g in zip(probs, grads))
    return [(p * (g - total)).astype(BF) for p, g in zip(probs, grads)]


def stack_rows(ref):
    value = ref[...]
    return value.reshape(-1, value.shape[-1])


def doubling(count):
    order, bit = [0], count // 2
    while bit:
        order = order + [mask | bit for mask in order]
        bit //= 2
    return order


def fetch(info, pieces, full, sems, where, take=None):
    node, core, stream, me = info[0], info[1], info[2], info[3]
    count = pieces[0].shape[0]
    copies = []
    for b, piece in enumerate(pieces):
        n = 1 - node if b & 1 else node
        s = 1 - stream if b & 2 else stream
        c = 1 - core if b & 4 else core
        for k, mask in enumerate(doubling(count)):
            src = jnp.bitwise_xor(me, mask)
            block = piece.at[k] if take is None else piece.at[k, take]
            copies.append(pltpu.make_async_copy(block, where(full, n, c, s, src), sems.at[b, k]))
    for copy in copies:
        copy.start(priority=1)
    return copies


def place_self(full, n, c, s, t):
    return full.at[n * 2 + c, t, s]


def place_cross(full, n, c, s, t):
    return full.at[n, t, c * 2 + s]


def forward(info, spans, *refs, items, tokens, patches):
    pieces = refs[:8]
    (
        h_own, h_oth, keys_hbm, values_hbm, keys_last, values_last, gain1, bias1, gain2, bias2,
        q_own, k_own, v_own, q_oth, k_oth, v_oth, mix, first_sum, first, cross_q, cross_mix, second_sum, second,
        full, small, keys, values, sems, small_sems, image_sems,
    ) = refs[8:]
    stream = info[2]
    copies = fetch(info, pieces, full, sems, place_self, pl.ds(0, full.shape[3]))
    later = fetch(info, pieces, small, small_sems, place_cross, pl.ds(full.shape[3], small.shape[3]))
    for at, (source, target) in enumerate(((keys_hbm, keys), (values_hbm, values))):
        later.append(pltpu.make_async_copy(source, target, image_sems.at[at]))
        later[-1].start(priority=1)
    for copy in copies:
        copy.wait()
    ho, hx = h_own[...], h_oth[...]
    for at, (own, oth) in enumerate(((q_own, q_oth), (k_own, k_oth), (v_own, v_oth))):
        weight = stack_rows(full.at[at])
        own[...] = nt(ho, weight).astype(BF)
        oth[...] = nt(hx, weight).astype(BF)
    width = ho.shape[1]

    def item(i, carry):
        rows = pl.ds(pl.multiple_of(i * tokens, tokens), tokens)
        valid = valid_keys(spans[i], stream, tokens, 4 * tokens)
        for u in range(width // QUAD):
            lanes = slice(u * QUAD, (u + 1) * QUAD)
            near = jnp.concatenate([k_own[rows, lanes], k_oth[rows, lanes]], axis=0)
            mixed = jnp.concatenate([v_own[rows, lanes], v_oth[rows, lanes]], axis=0)
            scores = nt(near, spread_heads(q_own[rows, lanes])) * SCALE
            (probs,) = softmax_keys([jnp.where(valid, scores, NEG)])
            mix[rows, lanes] = collect_heads(tn(probs.astype(BF), mixed)).astype(BF)
        return carry

    lax.fori_loop(0, items, item, 0)
    total = ho.astype(F32) + nn(mix[...], stack_rows(full.at[3]))
    first_sum[...] = total
    normed, _ = norm_stats(total)
    base = normed * gain1[...] + bias1[...]
    first[...] = base
    for copy in later:
        copy.wait()

    @pl.when(stream != 0)
    def _():
        second[...] = base
        second_sum[...] = base

    @pl.when(stream == 0)
    def _():
        cross_q[...] = nt(base.astype(BF), stack_rows(small.at[0])).astype(BF)

        def cross_item(i, carry):
            rows = pl.ds(pl.multiple_of(i * tokens, tokens), tokens)
            patch_rows = pl.ds(pl.multiple_of(i * patches, patches), patches)
            for u in range(width // QUAD):
                lanes = slice(u * QUAD, (u + 1) * QUAD)
                queries = spread_heads(cross_q[rows, lanes])
                scores = nt(keys[patch_rows, lanes], queries) * SCALE
                tail = nt(keys_last[:, lanes], queries) * SCALE
                tail = jnp.where(last_row(i, tail.shape), tail, NEG)
                probs, probs_tail = softmax_keys([scores, tail])
                out = tn(probs.astype(BF), values[patch_rows, lanes]) + tn(probs_tail.astype(BF), values_last[:, lanes])
                cross_mix[rows, lanes] = collect_heads(out).astype(BF)
            return carry

        lax.fori_loop(0, items, cross_item, 0)
        total = base + nn(cross_mix[...], stack_rows(small.at[1]))
        second_sum[...] = total
        normed, _ = norm_stats(total)
        second[...] = normed * gain2[...] + bias2[...]


def valid_keys(span, stream, tokens, columns):
    row = lax.broadcasted_iota(jnp.int32, (2 * tokens, columns), 0)
    own_limit = jnp.where(stream == 0, tokens, span)
    oth_limit = jnp.where(stream == 0, span, tokens)
    return ((row < tokens) & (row < own_limit)) | ((row >= tokens) & (row - tokens < oth_limit))


def image_forward(info, *refs):
    pieces = refs[:8]
    x, x_last, keys, values, keys_last, values_last, full, sems = refs[8:]

    @pl.when(info[2] == 0)
    def _():
        @pl.when(pl.program_id(0) == 0)
        def _():
            copies = fetch(info, pieces, full, sems, place_cross)
            for copy in copies:
                copy.wait()
            keys_last[...] = nt(x_last[...], stack_rows(full.at[0])).astype(BF)
            values_last[...] = nt(x_last[...], stack_rows(full.at[1])).astype(BF)

        keys[...] = nt(x[...], stack_rows(full.at[0])).astype(BF)
        values[...] = nt(x[...], stack_rows(full.at[1])).astype(BF)


def last_row(i, shape):
    return lax.broadcasted_iota(jnp.int32, shape, 0) == i


def ffn_both(info, *refs, pieces):
    weights = refs[:pieces], refs[pieces : 2 * pieces]
    (
        second, cot, gain, bias, out, grad_second, vectors, keep_down, send_down, keep_up, send_up,
        full, ups, acts, stage, sems, out_sems,
    ) = refs[2 * pieces :]
    node, core, me = info[0], info[1], info[3]
    blocks, width = full.shape[0], second.shape[1]
    nodes = keep_up.shape[0]
    copies = []
    for k, mask in enumerate(doubling(blocks)):
        src = jnp.bitwise_xor(me, mask)
        group = []
        for b in range(pieces):
            if pieces == 4:
                share = (1 - node if b & 1 else node) * 2 + (1 - core if b & 2 else core)
            else:
                share = 1 - core if b & 1 else core
            group.append(pltpu.make_async_copy(weights[k // 2][b].at[k % 2], full.at[src, share], sems.at[k, b]))
        for copy in group:
            copy.start()
        copies.append(group)

    written = []

    def emit(slot, value, keep, send, t):
        stage[slot] = value.astype(BF).reshape(stage.shape[1:])
        for n in range(nodes):
            for half, target in enumerate((keep, send)):
                part = n * 2 + (1 - core if half else core)
                copy = pltpu.make_async_copy(stage.at[slot, part], target.at[n, t], out_sems.at[slot, n * 2 + half])
                copy.start()
                written.append(copy)

    x = second[...]
    low = x.astype(BF)
    total = x
    for k, mask in enumerate(doubling(blocks)):
        for copy in copies[k]:
            copy.wait()
        both = stack_rows(full.at[jnp.bitwise_xor(me, mask)])
        up = nn(low, both[:width])
        ups[k] = up
        act = (up * (0.5 * (1.0 + lax.erf(up * 0.7071067811865476)))).astype(BF)
        acts[k] = act
        total = total + nt(act, both[width:])
    normed, inverse = norm_stats(total)
    out[...] = (normed * gain[...] + bias[...]).astype(BF)
    grad_third, grad_gain, grad_bias = norm_back(cot[...].astype(F32), normed, inverse, gain[...])
    vectors[...] = jnp.zeros_like(vectors)
    vectors[0:1] = grad_gain
    vectors[1:2] = grad_bias
    third_low = grad_third.astype(BF)
    for k, mask in enumerate(doubling(blocks)):
        emit(k, tn(third_low, acts[k]), keep_down, send_down, jnp.bitwise_xor(me, mask))
    back = grad_third
    for k, mask in enumerate(doubling(blocks)):
        both = stack_rows(full.at[jnp.bitwise_xor(me, mask)])
        up = ups[k]
        slope = 0.5 * (1.0 + lax.erf(up * 0.7071067811865476)) + up * (
            jnp.exp(-0.5 * up * up) * 0.3989422804014327
        )
        grad_up = (slope * nn(third_low, both[width:])).astype(BF)
        emit(blocks + k, tn(low, grad_up), keep_up, send_up, jnp.bitwise_xor(me, mask))
        back = back + nt(grad_up, both[:width])
    grad_second[...] = back
    for copy in written:
        copy.wait()


def cross_backward(info, *refs, items, tokens, patches):
    pieces = refs[:8]
    (
        grad_second, second_sum, first, first_sum, mix, cross_q, cross_mix, keys, values, keys_last, values_last, gain2, gain1,
        grad_keys, grad_values, grad_keys_last, grad_values_last, grad_first_sum, first_grad_low, vectors, keep, send,
        full, grad_mix, grad_q, stage, sems, out_sems,
    ) = refs[8:]
    is_query = info[2] == 0
    vectors[...] = jnp.zeros_like(vectors)
    blocks = stage.shape[0]
    per = stage.shape[1] // 3

    def write(at, value):
        value = value.astype(BF)
        for b in range(blocks):
            stage[b, at * per : (at + 1) * per, :] = value[b * per : (b + 1) * per]

    def finish(grad_first):
        normed, inverse = norm_stats(first_sum[...])
        out, grad_gain, grad_bias = norm_back(grad_first, normed, inverse, gain1[...])
        vectors[0:1] = grad_gain
        vectors[1:2] = grad_bias
        grad_first_sum[...] = out
        first_grad_low[...] = out.astype(BF)
        write(2, tn(out.astype(BF), mix[...]))

    @pl.when(jnp.logical_not(is_query))
    def _():
        stage[:, : 2 * per, :] = jnp.zeros_like(stage[:, : 2 * per, :])
        finish(grad_second[...])

    @pl.when(is_query)
    def _():
        copies = fetch(info, pieces, full, sems, place_cross, pl.ds(2 * full.shape[3], full.shape[3]))
        normed, inverse = norm_stats(second_sum[...])
        grad_cross, grad_gain, grad_bias = norm_back(grad_second[...], normed, inverse, gain2[...])
        vectors[2:3] = grad_gain
        vectors[3:4] = grad_bias
        low = grad_cross.astype(BF)
        width = low.shape[1]
        write(1, tn(low, cross_mix[...]))
        for copy in copies:
            copy.wait()
        grad_mix[...] = nt(low, stack_rows(full.at[1])).astype(BF)
        grad_keys_last[...] = jnp.zeros_like(grad_keys_last)
        grad_values_last[...] = jnp.zeros_like(grad_values_last)

        def item(i, carry):
            rows = pl.ds(pl.multiple_of(i * tokens, tokens), tokens)
            patch_rows = pl.ds(pl.multiple_of(i * patches, patches), patches)
            for u in range(width // QUAD):
                lanes = slice(u * QUAD, (u + 1) * QUAD)
                key, value = keys[patch_rows, lanes], values[patch_rows, lanes]
                key_last, value_last = keys_last[:, lanes], values_last[:, lanes]
                queries = spread_heads(cross_q[rows, lanes])
                pulls = spread_heads(grad_mix[rows, lanes])
                scores = nt(key, queries) * SCALE
                tail = nt(key_last, queries) * SCALE
                is_last = last_row(i, tail.shape)
                probs = softmax_keys([scores, jnp.where(is_last, tail, NEG)])
                back, back_tail = score_back(probs, [nt(value, pulls), nt(value_last, pulls)])
                grad_keys[patch_rows, lanes] = (nn(back, queries) * SCALE).astype(BF)
                grad_values[patch_rows, lanes] = nn(probs[0].astype(BF), pulls).astype(BF)
                grad_keys_last[:, lanes] += nn(back_tail, queries) * SCALE
                grad_values_last[:, lanes] += nn(probs[1].astype(BF), pulls)
                grad_q[rows, lanes] = (collect_heads(tn(back, key) + tn(back_tail, key_last)) * SCALE).astype(BF)
            return carry

        lax.fori_loop(0, items, item, 0)
        grad_cross_q = grad_q[...]
        write(0, tn(first[...].astype(BF), grad_cross_q))
        finish(grad_cross + nn(grad_cross_q, stack_rows(full.at[0])))

    for copy in send_blocks(stage, keep, send, info[1], out_sems, True):
        copy.wait()


def send_blocks(stage, keep, send, core, sems, swapped):
    nodes, streams = keep.shape[:2][:: -1 if swapped else 1]
    copies = []
    for n in range(nodes):
        for s in range(streams):
            for half, target in enumerate((keep, send)):
                part = (n * 2 + (1 - core if half else core)) * streams + s
                copies.append(pltpu.make_async_copy(
                    stage.at[part], target.at[(s, n) if swapped else (n, s)], sems.at[half, n * streams + s]
                ))
    for copy in copies:
        copy.start()
    return copies


def image_backward(
    info, x, x_last, grad_keys, keys_last, grad_values, values_last, keep, send, stage, sems
):
    blocks, width = stage.shape[0], stage.shape[2]
    image = stage.shape[1] // 2

    @pl.when(info[2] == 0)
    def _():
        for m, (grad, last) in enumerate(((grad_keys, keys_last), (grad_values, values_last))):
            for u in range(width // QUAD):
                lanes = slice(u * QUAD, (u + 1) * QUAD)
                value = (tn(x[...], grad[:, lanes]) + tn(x_last[...], last[:, lanes].astype(BF))).astype(BF)
                for b in range(blocks):
                    stage[b, m * image : (m + 1) * image, lanes] = value[b * image : (b + 1) * image]

    @pl.when(info[2] != 0)
    def _():
        stage[...] = jnp.zeros_like(stage)

    for copy in send_blocks(stage, keep, send, info[1], sems, True):
        copy.wait()


def self_backward(info, spans, *refs, items, tokens):
    pieces = refs[:8]
    (
        h_own, low_own, low_oth, q_own, k_own, v_own, q_oth, k_oth, v_oth, grad_first_sum, vectors12, vectors3,
        grad_input, keep, send, grads, full, pull_own, pull_oth, grad_q, grad_k, grad_v, sems, out_sems,
    ) = refs[8:]
    stream = info[2]
    copies = fetch(info, pieces, full, sems, place_self, pl.ds(0, full.shape[3]))
    for copy in copies:
        copy.wait()
    out_weight = stack_rows(full.at[3])
    pull_own[...] = nt(low_own[...], out_weight).astype(BF)
    pull_oth[...] = nt(low_oth[...], out_weight).astype(BF)
    width = h_own.shape[1]

    def item(i, carry):
        rows = pl.ds(pl.multiple_of(i * tokens, tokens), tokens)
        valid = valid_keys(spans[i], stream, tokens, 8 * tokens)
        for u in range(width // QUAD):
            lanes = slice(u * QUAD, (u + 1) * QUAD)
            keys = jnp.concatenate([k_own[rows, lanes], k_oth[rows, lanes]], axis=0)
            values = jnp.concatenate([v_own[rows, lanes], v_oth[rows, lanes]], axis=0)
            queries = jnp.concatenate([spread_heads(q_own[rows, lanes]), spread_heads(q_oth[rows, lanes])], axis=0)
            pulls = jnp.concatenate([spread_heads(pull_own[rows, lanes]), spread_heads(pull_oth[rows, lanes])], axis=0)
            scores = nt(keys, queries) * SCALE
            probs = softmax_keys([jnp.where(valid, scores, NEG)])
            (back,) = score_back(probs, [nt(values, pulls)])
            own_probs = probs[0].astype(BF)
            grad_k[rows, lanes] = (nn(back[:tokens], queries) * SCALE).astype(BF)
            grad_v[rows, lanes] = nn(own_probs[:tokens], pulls).astype(BF)
            grad_q[rows, lanes] = (collect_heads(tn(back[:, : 4 * tokens], keys)) * SCALE).astype(BF)
        return carry

    lax.fori_loop(0, items, item, 0)
    hidden = h_own[...]
    total = grad_first_sum[...]
    blocks, per = grads.shape[0], width // grads.shape[0]

    def write(at, value):
        value = value.astype(BF)
        for b in range(blocks):
            grads[b, at * per : (at + 1) * per, :] = value[b * per : (b + 1) * per]

    for at, ref in enumerate((grad_q, grad_k, grad_v)):
        value = ref[...]
        write(at, tn(hidden, value))
        total = total + nn(value, stack_rows(full.at[at]))
    tail = grads.shape[1] - 3 * per
    local = width // full.shape[1]
    source = lax.broadcasted_iota(jnp.int32, (width, width), 0)
    target = lax.rem(lax.broadcasted_iota(jnp.int32, (width, width), 1), local)
    lane = lax.broadcasted_iota(jnp.int32, (8, width), 1)

    def spread(vectors, size):
        value = vectors[...].astype(BF)
        parts = [jnp.where(lane // size == p, value, jnp.zeros_like(value)) for p in range(width // size)]
        chosen = jnp.where(lax.rem(source, size) == target, 1.0, 0.0).astype(BF)
        return nn(jnp.concatenate(parts, axis=0), chosen).astype(BF)

    shared, halves = spread(vectors12, per), spread(vectors3, 2 * per)
    for b in range(blocks):
        own = halves[b // 2 * 8 : b // 2 * 8 + 8]
        own = jnp.where(stream == b % 2, own, jnp.zeros_like(own))
        grads[b, 3 * per :, :] = jnp.concatenate([shared[b * 8 : b * 8 + 8], own], axis=0)
    grad_input[...] = total.astype(BF)
    for copy in send_blocks(grads, keep, send, info[1], out_sems, True):
        copy.wait()


VMEM = pl.BlockSpec(memory_space=pltpu.VMEM)
SMEM = pl.BlockSpec(memory_space=pltpu.SMEM)
ANY = pl.BlockSpec(memory_space=pl.ANY)


def shape(dims, kind):
    return jax.ShapeDtypeStruct(tuple(dims), kind)


def call(kernel, out_shapes, specs, scratch, micros, after=(), **more):
    count = len(specs)

    def body(*refs):
        kernel(*refs[:count], *refs[count + len(after) :])

    run = pl.pallas_call(
        body,
        out_shape=out_shapes,
        in_specs=specs + [ANY] * len(after),
        out_specs=more.pop("out_specs", [VMEM] * len(out_shapes)),
        scratch_shapes=scratch,
        compiler_params=pltpu.CompilerParams(vmem_limit_bytes=62 * 1024 * 1024),
        cost_estimate=pl.CostEstimate(flops=int(micros * 1.15e9), bytes_accessed=int(micros * 3.6e6), transcendentals=0),
        **more,
    )
    return lambda *operands: run(*operands, *after)


def pick(array, index, axis):
    return lax.dynamic_index_in_dim(array, index, axis, keepdims=False)


def add(a, b):
    return (a.astype(F32) + b.astype(F32)).astype(BF)


def swap(block, axis, bit=1):
    return lax.ppermute(block, axis, [(i, i ^ bit) for i in range(lax.axis_size(axis))])


def tie(value, *others):
    return jax.tree.map(lambda v: lax.optimization_barrier((v,) + others)[0], value)


def tensor_order(gathered, other, bit):
    upper = jnp.bitwise_and(lax.axis_index("tensor"), bit) != 0
    low, high = jnp.where(upper, other, gathered), jnp.where(upper, gathered, other)
    return jnp.stack([low, high], axis=1).reshape((-1,) + gathered.shape[1:])


def own_piece(pieces):
    pieces = pick(pick(pieces, lax.axis_index("core"), 1), lax.axis_index("stream"), 1)
    if lax.axis_size("node") == 2:
        return [pick(pieces, lax.axis_index("node"), 0)]
    return [pieces[0], pieces[1]]


def halve(pair, axis_name, axis, bit=1):
    keep, arrived = pair
    me = jnp.bitwise_and(lax.axis_index(axis_name) // bit, 1)
    sent = add(pick(keep, 1 - me, axis), pick(arrived, 1 - me, axis))
    kept = add(pick(keep, me, axis), pick(arrived, me, axis))
    return kept, swap(sent, axis_name, bit)


def over_nodes(pair):
    if lax.axis_size("node") == 2:
        return halve(pair, "node", 0)
    total = lax.psum_scatter(add(*pair), "node", scatter_dimension=0, tiled=False)
    return total, jnp.zeros_like(total)


def tensor_step(pair, bit):
    pair = [v.reshape((v.shape[0] // 2, 2) + v.shape[1:]) for v in pair]
    return halve(pair, "tensor", 1, bit)


def finish(pair):
    return (pair[0].astype(F32) + pair[1].astype(F32))[0]


def split_rows(pair):
    count, me = lax.axis_size("tensor"), lax.axis_index("tensor")
    rows, columns = pair[0].shape
    half, local = rows // 2, columns // count

    def kernel(bit, kept, arrived, stays, goes):
        total = (kept[...].astype(F32) + arrived[...].astype(F32)).astype(BF)
        upper = bit[0] == 1
        for p in range(count // 2):
            two = [
                jnp.concatenate([total[:half, t * local : (t + 1) * local], total[half:, t * local : (t + 1) * local]], axis=1)
                for t in (2 * p, 2 * p + 1)
            ]
            stays[p] = jnp.where(upper, two[1], two[0])
            goes[p] = jnp.where(upper, two[0], two[1])

    outs = [shape((count // 2, half, 2 * local), BF)] * 2
    bit = jnp.bitwise_and(me, 1).reshape(1)
    stays, goes = call(kernel, outs, [SMEM, VMEM, VMEM], [], 1, name="split_rows")(bit, *pair)
    return stays, swap(goes, "tensor", 1)


def finish_rows(pair, sizes):
    local = pair[0].shape[2] // 2

    def kernel(kept, arrived, *outs):
        both = kept[0].astype(F32) + arrived[0].astype(F32)
        total = jnp.concatenate([both[:, :local], both[:, local:]], axis=0)
        start = 0
        for out in outs:
            out[...] = total[start : start + out.shape[0]]
            start += out.shape[0]

    outs = [shape((size, local), F32) for size in sizes]
    return call(kernel, outs, [VMEM] * 2, [], 1, name="finish_rows")(*pair)


def shards(
    hidden_in, lengths, image_features, self_q, self_k, self_v, self_out, ln1_gain, ln1_bias,
    cross_q, cross_k, cross_v, cross_out, ln2_gain, ln2_bias, ffn_up, ffn_down, ln3_gain, ln3_bias, cotangent,
):
    nodes, streams, count = lax.axis_size("node"), lax.axis_size("stream"), lax.axis_size("tensor")
    node, core = lax.axis_index("node"), lax.axis_index("core")
    stream, me = lax.axis_index("stream"), lax.axis_index("tensor")
    devices = nodes * 2
    rows_all, width = hidden_in.shape[1:]
    local = self_q.shape[1]
    image_tokens, image_width = image_features.shape[1:]
    patches = image_tokens - 1
    items = lengths.shape[0] // count
    rows = rows_all // count
    tokens = rows // items
    info = jnp.stack([node if nodes == 2 else jnp.int32(0), core, stream, me]).astype(jnp.int32)

    self_pieces = jnp.stack([self_q.T, self_k.T, self_v.T, self_out.T]).reshape(2, 2, 2, local // 2, width)
    small_pieces = jnp.stack([cross_q.T, cross_out.T]).reshape(2, 2, 2, local // 4, width)
    image_pieces = jnp.stack([cross_k.T, cross_v.T]).reshape(2, 2, 2, local // 4, image_width)
    h_own = lax.dynamic_slice_in_dim(hidden_in[0], me * rows, rows, 0)
    h_oth = lax.ppermute(h_own, "stream", SWAP)
    spans = lax.dynamic_slice_in_dim(lengths, me * items, items, 0)
    cot = lax.dynamic_slice_in_dim(cotangent[0], me * rows, rows, 0)
    image = lax.dynamic_slice_in_dim(image_features, me * items, items, 0)
    x = image[:, :patches].reshape(items * patches, image_width)
    x_last = image[:, patches]

    z = lambda vs, bit: [swap(v, "tensor", bit) for v in vs]
    join = lambda a, b: [jnp.concatenate([v, w]) for v, w in zip(a, b)]
    nodes_too = lambda vs: vs + [swap(vs[0], "node")] if nodes == 2 else vs
    cores_too = lambda vs: vs + [swap(v, "core") for v in vs]
    one_way = lambda v: lax.ppermute(v, "stream", [(1, 0)])
    image_0 = [v[None] for v in own_piece(image_pieces)]
    self_0 = [v[None] for v in own_piece(jnp.concatenate([self_pieces, small_pieces], axis=3))]
    ffn_share = 4 if nodes == 2 else 2
    ffn_rows = jnp.concatenate([ffn_up[0], ffn_down[0]], axis=0).reshape(ffn_share, 1, 2 * width // ffn_share, -1)
    ffn_own = pick(ffn_rows, node * 2 + core if nodes == 2 else core, 0)
    ffn_0 = [ffn_own]

    image_1 = z(image_0, 2)
    image_2 = join(tie(image_0, x, h_oth), image_1)
    image_3 = z(image_2, 1)
    self_1 = z(tie(self_0, *image_1), 2)
    image_4 = join(image_2, image_3)
    image_near = nodes_too(image_4)
    image_side = [one_way(image_near[0])]
    self_2 = join(tie(self_0, *image_4), self_1)
    self_3 = z(self_2, 1)
    ffn_1 = z(tie(ffn_0, *self_1, *image_4), 2)
    image_side.append(one_way(tie(image_near[1], image_side[0], *self_3)))
    self_4 = join(self_2, self_3)
    self_near = nodes_too(tie(self_4, image_near[1], image_side[0]))
    image_full = cores_too(image_near + image_side)
    self_side = [swap(tie(self_near[0], image_side[1]), "stream")]

    act_low, act = shape((rows, width), BF), shape((rows, width), F32)
    image_kv, image_kv_last = shape((items * patches, width), BF), shape((items, width), BF)
    dma = pltpu.SemaphoreType.DMA
    self_scratch = pltpu.VMEM((4, count, 2, local // 2, width), BF)
    small_scratch = pltpu.VMEM((2, count, 4, local // 4, width), BF)
    image_scratch = pltpu.VMEM((2, count, 4, local // 4, image_width), BF)
    image_vmem = pltpu.VMEM((items * patches, width), BF)
    row = lambda v: v.reshape(1, width)

    image_keys, image_values, keys_last, values_last = call(
        image_forward,
        [image_kv] * 2 + [image_kv_last] * 2,
        [SMEM] + [ANY] * 8 + [pl.BlockSpec((patches, image_width), lambda i: (i, 0)), pl.BlockSpec((items, image_width), lambda i: (0, 0))],
        [image_scratch, dma((8, count))],
        3,
        after=(),
        grid=(items,),
        out_specs=[pl.BlockSpec((patches, width), lambda i: (i, 0))] * 2 + [pl.BlockSpec((items, width), lambda i: (0, 0))] * 2,
        name="image_forward",
    )(info, *image_full, x, x_last)

    self_side.append(swap(tie(self_near[1], image_keys, self_side[0], *ffn_1), "stream"))
    ffn_2 = join(tie(ffn_0, image_keys), ffn_1)
    ffn_3 = z(ffn_2, 1)
    ffn_near, ffn_late = nodes_too(ffn_2), nodes_too(ffn_3)
    self_full = cores_too(self_near + self_side)

    (
        q_own, k_own, v_own, q_oth, k_oth, v_oth, mix, first_sum, first, cross_queries, cross_mix, second_sum, second,
    ) = call(
        functools.partial(forward, items=items, tokens=tokens, patches=patches),
        [act_low] * 7 + [act] * 2 + [act_low] * 2 + [act] * 2,
        [SMEM, SMEM] + [ANY] * 8 + [VMEM] * 2 + [ANY] * 2 + [VMEM] * 6,
        [self_scratch, small_scratch, image_vmem, image_vmem, dma((8, count)), dma((8, count)), dma((2,))],
        5,
        after=tuple(ffn_3),
        name="forward",
    )(
        info, spans, *self_full, h_own, h_oth, image_keys, image_values, keys_last, values_last,
        row(ln1_gain), row(ln1_bias), row(ln2_gain), row(ln2_bias),
    )

    ffn_late = ffn_late[:-1] + [tie(ffn_late[-1], second)]
    ffn_full = cores_too(ffn_near) + cores_too(ffn_late)
    ffn_pieces = len(ffn_near) * 2
    half_grads = [shape((nodes, count, width // devices, width), BF)] * 2
    output, grad_second, vectors3, keep_down, send_down, keep_up, send_up = call(
        functools.partial(ffn_both, pieces=ffn_pieces),
        [act_low, act, shape((8, width), F32)] + half_grads * 2,
        [SMEM] + [ANY] * (2 * ffn_pieces) + [VMEM] * 4,
        [
            pltpu.VMEM((count, ffn_share, 2 * width // ffn_share, width), BF),
            pltpu.VMEM((count, rows, width), F32),
            pltpu.VMEM((count, rows, width), BF),
            pltpu.VMEM((2 * count, devices, width // devices, width), BF),
            dma((count, ffn_pieces)),
            dma((2 * count, 2 * nodes)),
        ],
        5,
        out_specs=[VMEM] * 3 + [ANY] * 4,
        name="ffn_both",
    )(info, *ffn_full, second, cot, ln3_gain, ln3_bias)
    down_core = keep_down, swap(send_down, "core")
    up_core = keep_up, swap(send_up, "core")
    output_1 = swap(output[None], "tensor", 2)
    down_nodes = over_nodes(down_core)
    blocks = devices * streams
    per, image_per, wide_per = width // blocks, image_width // blocks, width // devices
    tail = 16
    halves_of = lambda r: [shape((streams, nodes, r, width), BF)] * 2

    grad_keys, grad_values, grad_keys_last, grad_values_last, grad_first_sum, low_own, vectors12, keep_square, send_square = call(
        functools.partial(cross_backward, items=items, tokens=tokens, patches=patches),
        [
            image_kv, image_kv, shape((items, width), F32), shape((items, width), F32), act, act_low, shape((8, width), F32),
            *halves_of(3 * per),
        ],
        [SMEM] + [ANY] * 8 + [VMEM] * 13,
        [
            small_scratch, pltpu.VMEM((rows, width), BF), pltpu.VMEM((rows, width), BF),
            pltpu.VMEM((blocks, 3 * per, width), BF), dma((8, count)), dma((2, nodes * streams)),
        ],
        5,
        after=(down_nodes[0],),
        out_specs=[VMEM] * 7 + [ANY] * 2,
        name="cross_backward",
    )(
        info, *self_full, grad_second, second_sum, first, first_sum, mix, cross_queries, cross_mix, image_keys, image_values,
        keys_last, values_last, row(ln2_gain), row(ln1_gain),
    )
    square_core = keep_square, swap(tie(send_square, output_1, down_nodes[1], up_core[1]), "core")
    output_2 = tensor_order(tie(output[None], low_own), output_1, 2)
    output_3 = swap(output_2, "tensor", 1)
    low_oth = swap(low_own, "stream")
    up_nodes = over_nodes(tie(up_core, low_own))
    down_half = tensor_step(tie(down_nodes, low_own), 1)
    square_stream = halve(square_core, "stream", 0)
    keep_image, send_image = call(
        image_backward,
        halves_of(2 * image_per),
        [SMEM] + [VMEM] * 6,
        [pltpu.VMEM((blocks, 2 * image_per, width), BF), dma((2, nodes * streams))],
        5,
        after=(output_2, up_nodes[0], down_half[0], square_stream[0]),
        out_specs=[ANY] * 2,
        name="image_backward",
    )(info, x, x_last, grad_keys, grad_keys_last, grad_values, grad_values_last)

    ended = low_oth, up_nodes[1], down_half[1], output_3, square_stream[1]
    image_core = keep_image, swap(tie(send_image, *ended), "core")
    up_half = tensor_step(tie(up_nodes, keep_image), 1)
    down_quarter = tensor_step(tie(down_half, keep_image), 2)
    square_nodes = over_nodes(tie(square_stream, keep_image))
    image_stream = halve(image_core, "stream", 0)
    grad_input, keep_self, send_self = call(
        functools.partial(self_backward, items=items, tokens=tokens),
        [act_low] + halves_of(3 * per + tail),
        [SMEM, SMEM] + [ANY] * 8 + [VMEM] * 12,
        [pltpu.VMEM((blocks, 3 * per + tail, width), BF), self_scratch]
        + [pltpu.VMEM((rows, width), BF)] * 5
        + [dma((8, count)), dma((2, nodes * streams))],
        3,
        out_specs=[VMEM] + [ANY] * 2,
        after=(up_half[0], down_quarter[0], square_nodes[0], image_stream[0]),
        name="self_backward",
    )(info, spans, *self_full, h_own, low_own, low_oth, q_own, k_own, v_own, q_oth, k_oth, v_oth, grad_first_sum, vectors12, vectors3)

    ended = up_half[1], down_quarter[1], square_nodes[1], image_stream[1]
    self_core = keep_self, swap(tie(send_self, *ended), "core")
    self_stream = halve(self_core, "stream", 0)
    step = self_stream[0]
    grad_1 = swap(tie(grad_input[None], step), "tensor", 2)
    image_nodes = over_nodes(tie(image_stream, step))
    square_half = split_rows(tie(square_nodes, step))
    self_nodes = over_nodes(self_stream)
    step = self_nodes[0]
    output_4 = tensor_order(tie(output_2, step), output_3, 1)
    down_sum = finish(tie(down_quarter, step))
    square_quarter = tensor_step(tie(square_half, step), 2)
    grad_2 = tensor_order(tie(grad_input[None], step), grad_1, 2)
    grad_3 = swap(grad_2, "tensor", 1)
    self_half = split_rows(self_nodes)
    step = self_half[0]
    up_quarter = tensor_step(tie(up_half, step), 2)
    image_half = split_rows(tie(image_nodes, step))
    square_q, square_o, self_o = finish_rows(tie(square_quarter, step), (per, per, per))
    self_quarter = tensor_step(self_half, 2)
    step = self_quarter[0]
    image_quarter = tensor_step(tie(image_half, step), 2)
    grad_input = tensor_order(tie(grad_2, step), grad_3, 1)
    up_sum = finish(tie(up_quarter, step))
    self_q, self_k, self_v, vectors = finish_rows(tie(self_quarter, up_sum, grad_input), (per, per, per, tail))
    image_k, image_v = finish_rows(image_quarter, (image_per, image_per))

    vector = lambda r, n: vectors[r, :n]
    return (
        output_4.reshape(1, rows_all, width),
        grad_input.reshape(1, rows_all, width),
        self_q,
        self_k,
        self_v,
        self_o,
        vector(0, per),
        vector(1, per),
        square_q,
        image_k,
        image_v,
        square_o,
        vector(2, per),
        vector(3, per),
        up_sum[None],
        down_sum[None],
        vector(8, wide_per)[None],
        vector(9, wide_per)[None],
    )


def solution(mesh):
    sizes = mesh.devices.shape
    fine = Mesh(mesh.devices.reshape(sizes[0] // 2, 2, *sizes[1:]), ("node", "core", "stream", "tensor"))
    weight = P(None, "tensor")
    in_specs = (
        P("stream", DP, None), P(DP), P(DP, None, None), weight, weight, weight, weight, P(), P(),
        weight, weight, weight, weight, P(), P(), P("stream", None, "tensor"), P("stream", None, "tensor"),
        P("stream", None), P("stream", None), P("stream", DP, None),
    )
    over = ("node", "core", "stream")
    square, flat = P(over, "tensor"), P(over)
    out_specs = (
        P("stream", DP, None), P("stream", DP, None), square, square, square, square, flat, flat,
        square, square, square, square, flat, flat, P("stream", DP, "tensor"), P("stream", DP, "tensor"),
        P("stream", DP), P("stream", DP),
    )
    return jax.shard_map(shards, mesh=fine, in_specs=in_specs, out_specs=out_specs, check_vma=False)
```

```python
import functools

import jax
import jax.numpy as jnp
from jax import lax
from jax.experimental import pallas as pl
from jax.experimental.pallas import tpu as pltpu
from jax.sharding import Mesh, PartitionSpec as P

HD = 64
QUAD = 256
EPSILON = 1e-06
BF = jnp.bfloat16
F32 = jnp.float32
DP = ("node", "core")
SWAP = [(0, 1), (1, 0)]
SCALE = 0.125
NEG = -1e30


def nn(a, b):
    return lax.dot_general(a, b, (((1,), (0,)), ((), ())), preferred_element_type=F32)


def nt(a, b):
    return lax.dot_general(a, b, (((1,), (1,)), ((), ())), preferred_element_type=F32)


def tn(a, b):
    return lax.dot_general(a, b, (((0,), (0,)), ((), ())), preferred_element_type=F32)


def norm_stats(v):
    center = v - jnp.mean(v, axis=-1, keepdims=True)
    inverse = lax.rsqrt(jnp.mean(center * center, axis=-1, keepdims=True) + EPSILON)
    return center * inverse, inverse


def norm_back(e, normed, inverse, gain):
    scaled = e * gain
    out = inverse * (
        scaled
        - jnp.mean(scaled, axis=-1, keepdims=True)
        - normed * jnp.mean(scaled * normed, axis=-1, keepdims=True)
    )
    return out, jnp.sum(e * normed, axis=0, keepdims=True), jnp.sum(e, axis=0, keepdims=True)


def spread_heads(x):
    lane = lax.broadcasted_iota(jnp.int32, x.shape, 1) // HD
    zero = jnp.zeros_like(x)
    return jnp.concatenate([jnp.where(lane == j, x, zero) for j in range(QUAD // HD)], axis=0)


def collect_heads(x):
    rows = x.shape[0] * HD // QUAD
    lane = lax.broadcasted_iota(jnp.int32, (rows, QUAD), 1) // HD
    out = x[:rows]
    for j in range(1, QUAD // HD):
        out = jnp.where(lane == j, x[j * rows : (j + 1) * rows], out)
    return out


def softmax_keys(parts):
    peak = functools.reduce(jnp.maximum, [jnp.max(p, axis=0, keepdims=True) for p in parts])
    weights = [jnp.exp(p - peak) for p in parts]
    total = sum(jnp.sum(w, axis=0, keepdims=True) for w in weights)
    inverse = 1.0 / total
    return [w * inverse for w in weights]


def score_back(probs, grads):
    total = sum(jnp.sum(p * g, axis=0, keepdims=True) for p, g in zip(probs, grads))
    return [(p * (g - total)).astype(BF) for p, g in zip(probs, grads)]


def stack_rows(ref):
    value = ref[...]
    return value.reshape(-1, value.shape[-1])


def doubling(count):
    order, bit = [0], count // 2
    while bit:
        order = order + [mask | bit for mask in order]
        bit //= 2
    return order


def fetch(info, pieces, full, sems, where, take=None):
    node, core, stream, me = info[0], info[1], info[2], info[3]
    count = pieces[0].shape[0]
    copies = []
    for b, piece in enumerate(pieces):
        n = 1 - node if b & 1 else node
        s = 1 - stream if b & 2 else stream
        c = 1 - core if b & 4 else core
        for k, mask in enumerate(doubling(count)):
            src = jnp.bitwise_xor(me, mask)
            block = piece.at[k] if take is None else piece.at[k, take]
            copies.append(pltpu.make_async_copy(block, where(full, n, c, s, src), sems.at[b, k]))
    for copy in copies:
        copy.start(priority=1)
    return copies


def place_self(full, n, c, s, t):
    return full.at[n * 2 + c, t, s]


def place_cross(full, n, c, s, t):
    return full.at[n, t, c * 2 + s]


def forward(info, spans, *refs, items, tokens, patches):
    pieces = refs[:8]
    (
        h_own, h_oth, keys_hbm, values_hbm, keys_last, values_last, gain1, bias1, gain2, bias2,
        q_own, k_own, v_own, q_oth, k_oth, v_oth, mix, first_sum, first, cross_q, cross_mix, second_sum, second,
        full, small, keys, values, sems, small_sems, image_sems,
    ) = refs[8:]
    stream = info[2]
    copies = fetch(info, pieces, full, sems, place_self, pl.ds(0, full.shape[3]))
    later = fetch(info, pieces, small, small_sems, place_cross, pl.ds(full.shape[3], small.shape[3]))
    for at, (source, target) in enumerate(((keys_hbm, keys), (values_hbm, values))):
        later.append(pltpu.make_async_copy(source, target, image_sems.at[at]))
        later[-1].start(priority=1)
    for copy in copies:
        copy.wait()
    ho, hx = h_own[...], h_oth[...]
    for at, (own, oth) in enumerate(((q_own, q_oth), (k_own, k_oth), (v_own, v_oth))):
        weight = stack_rows(full.at[at])
        own[...] = nt(ho, weight).astype(BF)
        oth[...] = nt(hx, weight).astype(BF)
    width = ho.shape[1]

    def item(i, carry):
        rows = pl.ds(pl.multiple_of(i * tokens, tokens), tokens)
        valid = valid_keys(spans[i], stream, tokens, 4 * tokens)
        for u in range(width // QUAD):
            lanes = slice(u * QUAD, (u + 1) * QUAD)
            near = jnp.concatenate([k_own[rows, lanes], k_oth[rows, lanes]], axis=0)
            mixed = jnp.concatenate([v_own[rows, lanes], v_oth[rows, lanes]], axis=0)
            scores = nt(near, spread_heads(q_own[rows, lanes])) * SCALE
            (probs,) = softmax_keys([jnp.where(valid, scores, NEG)])
            mix[rows, lanes] = collect_heads(tn(probs.astype(BF), mixed)).astype(BF)
        return carry

    lax.fori_loop(0, items, item, 0)
    total = ho.astype(F32) + nn(mix[...], stack_rows(full.at[3]))
    first_sum[...] = total
    normed, _ = norm_stats(total)
    base = normed * gain1[...] + bias1[...]
    first[...] = base
    for copy in later:
        copy.wait()

    @pl.when(stream != 0)
    def _():
        second[...] = base
        second_sum[...] = base

    @pl.when(stream == 0)
    def _():
        cross_q[...] = nt(base.astype(BF), stack_rows(small.at[0])).astype(BF)

        def cross_item(i, carry):
            rows = pl.ds(pl.multiple_of(i * tokens, tokens), tokens)
            patch_rows = pl.ds(pl.multiple_of(i * patches, patches), patches)
            for u in range(width // QUAD):
                lanes = slice(u * QUAD, (u + 1) * QUAD)
                queries = spread_heads(cross_q[rows, lanes])
                scores = nt(keys[patch_rows, lanes], queries) * SCALE
                tail = nt(keys_last[:, lanes], queries) * SCALE
                tail = jnp.where(last_row(i, tail.shape), tail, NEG)
                probs, probs_tail = softmax_keys([scores, tail])
                out = tn(probs.astype(BF), values[patch_rows, lanes]) + tn(probs_tail.astype(BF), values_last[:, lanes])
                cross_mix[rows, lanes] = collect_heads(out).astype(BF)
            return carry

        lax.fori_loop(0, items, cross_item, 0)
        total = base + nn(cross_mix[...], stack_rows(small.at[1]))
        second_sum[...] = total
        normed, _ = norm_stats(total)
        second[...] = normed * gain2[...] + bias2[...]


def valid_keys(span, stream, tokens, columns):
    row = lax.broadcasted_iota(jnp.int32, (2 * tokens, columns), 0)
    own_limit = jnp.where(stream == 0, tokens, span)
    oth_limit = jnp.where(stream == 0, span, tokens)
    return ((row < tokens) & (row < own_limit)) | ((row >= tokens) & (row - tokens < oth_limit))


def image_forward(info, *refs):
    pieces = refs[:8]
    x, x_last, keys, values, keys_last, values_last, full, sems = refs[8:]

    @pl.when(info[2] == 0)
    def _():
        @pl.when(pl.program_id(0) == 0)
        def _():
            copies = fetch(info, pieces, full, sems, place_cross)
            for copy in copies:
                copy.wait()
            keys_last[...] = nt(x_last[...], stack_rows(full.at[0])).astype(BF)
            values_last[...] = nt(x_last[...], stack_rows(full.at[1])).astype(BF)

        keys[...] = nt(x[...], stack_rows(full.at[0])).astype(BF)
        values[...] = nt(x[...], stack_rows(full.at[1])).astype(BF)


def last_row(i, shape):
    return lax.broadcasted_iota(jnp.int32, shape, 0) == i


def ffn_both(info, *refs, pieces):
    weights = refs[:pieces], refs[pieces : 2 * pieces]
    (
        second, cot, gain, bias, out, grad_second, vectors, keep_down, send_down, keep_up, send_up,
        full, ups, acts, stage, sems, out_sems,
    ) = refs[2 * pieces :]
    node, core, me = info[0], info[1], info[3]
    blocks, width = full.shape[0], second.shape[1]
    nodes = keep_up.shape[0]
    copies = []
    for k, mask in enumerate(doubling(blocks)):
        src = jnp.bitwise_xor(me, mask)
        group = []
        for b in range(pieces):
            if pieces == 4:
                share = (1 - node if b & 1 else node) * 2 + (1 - core if b & 2 else core)
            else:
                share = 1 - core if b & 1 else core
            group.append(pltpu.make_async_copy(weights[k // 2][b].at[k % 2], full.at[src, share], sems.at[k, b]))
        for copy in group:
            copy.start()
        copies.append(group)

    written = []

    def emit(slot, value, keep, send, t):
        stage[slot] = value.astype(BF).reshape(stage.shape[1:])
        for n in range(nodes):
            for half, target in enumerate((keep, send)):
                part = n * 2 + (1 - core if half else core)
                copy = pltpu.make_async_copy(stage.at[slot, part], target.at[n, t], out_sems.at[slot, n * 2 + half])
                copy.start()
                written.append(copy)

    x = second[...]
    low = x.astype(BF)
    total = x
    for k, mask in enumerate(doubling(blocks)):
        for copy in copies[k]:
            copy.wait()
        both = stack_rows(full.at[jnp.bitwise_xor(me, mask)])
        up = nn(low, both[:width])
        ups[k] = up
        act = (up * (0.5 * (1.0 + lax.erf(up * 0.7071067811865476)))).astype(BF)
        acts[k] = act
        total = total + nt(act, both[width:])
    normed, inverse = norm_stats(total)
    out[...] = (normed * gain[...] + bias[...]).astype(BF)
    grad_third, grad_gain, grad_bias = norm_back(cot[...].astype(F32), normed, inverse, gain[...])
    vectors[...] = jnp.zeros_like(vectors)
    vectors[0:1] = grad_gain
    vectors[1:2] = grad_bias
    third_low = grad_third.astype(BF)
    for k, mask in enumerate(doubling(blocks)):
        emit(k, tn(third_low, acts[k]), keep_down, send_down, jnp.bitwise_xor(me, mask))
    back = grad_third
    for k, mask in enumerate(doubling(blocks)):
        both = stack_rows(full.at[jnp.bitwise_xor(me, mask)])
        up = ups[k]
        slope = 0.5 * (1.0 + lax.erf(up * 0.7071067811865476)) + up * (
            jnp.exp(-0.5 * up * up) * 0.3989422804014327
        )
        grad_up = (slope * nn(third_low, both[width:])).astype(BF)
        emit(blocks + k, tn(low, grad_up), keep_up, send_up, jnp.bitwise_xor(me, mask))
        back = back + nt(grad_up, both[:width])
    grad_second[...] = back
    for copy in written:
        copy.wait()


def cross_backward(info, *refs, items, tokens, patches):
    pieces = refs[:8]
    (
        grad_second, second_sum, first, first_sum, mix, cross_q, cross_mix, keys, values, keys_last, values_last, gain2, gain1,
        grad_keys, grad_values, grad_keys_last, grad_values_last, grad_first_sum, first_grad_low, vectors, keep, send,
        full, grad_mix, grad_q, stage, sems, out_sems,
    ) = refs[8:]
    is_query = info[2] == 0
    vectors[...] = jnp.zeros_like(vectors)
    blocks = stage.shape[0]
    per = stage.shape[1] // 3

    def write(at, value):
        value = value.astype(BF)
        for b in range(blocks):
            stage[b, at * per : (at + 1) * per, :] = value[b * per : (b + 1) * per]

    def finish(grad_first):
        normed, inverse = norm_stats(first_sum[...])
        out, grad_gain, grad_bias = norm_back(grad_first, normed, inverse, gain1[...])
        vectors[0:1] = grad_gain
        vectors[1:2] = grad_bias
        grad_first_sum[...] = out
        first_grad_low[...] = out.astype(BF)
        write(2, tn(out.astype(BF), mix[...]))

    @pl.when(jnp.logical_not(is_query))
    def _():
        stage[:, : 2 * per, :] = jnp.zeros_like(stage[:, : 2 * per, :])
        finish(grad_second[...])

    @pl.when(is_query)
    def _():
        copies = fetch(info, pieces, full, sems, place_cross, pl.ds(2 * full.shape[3], full.shape[3]))
        normed, inverse = norm_stats(second_sum[...])
        grad_cross, grad_gain, grad_bias = norm_back(grad_second[...], normed, inverse, gain2[...])
        vectors[2:3] = grad_gain
        vectors[3:4] = grad_bias
        low = grad_cross.astype(BF)
        width = low.shape[1]
        write(1, tn(low, cross_mix[...]))
        for copy in copies:
            copy.wait()
        grad_mix[...] = nt(low, stack_rows(full.at[1])).astype(BF)
        grad_keys_last[...] = jnp.zeros_like(grad_keys_last)
        grad_values_last[...] = jnp.zeros_like(grad_values_last)

        def item(i, carry):
            rows = pl.ds(pl.multiple_of(i * tokens, tokens), tokens)
            patch_rows = pl.ds(pl.multiple_of(i * patches, patches), patches)
            for u in range(width // QUAD):
                lanes = slice(u * QUAD, (u + 1) * QUAD)
                key, value = keys[patch_rows, lanes], values[patch_rows, lanes]
                key_last, value_last = keys_last[:, lanes], values_last[:, lanes]
                queries = spread_heads(cross_q[rows, lanes])
                pulls = spread_heads(grad_mix[rows, lanes])
                scores = nt(key, queries) * SCALE
                tail = nt(key_last, queries) * SCALE
                is_last = last_row(i, tail.shape)
                probs = softmax_keys([scores, jnp.where(is_last, tail, NEG)])
                back, back_tail = score_back(probs, [nt(value, pulls), nt(value_last, pulls)])
                grad_keys[patch_rows, lanes] = (nn(back, queries) * SCALE).astype(BF)
                grad_values[patch_rows, lanes] = nn(probs[0].astype(BF), pulls).astype(BF)
                grad_keys_last[:, lanes] += nn(back_tail, queries) * SCALE
                grad_values_last[:, lanes] += nn(probs[1].astype(BF), pulls)
                grad_q[rows, lanes] = (collect_heads(tn(back, key) + tn(back_tail, key_last)) * SCALE).astype(BF)
            return carry

        lax.fori_loop(0, items, item, 0)
        grad_cross_q = grad_q[...]
        write(0, tn(first[...].astype(BF), grad_cross_q))
        finish(grad_cross + nn(grad_cross_q, stack_rows(full.at[0])))

    for copy in send_blocks(stage, keep, send, info[1], out_sems, True):
        copy.wait()


def send_blocks(stage, keep, send, core, sems, swapped):
    nodes, streams = keep.shape[:2][:: -1 if swapped else 1]
    copies = []
    for n in range(nodes):
        for s in range(streams):
            for half, target in enumerate((keep, send)):
                part = (n * 2 + (1 - core if half else core)) * streams + s
                copies.append(pltpu.make_async_copy(
                    stage.at[part], target.at[(s, n) if swapped else (n, s)], sems.at[half, n * streams + s]
                ))
    for copy in copies:
        copy.start()
    return copies


def image_backward(
    info, x, x_last, grad_keys, keys_last, grad_values, values_last, keep, send, stage, sems
):
    blocks, width = stage.shape[0], stage.shape[2]
    image = stage.shape[1] // 2

    @pl.when(info[2] == 0)
    def _():
        for m, (grad, last) in enumerate(((grad_keys, keys_last), (grad_values, values_last))):
            for u in range(width // QUAD):
                lanes = slice(u * QUAD, (u + 1) * QUAD)
                value = (tn(x[...], grad[:, lanes]) + tn(x_last[...], last[:, lanes].astype(BF))).astype(BF)
                for b in range(blocks):
                    stage[b, m * image : (m + 1) * image, lanes] = value[b * image : (b + 1) * image]

    @pl.when(info[2] != 0)
    def _():
        stage[...] = jnp.zeros_like(stage)

    for copy in send_blocks(stage, keep, send, info[1], sems, True):
        copy.wait()


def self_backward(info, spans, *refs, items, tokens):
    pieces = refs[:8]
    (
        h_own, low_own, low_oth, q_own, k_own, v_own, q_oth, k_oth, v_oth, grad_first_sum, vectors12, vectors3,
        grad_input, keep, send, grads, full, pull_own, pull_oth, grad_q, grad_k, grad_v, sems, out_sems,
    ) = refs[8:]
    stream = info[2]
    copies = fetch(info, pieces, full, sems, place_self, pl.ds(0, full.shape[3]))
    for copy in copies:
        copy.wait()
    out_weight = stack_rows(full.at[3])
    pull_own[...] = nt(low_own[...], out_weight).astype(BF)
    pull_oth[...] = nt(low_oth[...], out_weight).astype(BF)
    width = h_own.shape[1]

    def item(i, carry):
        rows = pl.ds(pl.multiple_of(i * tokens, tokens), tokens)
        valid = valid_keys(spans[i], stream, tokens, 8 * tokens)
        for u in range(width // QUAD):
            lanes = slice(u * QUAD, (u + 1) * QUAD)
            keys = jnp.concatenate([k_own[rows, lanes], k_oth[rows, lanes]], axis=0)
            values = jnp.concatenate([v_own[rows, lanes], v_oth[rows, lanes]], axis=0)
            queries = jnp.concatenate([spread_heads(q_own[rows, lanes]), spread_heads(q_oth[rows, lanes])], axis=0)
            pulls = jnp.concatenate([spread_heads(pull_own[rows, lanes]), spread_heads(pull_oth[rows, lanes])], axis=0)
            scores = nt(keys, queries) * SCALE
            probs = softmax_keys([jnp.where(valid, scores, NEG)])
            (back,) = score_back(probs, [nt(values, pulls)])
            own_probs = probs[0].astype(BF)
            grad_k[rows, lanes] = (nn(back[:tokens], queries) * SCALE).astype(BF)
            grad_v[rows, lanes] = nn(own_probs[:tokens], pulls).astype(BF)
            grad_q[rows, lanes] = (collect_heads(tn(back[:, : 4 * tokens], keys)) * SCALE).astype(BF)
        return carry

    lax.fori_loop(0, items, item, 0)
    hidden = h_own[...]
    total = grad_first_sum[...]
    blocks, per = grads.shape[0], width // grads.shape[0]

    def write(at, value):
        value = value.astype(BF)
        for b in range(blocks):
            grads[b, at * per : (at + 1) * per, :] = value[b * per : (b + 1) * per]

    for at, ref in enumerate((grad_q, grad_k, grad_v)):
        value = ref[...]
        write(at, tn(hidden, value))
        total = total + nn(value, stack_rows(full.at[at]))
    tail = grads.shape[1] - 3 * per
    local = width // full.shape[1]
    source = lax.broadcasted_iota(jnp.int32, (width, width), 0)
    target = lax.rem(lax.broadcasted_iota(jnp.int32, (width, width), 1), local)
    lane = lax.broadcasted_iota(jnp.int32, (8, width), 1)

    def spread(vectors, size):
        value = vectors[...].astype(BF)
        parts = [jnp.where(lane // size == p, value, jnp.zeros_like(value)) for p in range(width // size)]
        chosen = jnp.where(lax.rem(source, size) == target, 1.0, 0.0).astype(BF)
        return nn(jnp.concatenate(parts, axis=0), chosen).astype(BF)

    shared, halves = spread(vectors12, per), spread(vectors3, 2 * per)
    for b in range(blocks):
        own = halves[b // 2 * 8 : b // 2 * 8 + 8]
        own = jnp.where(stream == b % 2, own, jnp.zeros_like(own))
        grads[b, 3 * per :, :] = jnp.concatenate([shared[b * 8 : b * 8 + 8], own], axis=0)
    grad_input[...] = total.astype(BF)
    for copy in send_blocks(grads, keep, send, info[1], out_sems, True):
        copy.wait()


VMEM = pl.BlockSpec(memory_space=pltpu.VMEM)
SMEM = pl.BlockSpec(memory_space=pltpu.SMEM)
ANY = pl.BlockSpec(memory_space=pl.ANY)


def shape(dims, kind):
    return jax.ShapeDtypeStruct(tuple(dims), kind)


def call(kernel, out_shapes, specs, scratch, micros, after=(), **more):
    count = len(specs)

    def body(*refs):
        kernel(*refs[:count], *refs[count + len(after) :])

    run = pl.pallas_call(
        body,
        out_shape=out_shapes,
        in_specs=specs + [ANY] * len(after),
        out_specs=more.pop("out_specs", [VMEM] * len(out_shapes)),
        scratch_shapes=scratch,
        compiler_params=pltpu.CompilerParams(vmem_limit_bytes=62 * 1024 * 1024),
        cost_estimate=pl.CostEstimate(flops=int(micros * 1.15e9), bytes_accessed=int(micros * 3.6e6), transcendentals=0),
        **more,
    )
    return lambda *operands: run(*operands, *after)


def pick(array, index, axis):
    return lax.dynamic_index_in_dim(array, index, axis, keepdims=False)


def add(a, b):
    return (a.astype(F32) + b.astype(F32)).astype(BF)


def swap(block, axis, bit=1):
    return lax.ppermute(block, axis, [(i, i ^ bit) for i in range(lax.axis_size(axis))])


def tie(value, *others):
    return jax.tree.map(lambda v: lax.optimization_barrier((v,) + others)[0], value)


def tensor_order(gathered, other, bit):
    upper = jnp.bitwise_and(lax.axis_index("tensor"), bit) != 0
    low, high = jnp.where(upper, other, gathered), jnp.where(upper, gathered, other)
    return jnp.stack([low, high], axis=1).reshape((-1,) + gathered.shape[1:])


def own_piece(pieces):
    pieces = pick(pick(pieces, lax.axis_index("core"), 1), lax.axis_index("stream"), 1)
    if lax.axis_size("node") == 2:
        return [pick(pieces, lax.axis_index("node"), 0)]
    return [pieces[0], pieces[1]]


def halve(pair, axis_name, axis, bit=1):
    keep, arrived = pair
    me = jnp.bitwise_and(lax.axis_index(axis_name) // bit, 1)
    sent = add(pick(keep, 1 - me, axis), pick(arrived, 1 - me, axis))
    kept = add(pick(keep, me, axis), pick(arrived, me, axis))
    return kept, swap(sent, axis_name, bit)


def over_nodes(pair):
    if lax.axis_size("node") == 2:
        return halve(pair, "node", 0)
    total = lax.psum_scatter(add(*pair), "node", scatter_dimension=0, tiled=False)
    return total, jnp.zeros_like(total)


def tensor_step(pair, bit):
    pair = [v.reshape((v.shape[0] // 2, 2) + v.shape[1:]) for v in pair]
    return halve(pair, "tensor", 1, bit)


def finish(pair):
    return (pair[0].astype(F32) + pair[1].astype(F32))[0]


def split_rows(pair):
    count, me = lax.axis_size("tensor"), lax.axis_index("tensor")
    rows, columns = pair[0].shape
    half, local = rows // 2, columns // count

    def kernel(bit, kept, arrived, stays, goes):
        total = (kept[...].astype(F32) + arrived[...].astype(F32)).astype(BF)
        upper = bit[0] == 1
        for p in range(count // 2):
            two = [
                jnp.concatenate([total[:half, t * local : (t + 1) * local], total[half:, t * local : (t + 1) * local]], axis=1)
                for t in (2 * p, 2 * p + 1)
            ]
            stays[p] = jnp.where(upper, two[1], two[0])
            goes[p] = jnp.where(upper, two[0], two[1])

    outs = [shape((count // 2, half, 2 * local), BF)] * 2
    bit = jnp.bitwise_and(me, 1).reshape(1)
    stays, goes = call(kernel, outs, [SMEM, VMEM, VMEM], [], 1, name="split_rows")(bit, *pair)
    return stays, swap(goes, "tensor", 1)


def finish_rows(pair, sizes):
    local = pair[0].shape[2] // 2

    def kernel(kept, arrived, *outs):
        both = kept[0].astype(F32) + arrived[0].astype(F32)
        total = jnp.concatenate([both[:, :local], both[:, local:]], axis=0)
        start = 0
        for out in outs:
            out[...] = total[start : start + out.shape[0]]
            start += out.shape[0]

    outs = [shape((size, local), F32) for size in sizes]
    return call(kernel, outs, [VMEM] * 2, [], 1, name="finish_rows")(*pair)


def shards(
    hidden_in, lengths, image_features, self_q, self_k, self_v, self_out, ln1_gain, ln1_bias,
    cross_q, cross_k, cross_v, cross_out, ln2_gain, ln2_bias, ffn_up, ffn_down, ln3_gain, ln3_bias, cotangent,
):
    nodes, streams, count = lax.axis_size("node"), lax.axis_size("stream"), lax.axis_size("tensor")
    node, core = lax.axis_index("node"), lax.axis_index("core")
    stream, me = lax.axis_index("stream"), lax.axis_index("tensor")
    devices = nodes * 2
    rows_all, width = hidden_in.shape[1:]
    local = self_q.shape[1]
    image_tokens, image_width = image_features.shape[1:]
    patches = image_tokens - 1
    items = lengths.shape[0] // count
    rows = rows_all // count
    tokens = rows // items
    info = jnp.stack([node if nodes == 2 else jnp.int32(0), core, stream, me]).astype(jnp.int32)

    self_pieces = jnp.stack([self_q.T, self_k.T, self_v.T, self_out.T]).reshape(2, 2, 2, local // 2, width)
    small_pieces = jnp.stack([cross_q.T, cross_out.T]).reshape(2, 2, 2, local // 4, width)
    image_pieces = jnp.stack([cross_k.T, cross_v.T]).reshape(2, 2, 2, local // 4, image_width)
    h_own = lax.dynamic_slice_in_dim(hidden_in[0], me * rows, rows, 0)
    h_oth = lax.ppermute(h_own, "stream", SWAP)
    spans = lax.dynamic_slice_in_dim(lengths, me * items, items, 0)
    cot = lax.dynamic_slice_in_dim(cotangent[0], me * rows, rows, 0)
    image = lax.dynamic_slice_in_dim(image_features, me * items, items, 0)
    x = image[:, :patches].reshape(items * patches, image_width)
    x_last = image[:, patches]

    z = lambda vs, bit: [swap(v, "tensor", bit) for v in vs]
    join = lambda a, b: [jnp.concatenate([v, w]) for v, w in zip(a, b)]
    nodes_too = lambda vs: vs + [swap(vs[0], "node")] if nodes == 2 else vs
    cores_too = lambda vs: vs + [swap(v, "core") for v in vs]
    one_way = lambda v: lax.ppermute(v, "stream", [(1, 0)])
    image_0 = [v[None] for v in own_piece(image_pieces)]
    self_0 = [v[None] for v in own_piece(jnp.concatenate([self_pieces, small_pieces], axis=3))]
    ffn_share = 4 if nodes == 2 else 2
    ffn_rows = jnp.concatenate([ffn_up[0], ffn_down[0]], axis=0).reshape(ffn_share, 1, 2 * width // ffn_share, -1)
    ffn_own = pick(ffn_rows, node * 2 + core if nodes == 2 else core, 0)
    ffn_0 = [ffn_own]

    image_1 = z(image_0, 2)
    image_2 = join(tie(image_0, x, h_oth), image_1)
    image_3 = z(image_2, 1)
    self_1 = z(tie(self_0, *image_1), 2)
    image_4 = join(image_2, image_3)
    image_near = nodes_too(image_4)
    image_side = [one_way(image_near[0])]
    self_2 = join(tie(self_0, *image_4), self_1)
    self_3 = z(self_2, 1)
    ffn_1 = z(tie(ffn_0, *self_1, *image_4), 2)
    image_side.append(one_way(tie(image_near[1], image_side[0], *self_3)))
    self_4 = join(self_2, self_3)
    self_near = nodes_too(tie(self_4, image_near[1], image_side[0]))
    image_full = cores_too(image_near + image_side)
    self_side = [swap(tie(self_near[0], image_side[1]), "stream")]

    act_low, act = shape((rows, width), BF), shape((rows, width), F32)
    image_kv, image_kv_last = shape((items * patches, width), BF), shape((items, width), BF)
    dma = pltpu.SemaphoreType.DMA
    self_scratch = pltpu.VMEM((4, count, 2, local // 2, width), BF)
    small_scratch = pltpu.VMEM((2, count, 4, local // 4, width), BF)
    image_scratch = pltpu.VMEM((2, count, 4, local // 4, image_width), BF)
    image_vmem = pltpu.VMEM((items * patches, width), BF)
    row = lambda v: v.reshape(1, width)

    image_keys, image_values, keys_last, values_last = call(
        image_forward,
        [image_kv] * 2 + [image_kv_last] * 2,
        [SMEM] + [ANY] * 8 + [pl.BlockSpec((patches, image_width), lambda i: (i, 0)), pl.BlockSpec((items, image_width), lambda i: (0, 0))],
        [image_scratch, dma((8, count))],
        3,
        after=(),
        grid=(items,),
        out_specs=[pl.BlockSpec((patches, width), lambda i: (i, 0))] * 2 + [pl.BlockSpec((items, width), lambda i: (0, 0))] * 2,
        name="image_forward",
    )(info, *image_full, x, x_last)

    self_side.append(swap(tie(self_near[1], image_keys, self_side[0], *ffn_1), "stream"))
    ffn_2 = join(tie(ffn_0, image_keys), ffn_1)
    ffn_3 = z(ffn_2, 1)
    ffn_near, ffn_late = nodes_too(ffn_2), nodes_too(ffn_3)
    self_full = cores_too(self_near + self_side)

    (
        q_own, k_own, v_own, q_oth, k_oth, v_oth, mix, first_sum, first, cross_queries, cross_mix, second_sum, second,
    ) = call(
        functools.partial(forward, items=items, tokens=tokens, patches=patches),
        [act_low] * 7 + [act] * 2 + [act_low] * 2 + [act] * 2,
        [SMEM, SMEM] + [ANY] * 8 + [VMEM] * 2 + [ANY] * 2 + [VMEM] * 6,
        [self_scratch, small_scratch, image_vmem, image_vmem, dma((8, count)), dma((8, count)), dma((2,))],
        5,
        after=tuple(ffn_3),
        name="forward",
    )(
        info, spans, *self_full, h_own, h_oth, image_keys, image_values, keys_last, values_last,
        row(ln1_gain), row(ln1_bias), row(ln2_gain), row(ln2_bias),
    )

    ffn_late = ffn_late[:-1] + [tie(ffn_late[-1], second)]
    ffn_full = cores_too(ffn_near) + cores_too(ffn_late)
    ffn_pieces = len(ffn_near) * 2
    half_grads = [shape((nodes, count, width // devices, width), BF)] * 2
    output, grad_second, vectors3, keep_down, send_down, keep_up, send_up = call(
        functools.partial(ffn_both, pieces=ffn_pieces),
        [act_low, act, shape((8, width), F32)] + half_grads * 2,
        [SMEM] + [ANY] * (2 * ffn_pieces) + [VMEM] * 4,
        [
            pltpu.VMEM((count, ffn_share, 2 * width // ffn_share, width), BF),
            pltpu.VMEM((count, rows, width), F32),
            pltpu.VMEM((count, rows, width), BF),
            pltpu.VMEM((2 * count, devices, width // devices, width), BF),
            dma((count, ffn_pieces)),
            dma((2 * count, 2 * nodes)),
        ],
        5,
        out_specs=[VMEM] * 3 + [ANY] * 4,
        name="ffn_both",
    )(info, *ffn_full, second, cot, ln3_gain, ln3_bias)
    down_core = keep_down, swap(send_down, "core")
    up_core = keep_up, swap(send_up, "core")
    output_1 = swap(output[None], "tensor", 2)
    down_nodes = over_nodes(down_core)
    blocks = devices * streams
    per, image_per, wide_per = width // blocks, image_width // blocks, width // devices
    tail = 16
    halves_of = lambda r, first=streams, then=nodes: [shape((first, then, r, width), BF)] * 2

    grad_keys, grad_values, grad_keys_last, grad_values_last, grad_first_sum, low_own, vectors12, keep_square, send_square = call(
        functools.partial(cross_backward, items=items, tokens=tokens, patches=patches),
        [
            image_kv, image_kv, shape((items, width), F32), shape((items, width), F32), act, act_low, shape((8, width), F32),
            *halves_of(3 * per),
        ],
        [SMEM] + [ANY] * 8 + [VMEM] * 13,
        [
            small_scratch, pltpu.VMEM((rows, width), BF), pltpu.VMEM((rows, width), BF),
            pltpu.VMEM((blocks, 3 * per, width), BF), dma((8, count)), dma((2, nodes * streams)),
        ],
        5,
        after=(down_nodes[0],),
        out_specs=[VMEM] * 7 + [ANY] * 2,
        name="cross_backward",
    )(
        info, *self_full, grad_second, second_sum, first, first_sum, mix, cross_queries, cross_mix, image_keys, image_values,
        keys_last, values_last, row(ln2_gain), row(ln1_gain),
    )
    ended = output_1, down_nodes[1], up_core[1]
    low_oth = swap(tie(low_own, *ended), "stream")
    square_core = keep_square, swap(tie(send_square, *ended), "core")
    output_2 = tensor_order(tie(output[None], low_own), output_1, 2)
    output_3 = swap(output_2, "tensor", 1)
    up_nodes = over_nodes(tie(up_core, low_own))
    down_half = tensor_step(tie(down_nodes, low_own), 1)
    square_stream = halve(tie(square_core, low_oth), "stream", 0)
    grad_input, keep_self, send_self = call(
        functools.partial(self_backward, items=items, tokens=tokens),
        [act_low] + halves_of(3 * per + tail),
        [SMEM, SMEM] + [ANY] * 8 + [VMEM] * 12,
        [pltpu.VMEM((blocks, 3 * per + tail, width), BF), self_scratch]
        + [pltpu.VMEM((rows, width), BF)] * 5
        + [dma((8, count)), dma((2, nodes * streams))],
        3,
        out_specs=[VMEM] + [ANY] * 2,
        after=(up_nodes[0], down_half[0], square_stream[0], output_2),
        name="self_backward",
    )(info, spans, *self_full, h_own, low_own, low_oth, q_own, k_own, v_own, q_oth, k_oth, v_oth, grad_first_sum, vectors12, vectors3)

    ended = up_nodes[1], down_half[1], square_stream[1], output_3
    self_core = keep_self, swap(tie(send_self, *ended), "core")
    up_half = tensor_step(tie(up_nodes, grad_input), 1)
    grad_1 = swap(grad_input[None], "tensor", 2)
    square_nodes = over_nodes(tie(square_stream, grad_input))
    self_stream = halve(self_core, "stream", 0)
    keep_image, send_image = call(
        image_backward,
        halves_of(2 * image_per),
        [SMEM] + [VMEM] * 6,
        [pltpu.VMEM((blocks, 2 * image_per, width), BF), dma((2, nodes * streams))],
        5,
        after=(self_stream[0], square_nodes[0], up_half[0]),
        out_specs=[ANY] * 2,
        name="image_backward",
    )(info, x, x_last, grad_keys, grad_keys_last, grad_values, grad_values_last)

    ended = up_half[1], grad_1, square_nodes[1], self_stream[1]
    image_core = keep_image, swap(tie(send_image, *ended), "core")
    image_stream = halve(image_core, "stream", 0)
    step = image_stream[0]
    grad_2 = tensor_order(tie(grad_input[None], step), grad_1, 2)
    grad_3 = swap(grad_2, "tensor", 1)
    down_quarter = tensor_step(tie(down_half, step), 2)
    self_nodes = over_nodes(tie(self_stream, step))
    square_half = split_rows(tie(square_nodes, step))
    image_nodes = over_nodes(image_stream)
    step = image_nodes[0]
    self_half = split_rows(tie(self_nodes, step))
    up_quarter = tensor_step(tie(up_half, step), 2)
    square_quarter = tensor_step(tie(square_half, step), 2)
    output_4 = tensor_order(tie(output_2, step), output_3, 1)
    down_sum = finish(tie(down_quarter, step))
    image_half = split_rows(image_nodes)
    step = image_half[0]
    self_quarter = tensor_step(tie(self_half, step), 2)
    square_q, square_o, self_o = finish_rows(tie(square_quarter, step), (per, per, per))
    image_quarter = tensor_step(image_half, 2)
    step = image_quarter[0]
    grad_input = tensor_order(tie(grad_2, step), grad_3, 1)
    up_sum = finish(tie(up_quarter, step))
    self_q, self_k, self_v, vectors = finish_rows(tie(self_quarter, step), (per, per, per, tail))
    image_k, image_v = finish_rows(tie(image_quarter, up_sum, grad_input, self_q), (image_per, image_per))

    vector = lambda r, n: vectors[r, :n]
    return (
        output_4.reshape(1, rows_all, width),
        grad_input.reshape(1, rows_all, width),
        self_q,
        self_k,
        self_v,
        self_o,
        vector(0, per),
        vector(1, per),
        square_q,
        image_k,
        image_v,
        square_o,
        vector(2, per),
        vector(3, per),
        up_sum[None],
        down_sum[None],
        vector(8, wide_per)[None],
        vector(9, wide_per)[None],
    )


def solution(mesh):
    sizes = mesh.devices.shape
    fine = Mesh(mesh.devices.reshape(sizes[0] // 2, 2, *sizes[1:]), ("node", "core", "stream", "tensor"))
    weight = P(None, "tensor")
    in_specs = (
        P("stream", DP, None), P(DP), P(DP, None, None), weight, weight, weight, weight, P(), P(),
        weight, weight, weight, weight, P(), P(), P("stream", None, "tensor"), P("stream", None, "tensor"),
        P("stream", None), P("stream", None), P("stream", DP, None),
    )
    over = ("node", "core", "stream")
    square, flat = P(over, "tensor"), P(over)
    out_specs = (
        P("stream", DP, None), P("stream", DP, None), square, square, square, square, flat, flat,
        square, square, square, square, flat, flat, P("stream", DP, "tensor"), P("stream", DP, "tensor"),
        P("stream", DP), P("stream", DP),
    )
    return jax.shard_map(shards, mesh=fine, in_specs=in_specs, out_specs=out_specs, check_vma=False)
```

```python
import functools

import jax
import jax.numpy as jnp
from jax import lax
from jax.experimental import pallas as pl
from jax.experimental.pallas import tpu as pltpu
from jax.sharding import Mesh, PartitionSpec as P

HD = 64
QUAD = 256
EPSILON = 1e-06
BF = jnp.bfloat16
F32 = jnp.float32
DP = ("node", "core")
SWAP = [(0, 1), (1, 0)]
SCALE = 0.125
NEG = -1e30


def nn(a, b):
    return lax.dot_general(a, b, (((1,), (0,)), ((), ())), preferred_element_type=F32)


def nt(a, b):
    return lax.dot_general(a, b, (((1,), (1,)), ((), ())), preferred_element_type=F32)


def tn(a, b):
    return lax.dot_general(a, b, (((0,), (0,)), ((), ())), preferred_element_type=F32)


def norm_stats(v):
    center = v - jnp.mean(v, axis=-1, keepdims=True)
    inverse = lax.rsqrt(jnp.mean(center * center, axis=-1, keepdims=True) + EPSILON)
    return center * inverse, inverse


def norm_back(e, normed, inverse, gain):
    scaled = e * gain
    out = inverse * (
        scaled
        - jnp.mean(scaled, axis=-1, keepdims=True)
        - normed * jnp.mean(scaled * normed, axis=-1, keepdims=True)
    )
    return out, jnp.sum(e * normed, axis=0, keepdims=True), jnp.sum(e, axis=0, keepdims=True)


def head_masks(rows):
    lane = lax.broadcasted_iota(jnp.int32, (rows, QUAD), 1) // HD
    return [jnp.where(lane == j, 1.0, 0.0).astype(BF) for j in range(QUAD // HD)]


def spread_heads(x, masks):
    return jnp.concatenate([x * mask for mask in masks], axis=0)


def collect_heads(x):
    rows = x.shape[0] * HD // QUAD
    lane = lax.broadcasted_iota(jnp.int32, (rows, QUAD), 1) // HD
    out = x[:rows]
    for j in range(1, QUAD // HD):
        out = jnp.where(lane == j, x[j * rows : (j + 1) * rows], out)
    return out


def softmax_keys(parts):
    peak = functools.reduce(jnp.maximum, [jnp.max(p, axis=0, keepdims=True) for p in parts])
    weights = [jnp.exp(p - peak) for p in parts]
    total = sum(jnp.sum(w, axis=0, keepdims=True) for w in weights)
    inverse = 1.0 / total
    return [w * inverse for w in weights]


def score_back(probs, grads):
    total = sum(jnp.sum(p * g, axis=0, keepdims=True) for p, g in zip(probs, grads))
    return [(p * (g - total)).astype(BF) for p, g in zip(probs, grads)]


def stack_rows(ref):
    value = ref[...]
    return value.reshape(-1, value.shape[-1])


def doubling(count):
    order, bit = [0], count // 2
    while bit:
        order = order + [mask | bit for mask in order]
        bit //= 2
    return order


def fetch(info, pieces, full, sems, where, take=None):
    node, core, stream, me = info[0], info[1], info[2], info[3]
    count = pieces[0].shape[0]
    copies = []
    for b, piece in enumerate(pieces):
        n = 1 - node if b & 1 else node
        s = 1 - stream if b & 2 else stream
        c = 1 - core if b & 4 else core
        for k, mask in enumerate(doubling(count)):
            src = jnp.bitwise_xor(me, mask)
            block = piece.at[k] if take is None else piece.at[k, take]
            copies.append(pltpu.make_async_copy(block, where(full, n, c, s, src), sems.at[b, k]))
    for copy in copies:
        copy.start(priority=1)
    return copies


def place_self(full, n, c, s, t):
    return full.at[n * 2 + c, t, s]


def place_cross(full, n, c, s, t):
    return full.at[n, t, c * 2 + s]


def forward(info, spans, *refs, items, tokens, patches):
    pieces = refs[:8]
    (
        h_own, h_oth, keys_hbm, values_hbm, keys_last, values_last, gain1, bias1, gain2, bias2,
        q_own, k_own, v_own, q_oth, k_oth, v_oth, mix, first_sum, first, cross_q, cross_mix, second_sum, second,
        full, small, keys, values, sems, small_sems, image_sems,
    ) = refs[8:]
    stream = info[2]
    copies = fetch(info, pieces, full, sems, place_self, pl.ds(0, full.shape[3]))
    later = fetch(info, pieces, small, small_sems, place_cross, pl.ds(full.shape[3], small.shape[3]))
    for at, (source, target) in enumerate(((keys_hbm, keys), (values_hbm, values))):
        later.append(pltpu.make_async_copy(source, target, image_sems.at[at]))
        later[-1].start(priority=1)
    for copy in copies:
        copy.wait()
    ho, hx = h_own[...], h_oth[...]
    for at, (own, oth) in enumerate(((q_own, q_oth), (k_own, k_oth), (v_own, v_oth))):
        weight = stack_rows(full.at[at])
        own[...] = nt(ho, weight).astype(BF)
        oth[...] = nt(hx, weight).astype(BF)
    width = ho.shape[1]

    masks = head_masks(tokens)

    def item(i, carry):
        rows = pl.ds(pl.multiple_of(i * tokens, tokens), tokens)
        valid = valid_keys(spans[i], stream, tokens, 4 * tokens)
        for u in range(width // QUAD):
            lanes = slice(u * QUAD, (u + 1) * QUAD)
            near = jnp.concatenate([k_own[rows, lanes], k_oth[rows, lanes]], axis=0)
            mixed = jnp.concatenate([v_own[rows, lanes], v_oth[rows, lanes]], axis=0)
            scores = nt(near, spread_heads(q_own[rows, lanes] * BF(SCALE), masks))
            (probs,) = softmax_keys([jnp.where(valid, scores, NEG)])
            mix[rows, lanes] = collect_heads(tn(probs.astype(BF), mixed)).astype(BF)
        return carry

    lax.fori_loop(0, items, item, 0, unroll=2)
    total = ho.astype(F32) + nn(mix[...], stack_rows(full.at[3]))
    first_sum[...] = total
    normed, _ = norm_stats(total)
    base = normed * gain1[...] + bias1[...]
    first[...] = base
    for copy in later:
        copy.wait()

    @pl.when(stream != 0)
    def _():
        second[...] = base
        second_sum[...] = base

    @pl.when(stream == 0)
    def _():
        cross_q[...] = nt(base.astype(BF), stack_rows(small.at[0])).astype(BF)

        def cross_item(i, carry):
            rows = pl.ds(pl.multiple_of(i * tokens, tokens), tokens)
            patch_rows = pl.ds(pl.multiple_of(i * patches, patches), patches)
            for u in range(width // QUAD):
                lanes = slice(u * QUAD, (u + 1) * QUAD)
                queries = spread_heads(cross_q[rows, lanes] * BF(SCALE), masks)
                scores = nt(keys[patch_rows, lanes], queries)
                tail = nt(keys_last[:, lanes], queries)
                tail = jnp.where(last_row(i, tail.shape), tail, NEG)
                probs, probs_tail = softmax_keys([scores, tail])
                out = tn(probs.astype(BF), values[patch_rows, lanes]) + tn(probs_tail.astype(BF), values_last[:, lanes])
                cross_mix[rows, lanes] = collect_heads(out).astype(BF)
            return carry

        lax.fori_loop(0, items, cross_item, 0, unroll=2)
        total = base + nn(cross_mix[...], stack_rows(small.at[1]))
        second_sum[...] = total
        normed, _ = norm_stats(total)
        second[...] = normed * gain2[...] + bias2[...]


def valid_keys(span, stream, tokens, columns):
    row = lax.broadcasted_iota(jnp.int32, (2 * tokens, columns), 0)
    own_limit = jnp.where(stream == 0, tokens, span)
    oth_limit = jnp.where(stream == 0, span, tokens)
    return ((row < tokens) & (row < own_limit)) | ((row >= tokens) & (row - tokens < oth_limit))


def image_forward(info, *refs):
    pieces = refs[:8]
    x, x_last, keys, values, keys_last, values_last, full, sems = refs[8:]

    @pl.when(info[2] == 0)
    def _():
        @pl.when(pl.program_id(0) == 0)
        def _():
            copies = fetch(info, pieces, full, sems, place_cross)
            for copy in copies:
                copy.wait()
            keys_last[...] = nt(x_last[...], stack_rows(full.at[0])).astype(BF)
            values_last[...] = nt(x_last[...], stack_rows(full.at[1])).astype(BF)

        keys[...] = nt(x[...], stack_rows(full.at[0])).astype(BF)
        values[...] = nt(x[...], stack_rows(full.at[1])).astype(BF)


def last_row(i, shape):
    return lax.broadcasted_iota(jnp.int32, shape, 0) == i


def ffn_both(info, *refs, pieces):
    weights = refs[:pieces], refs[pieces : 2 * pieces]
    (
        second, cot, gain, bias, out, grad_second, vectors, keep_down, send_down, keep_up, send_up,
        full, ups, acts, stage, sems, out_sems,
    ) = refs[2 * pieces :]
    node, core, me = info[0], info[1], info[3]
    blocks, width = full.shape[0], second.shape[1]
    nodes = keep_up.shape[0]
    copies = []
    for k, mask in enumerate(doubling(blocks)):
        src = jnp.bitwise_xor(me, mask)
        group = []
        for b in range(pieces):
            if pieces == 4:
                share = (1 - node if b & 1 else node) * 2 + (1 - core if b & 2 else core)
            else:
                share = 1 - core if b & 1 else core
            group.append(pltpu.make_async_copy(weights[k // 2][b].at[k % 2], full.at[src, share], sems.at[k, b]))
        for copy in group:
            copy.start()
        copies.append(group)

    written = []

    def emit(slot, value, keep, send, t):
        stage[slot] = value.astype(BF).reshape(stage.shape[1:])
        for n in range(nodes):
            for half, target in enumerate((keep, send)):
                part = n * 2 + (1 - core if half else core)
                copy = pltpu.make_async_copy(stage.at[slot, part], target.at[n, t], out_sems.at[slot, n * 2 + half])
                copy.start()
                written.append(copy)

    x = second[...]
    low = x.astype(BF)
    total = x
    for k, mask in enumerate(doubling(blocks)):
        for copy in copies[k]:
            copy.wait()
        both = stack_rows(full.at[jnp.bitwise_xor(me, mask)])
        up = nn(low, both[:width])
        ups[k] = up
        act = (up * (0.5 * (1.0 + lax.erf(up * 0.7071067811865476)))).astype(BF)
        acts[k] = act
        total = total + nt(act, both[width:])
    normed, inverse = norm_stats(total)
    out[...] = (normed * gain[...] + bias[...]).astype(BF)
    grad_third, grad_gain, grad_bias = norm_back(cot[...].astype(F32), normed, inverse, gain[...])
    vectors[...] = jnp.zeros_like(vectors)
    vectors[0:1] = grad_gain
    vectors[1:2] = grad_bias
    third_low = grad_third.astype(BF)
    for k, mask in enumerate(doubling(blocks)):
        emit(k, tn(third_low, acts[k]), keep_down, send_down, jnp.bitwise_xor(me, mask))
    back = grad_third
    for k, mask in enumerate(doubling(blocks)):
        both = stack_rows(full.at[jnp.bitwise_xor(me, mask)])
        up = ups[k]
        slope = 0.5 * (1.0 + lax.erf(up * 0.7071067811865476)) + up * (
            jnp.exp(-0.5 * up * up) * 0.3989422804014327
        )
        grad_up = (slope * nn(third_low, both[width:])).astype(BF)
        emit(blocks + k, tn(low, grad_up), keep_up, send_up, jnp.bitwise_xor(me, mask))
        back = back + nt(grad_up, both[:width])
    grad_second[...] = back
    for copy in written:
        copy.wait()


def cross_backward(info, *refs, items, tokens, patches):
    pieces = refs[:8]
    (
        grad_second, second_sum, first, first_sum, mix, cross_q, cross_mix, keys, values, keys_last, values_last, gain2, gain1,
        grad_keys, grad_values, grad_keys_last, grad_values_last, grad_first_sum, first_grad_low, vectors, keep, send,
        full, grad_mix, grad_q, stage, sems, out_sems,
    ) = refs[8:]
    is_query = info[2] == 0
    vectors[...] = jnp.zeros_like(vectors)
    blocks = stage.shape[0]
    per = stage.shape[1] // 3

    def write(at, value):
        value = value.astype(BF)
        for b in range(blocks):
            stage[b, at * per : (at + 1) * per, :] = value[b * per : (b + 1) * per]

    def finish(grad_first):
        normed, inverse = norm_stats(first_sum[...])
        out, grad_gain, grad_bias = norm_back(grad_first, normed, inverse, gain1[...])
        vectors[0:1] = grad_gain
        vectors[1:2] = grad_bias
        grad_first_sum[...] = out
        first_grad_low[...] = out.astype(BF)
        write(2, tn(out.astype(BF), mix[...]))

    @pl.when(jnp.logical_not(is_query))
    def _():
        stage[:, : 2 * per, :] = jnp.zeros_like(stage[:, : 2 * per, :])
        finish(grad_second[...])

    @pl.when(is_query)
    def _():
        copies = fetch(info, pieces, full, sems, place_cross, pl.ds(2 * full.shape[3], full.shape[3]))
        normed, inverse = norm_stats(second_sum[...])
        grad_cross, grad_gain, grad_bias = norm_back(grad_second[...], normed, inverse, gain2[...])
        vectors[2:3] = grad_gain
        vectors[3:4] = grad_bias
        low = grad_cross.astype(BF)
        width = low.shape[1]
        write(1, tn(low, cross_mix[...]))
        for copy in copies:
            copy.wait()
        grad_mix[...] = nt(low, stack_rows(full.at[1])).astype(BF)
        grad_keys_last[...] = jnp.zeros_like(grad_keys_last)
        grad_values_last[...] = jnp.zeros_like(grad_values_last)
        masks = head_masks(tokens)

        def item(i, carry):
            rows = pl.ds(pl.multiple_of(i * tokens, tokens), tokens)
            patch_rows = pl.ds(pl.multiple_of(i * patches, patches), patches)
            for u in range(width // QUAD):
                lanes = slice(u * QUAD, (u + 1) * QUAD)
                key, value = keys[patch_rows, lanes], values[patch_rows, lanes]
                key_last, value_last = keys_last[:, lanes], values_last[:, lanes]
                queries = spread_heads(cross_q[rows, lanes] * BF(SCALE), masks)
                pulls = spread_heads(grad_mix[rows, lanes], masks)
                scores = nt(key, queries)
                tail = nt(key_last, queries)
                is_last = last_row(i, tail.shape)
                probs = softmax_keys([scores, jnp.where(is_last, tail, NEG)])
                back, back_tail = score_back(probs, [nt(value, pulls), nt(value_last, pulls)])
                grad_keys[patch_rows, lanes] = nn(back, queries).astype(BF)
                grad_values[patch_rows, lanes] = nn(probs[0].astype(BF), pulls).astype(BF)
                grad_keys_last[:, lanes] += nn(back_tail, queries)
                grad_values_last[:, lanes] += nn(probs[1].astype(BF), pulls)
                grad_q[rows, lanes] = (collect_heads(tn(back, key) + tn(back_tail, key_last)) * SCALE).astype(BF)
            return carry

        lax.fori_loop(0, items, item, 0, unroll=2)
        grad_cross_q = grad_q[...]
        write(0, tn(first[...].astype(BF), grad_cross_q))
        finish(grad_cross + nn(grad_cross_q, stack_rows(full.at[0])))

    for copy in send_blocks(stage, keep, send, info[1], out_sems, True):
        copy.wait()


def send_blocks(stage, keep, send, core, sems, swapped):
    nodes, streams = keep.shape[:2][:: -1 if swapped else 1]
    copies = []
    for n in range(nodes):
        for s in range(streams):
            for half, target in enumerate((keep, send)):
                part = (n * 2 + (1 - core if half else core)) * streams + s
                copies.append(pltpu.make_async_copy(
                    stage.at[part], target.at[(s, n) if swapped else (n, s)], sems.at[half, n * streams + s]
                ))
    for copy in copies:
        copy.start()
    return copies


def image_backward(
    info, x, x_last, grad_keys, keys_last, grad_values, values_last,
    keep_keys, send_keys, keep_values, send_values, stage_keys, stage_values, sems,
):
    blocks, image, width = stage_keys.shape
    copies = []
    for m, (grad, last, stage, keep, send) in enumerate((
        (grad_keys, keys_last, stage_keys, keep_keys, send_keys),
        (grad_values, values_last, stage_values, keep_values, send_values),
    )):
        @pl.when(info[2] == 0)
        def _():
            for u in range(width // QUAD):
                lanes = slice(u * QUAD, (u + 1) * QUAD)
                value = (tn(x[...], grad[:, lanes]) + tn(x_last[...], last[:, lanes].astype(BF))).astype(BF)
                for b in range(blocks):
                    stage[b, :, lanes] = value[b * image : (b + 1) * image]

        @pl.when(info[2] != 0)
        def _():
            stage[...] = jnp.zeros_like(stage)

        copies += send_blocks(stage, keep, send, info[1], sems.at[m], m == 0)
    for copy in copies:
        copy.wait()


def self_backward(info, spans, *refs, items, tokens):
    pieces = refs[:8]
    (
        h_own, low_own, low_oth, q_own, k_own, v_own, q_oth, k_oth, v_oth, grad_first_sum, vectors12, vectors3,
        grad_input, keep, send, grads, full, pull_own, pull_oth, grad_q, grad_k, grad_v, sems, out_sems,
    ) = refs[8:]
    stream = info[2]
    copies = fetch(info, pieces, full, sems, place_self, pl.ds(0, full.shape[3]))
    for copy in copies:
        copy.wait()
    out_weight = stack_rows(full.at[3])
    pull_own[...] = nt(low_own[...], out_weight).astype(BF)
    pull_oth[...] = nt(low_oth[...], out_weight).astype(BF)
    width = h_own.shape[1]
    masks = head_masks(tokens)

    def item(i, carry):
        rows = pl.ds(pl.multiple_of(i * tokens, tokens), tokens)
        valid = valid_keys(spans[i], stream, tokens, 8 * tokens)
        for u in range(width // QUAD):
            lanes = slice(u * QUAD, (u + 1) * QUAD)
            keys = jnp.concatenate([k_own[rows, lanes], k_oth[rows, lanes]], axis=0)
            values = jnp.concatenate([v_own[rows, lanes], v_oth[rows, lanes]], axis=0)
            both = [spread_heads(q[rows, lanes] * BF(SCALE), masks) for q in (q_own, q_oth)]
            queries = jnp.concatenate(both, axis=0)
            pulls = jnp.concatenate([spread_heads(pull[rows, lanes], masks) for pull in (pull_own, pull_oth)], axis=0)
            scores = nt(keys, queries)
            probs = softmax_keys([jnp.where(valid, scores, NEG)])
            (back,) = score_back(probs, [nt(values, pulls)])
            own_probs = probs[0].astype(BF)
            grad_k[rows, lanes] = nn(back[:tokens], queries).astype(BF)
            grad_v[rows, lanes] = nn(own_probs[:tokens], pulls).astype(BF)
            grad_q[rows, lanes] = (collect_heads(tn(back[:, : 4 * tokens], keys)) * SCALE).astype(BF)
        return carry

    lax.fori_loop(0, items, item, 0, unroll=2)
    hidden = h_own[...]
    total = grad_first_sum[...]
    blocks, per = grads.shape[0], width // grads.shape[0]

    def write(at, value):
        value = value.astype(BF)
        for b in range(blocks):
            grads[b, at * per : (at + 1) * per, :] = value[b * per : (b + 1) * per]

    for at, ref in enumerate((grad_q, grad_k, grad_v)):
        value = ref[...]
        write(at, tn(hidden, value))
        total = total + nn(value, stack_rows(full.at[at]))
    tail = grads.shape[1] - 3 * per
    local = width // full.shape[1]
    source = lax.broadcasted_iota(jnp.int32, (width, width), 0)
    target = lax.rem(lax.broadcasted_iota(jnp.int32, (width, width), 1), local)
    lane = lax.broadcasted_iota(jnp.int32, (8, width), 1)

    def spread(vectors, size):
        value = vectors[...].astype(BF)
        parts = [jnp.where(lane // size == p, value, jnp.zeros_like(value)) for p in range(width // size)]
        chosen = jnp.where(lax.rem(source, size) == target, 1.0, 0.0).astype(BF)
        return nn(jnp.concatenate(parts, axis=0), chosen).astype(BF)

    shared, halves = spread(vectors12, per), spread(vectors3, 2 * per)
    for b in range(blocks):
        own = halves[b // 2 * 8 : b // 2 * 8 + 8]
        own = jnp.where(stream == b % 2, own, jnp.zeros_like(own))
        grads[b, 3 * per :, :] = jnp.concatenate([shared[b * 8 : b * 8 + 8], own], axis=0)
    grad_input[...] = total.astype(BF)
    for copy in send_blocks(grads, keep, send, info[1], out_sems, True):
        copy.wait()


VMEM = pl.BlockSpec(memory_space=pltpu.VMEM)
SMEM = pl.BlockSpec(memory_space=pltpu.SMEM)
ANY = pl.BlockSpec(memory_space=pl.ANY)


def shape(dims, kind):
    return jax.ShapeDtypeStruct(tuple(dims), kind)


def call(kernel, out_shapes, specs, scratch, micros, after=(), **more):
    count = len(specs)

    def body(*refs):
        kernel(*refs[:count], *refs[count + len(after) :])

    run = pl.pallas_call(
        body,
        out_shape=out_shapes,
        in_specs=specs + [ANY] * len(after),
        out_specs=more.pop("out_specs", [VMEM] * len(out_shapes)),
        scratch_shapes=scratch,
        compiler_params=pltpu.CompilerParams(vmem_limit_bytes=62 * 1024 * 1024),
        cost_estimate=pl.CostEstimate(flops=int(micros * 1.15e9), bytes_accessed=int(micros * 3.6e6), transcendentals=0),
        **more,
    )
    return lambda *operands: run(*operands, *after)


def pick(array, index, axis):
    return lax.dynamic_index_in_dim(array, index, axis, keepdims=False)


def add(a, b):
    return (a.astype(F32) + b.astype(F32)).astype(BF)


def swap(block, axis, bit=1):
    return lax.ppermute(block, axis, [(i, i ^ bit) for i in range(lax.axis_size(axis))])


def tie(value, *others):
    return jax.tree.map(lambda v: lax.optimization_barrier((v,) + others)[0], value)


def tensor_order(gathered, other, bit):
    upper = jnp.bitwise_and(lax.axis_index("tensor"), bit) != 0
    low, high = jnp.where(upper, other, gathered), jnp.where(upper, gathered, other)
    return jnp.stack([low, high], axis=1).reshape((-1,) + gathered.shape[1:])


def own_piece(pieces):
    pieces = pick(pick(pieces, lax.axis_index("core"), 1), lax.axis_index("stream"), 1)
    if lax.axis_size("node") == 2:
        return [pick(pieces, lax.axis_index("node"), 0)]
    return [pieces[0], pieces[1]]


def halve(pair, axis_name, axis, bit=1):
    keep, arrived = pair
    me = jnp.bitwise_and(lax.axis_index(axis_name) // bit, 1)
    sent = add(pick(keep, 1 - me, axis), pick(arrived, 1 - me, axis))
    kept = add(pick(keep, me, axis), pick(arrived, me, axis))
    return kept, swap(sent, axis_name, bit)


def over_nodes(pair):
    if lax.axis_size("node") == 2:
        return halve(pair, "node", 0)
    total = lax.psum_scatter(add(*pair), "node", scatter_dimension=0, tiled=False)
    return total, jnp.zeros_like(total)


def tensor_step(pair, bit):
    pair = [v.reshape((v.shape[0] // 2, 2) + v.shape[1:]) for v in pair]
    return halve(pair, "tensor", 1, bit)


def finish(pair):
    return (pair[0].astype(F32) + pair[1].astype(F32))[0]


def split_rows(*pairs):
    count, me = lax.axis_size("tensor"), lax.axis_index("tensor")
    rows, columns = sum(pair[0].shape[0] for pair in pairs), pairs[0][0].shape[1]
    half, local = rows // 2, columns // count

    def kernel(bit, *refs):
        *inputs, stays, goes = refs
        totals = [
            (kept[...].astype(F32) + arrived[...].astype(F32)).astype(BF) for kept, arrived in zip(inputs[::2], inputs[1::2])
        ]
        total = jnp.concatenate(totals, axis=0)
        upper = bit[0] == 1
        for p in range(count // 2):
            two = [
                jnp.concatenate([total[:half, t * local : (t + 1) * local], total[half:, t * local : (t + 1) * local]], axis=1)
                for t in (2 * p, 2 * p + 1)
            ]
            stays[p] = jnp.where(upper, two[1], two[0])
            goes[p] = jnp.where(upper, two[0], two[1])

    outs = [shape((count // 2, half, 2 * local), BF)] * 2
    bit = jnp.bitwise_and(me, 1).reshape(1)
    operands = [v for pair in pairs for v in pair]
    stays, goes = call(kernel, outs, [SMEM] + [VMEM] * len(operands), [], 1, name="split_rows")(bit, *operands)
    return stays, swap(goes, "tensor", 1)


def finish_rows(plain, *packs):
    local = packs[0][0][0].shape[2] // 2

    def kernel(*refs):
        inputs, outs = refs[: 2 + 2 * len(packs)], refs[2 + 2 * len(packs) :]
        outs[0][...] = inputs[0][0].astype(F32) + inputs[1][0].astype(F32)
        at = 1
        for p, (_, sizes) in enumerate(packs):
            both = inputs[2 + 2 * p][0].astype(F32) + inputs[3 + 2 * p][0].astype(F32)
            total = jnp.concatenate([both[:, :local], both[:, local:]], axis=0)
            start = 0
            for size in sizes:
                outs[at][...] = total[start : start + size]
                start += size
                at += 1

    outs = [shape(plain[0].shape[1:], F32)] + [shape((size, local), F32) for _, sizes in packs for size in sizes]
    operands = [*plain, *(v for pair, _ in packs for v in pair)]
    return call(kernel, outs, [VMEM] * len(operands), [], 1, name="finish_rows")(*operands)


def shards(
    hidden_in, lengths, image_features, self_q, self_k, self_v, self_out, ln1_gain, ln1_bias,
    cross_q, cross_k, cross_v, cross_out, ln2_gain, ln2_bias, ffn_up, ffn_down, ln3_gain, ln3_bias, cotangent,
):
    nodes, streams, count = lax.axis_size("node"), lax.axis_size("stream"), lax.axis_size("tensor")
    node, core = lax.axis_index("node"), lax.axis_index("core")
    stream, me = lax.axis_index("stream"), lax.axis_index("tensor")
    devices = nodes * 2
    rows_all, width = hidden_in.shape[1:]
    local = self_q.shape[1]
    image_tokens, image_width = image_features.shape[1:]
    patches = image_tokens - 1
    items = lengths.shape[0] // count
    rows = rows_all // count
    tokens = rows // items
    info = jnp.stack([node if nodes == 2 else jnp.int32(0), core, stream, me]).astype(jnp.int32)

    self_pieces = jnp.stack([self_q.T, self_k.T, self_v.T, self_out.T]).reshape(2, 2, 2, local // 2, width)
    small_pieces = jnp.stack([cross_q.T, cross_out.T]).reshape(2, 2, 2, local // 4, width)
    image_pieces = jnp.stack([cross_k.T, cross_v.T]).reshape(2, 2, 2, local // 4, image_width)
    h_own = lax.dynamic_slice_in_dim(hidden_in[0], me * rows, rows, 0)
    h_oth = lax.ppermute(h_own, "stream", SWAP)
    spans = lax.dynamic_slice_in_dim(lengths, me * items, items, 0)
    cot = lax.dynamic_slice_in_dim(cotangent[0], me * rows, rows, 0)
    image = lax.dynamic_slice_in_dim(image_features, me * items, items, 0)
    x = image[:, :patches].reshape(items * patches, image_width)
    x_last = image[:, patches]

    z = lambda vs, bit: [swap(v, "tensor", bit) for v in vs]
    join = lambda a, b: [jnp.concatenate([v, w]) for v, w in zip(a, b)]
    nodes_too = lambda vs: vs + [swap(vs[0], "node")] if nodes == 2 else vs
    cores_too = lambda vs: vs + [swap(v, "core") for v in vs]
    one_way = lambda v: lax.ppermute(v, "stream", [(1, 0)])
    image_0 = [v[None] for v in own_piece(image_pieces)]
    self_0 = [v[None] for v in own_piece(jnp.concatenate([self_pieces, small_pieces], axis=3))]
    ffn_share = 4 if nodes == 2 else 2
    ffn_rows = jnp.concatenate([ffn_up[0], ffn_down[0]], axis=0).reshape(ffn_share, 1, 2 * width // ffn_share, -1)
    ffn_own = pick(ffn_rows, node * 2 + core if nodes == 2 else core, 0)
    ffn_0 = [ffn_own]

    image_1 = z(image_0, 2)
    image_2 = join(tie(image_0, x, h_oth), image_1)
    image_3 = z(image_2, 1)
    self_1 = z(tie(self_0, *image_1), 2)
    image_4 = join(image_2, image_3)
    image_near = nodes_too(image_4)
    image_side = [one_way(image_near[0])]
    self_2 = join(tie(self_0, *image_4), self_1)
    self_3 = z(self_2, 1)
    ffn_1 = z(tie(ffn_0, *self_1, *image_4), 2)
    image_side.append(one_way(tie(image_near[1], image_side[0], *self_3)))
    self_4 = join(self_2, self_3)
    self_near = nodes_too(tie(self_4, image_near[1], image_side[0]))
    image_full = cores_too(image_near + image_side)
    self_side = [swap(tie(self_near[0], image_side[1]), "stream")]

    act_low, act = shape((rows, width), BF), shape((rows, width), F32)
    image_kv, image_kv_last = shape((items * patches, width), BF), shape((items, width), BF)
    dma = pltpu.SemaphoreType.DMA
    self_scratch = pltpu.VMEM((4, count, 2, local // 2, width), BF)
    small_scratch = pltpu.VMEM((2, count, 4, local // 4, width), BF)
    image_scratch = pltpu.VMEM((2, count, 4, local // 4, image_width), BF)
    image_vmem = pltpu.VMEM((items * patches, width), BF)
    row = lambda v: v.reshape(1, width)

    image_keys, image_values, keys_last, values_last = call(
        image_forward,
        [image_kv] * 2 + [image_kv_last] * 2,
        [SMEM] + [ANY] * 8 + [pl.BlockSpec((patches, image_width), lambda i: (i, 0)), pl.BlockSpec((items, image_width), lambda i: (0, 0))],
        [image_scratch, dma((8, count))],
        3,
        after=(),
        grid=(items,),
        out_specs=[pl.BlockSpec((patches, width), lambda i: (i, 0))] * 2 + [pl.BlockSpec((items, width), lambda i: (0, 0))] * 2,
        name="image_forward",
    )(info, *image_full, x, x_last)

    self_side.append(swap(tie(self_near[1], image_keys, self_side[0], *ffn_1), "stream"))
    ffn_2 = join(tie(ffn_0, image_keys), ffn_1)
    ffn_3 = z(ffn_2, 1)
    ffn_near, ffn_late = nodes_too(ffn_2), nodes_too(ffn_3)
    self_full = cores_too(self_near + self_side)

    (
        q_own, k_own, v_own, q_oth, k_oth, v_oth, mix, first_sum, first, cross_queries, cross_mix, second_sum, second,
    ) = call(
        functools.partial(forward, items=items, tokens=tokens, patches=patches),
        [act_low] * 7 + [act] * 2 + [act_low] * 2 + [act] * 2,
        [SMEM, SMEM] + [ANY] * 8 + [VMEM] * 2 + [ANY] * 2 + [VMEM] * 6,
        [self_scratch, small_scratch, image_vmem, image_vmem, dma((8, count)), dma((8, count)), dma((2,))],
        5,
        after=tuple(ffn_3),
        name="forward",
    )(
        info, spans, *self_full, h_own, h_oth, image_keys, image_values, keys_last, values_last,
        row(ln1_gain), row(ln1_bias), row(ln2_gain), row(ln2_bias),
    )

    ffn_late = ffn_late[:-1] + [tie(ffn_late[-1], second)]
    ffn_full = cores_too(ffn_near) + cores_too(ffn_late)
    ffn_pieces = len(ffn_near) * 2
    half_grads = [shape((nodes, count, width // devices, width), BF)] * 2
    output, grad_second, vectors3, keep_down, send_down, keep_up, send_up = call(
        functools.partial(ffn_both, pieces=ffn_pieces),
        [act_low, act, shape((8, width), F32)] + half_grads * 2,
        [SMEM] + [ANY] * (2 * ffn_pieces) + [VMEM] * 4,
        [
            pltpu.VMEM((count, ffn_share, 2 * width // ffn_share, width), BF),
            pltpu.VMEM((count, rows, width), F32),
            pltpu.VMEM((count, rows, width), BF),
            pltpu.VMEM((2 * count, devices, width // devices, width), BF),
            dma((count, ffn_pieces)),
            dma((2 * count, 2 * nodes)),
        ],
        5,
        out_specs=[VMEM] * 3 + [ANY] * 4,
        name="ffn_both",
    )(info, *ffn_full, second, cot, ln3_gain, ln3_bias)
    down_core = keep_down, swap(send_down, "core")
    up_core = keep_up, swap(send_up, "core")
    output_1 = swap(output[None], "tensor", 2)
    down_nodes = over_nodes(down_core)
    blocks = devices * streams
    per, image_per, wide_per = width // blocks, image_width // blocks, width // devices
    tail = 16
    halves_of = lambda r, first=streams, then=nodes: [shape((first, then, r, width), BF)] * 2

    grad_keys, grad_values, grad_keys_last, grad_values_last, grad_first_sum, low_own, vectors12, keep_square, send_square = call(
        functools.partial(cross_backward, items=items, tokens=tokens, patches=patches),
        [
            image_kv, image_kv, shape((items, width), F32), shape((items, width), F32), act, act_low, shape((8, width), F32),
            *halves_of(3 * per),
        ],
        [SMEM] + [ANY] * 8 + [VMEM] * 13,
        [
            small_scratch, pltpu.VMEM((rows, width), BF), pltpu.VMEM((rows, width), BF),
            pltpu.VMEM((blocks, 3 * per, width), BF), dma((8, count)), dma((2, nodes * streams)),
        ],
        5,
        after=(down_nodes[0],),
        out_specs=[VMEM] * 7 + [ANY] * 2,
        name="cross_backward",
    )(
        info, *self_full, grad_second, second_sum, first, first_sum, mix, cross_queries, cross_mix, image_keys, image_values,
        keys_last, values_last, row(ln2_gain), row(ln1_gain),
    )
    ended = output_1, down_nodes[1], up_core[1]
    low_oth = swap(tie(low_own, *ended), "stream")
    square_core = keep_square, swap(tie(send_square, *ended), "core")
    output_2 = tensor_order(tie(output[None], low_own), output_1, 2)
    output_3 = swap(output_2, "tensor", 1)
    up_nodes = over_nodes(tie(up_core, low_own))
    down_half = tensor_step(tie(down_nodes, low_own), 1)
    square_stream = halve(tie(square_core, low_oth), "stream", 0)
    grad_input, keep_self, send_self = call(
        functools.partial(self_backward, items=items, tokens=tokens),
        [act_low] + halves_of(3 * per + tail),
        [SMEM, SMEM] + [ANY] * 8 + [VMEM] * 12,
        [pltpu.VMEM((blocks, 3 * per + tail, width), BF), self_scratch]
        + [pltpu.VMEM((rows, width), BF)] * 5
        + [dma((8, count)), dma((2, nodes * streams))],
        3,
        out_specs=[VMEM] + [ANY] * 2,
        after=(up_nodes[0], down_half[0], square_stream[0], output_2),
        name="self_backward",
    )(info, spans, *self_full, h_own, low_own, low_oth, q_own, k_own, v_own, q_oth, k_oth, v_oth, grad_first_sum, vectors12, vectors3)

    ended = up_nodes[1], down_half[1], square_stream[1], output_3
    self_core = keep_self, swap(tie(send_self, *ended), "core")
    up_half = tensor_step(tie(up_nodes, grad_input), 1)
    grad_1 = swap(grad_input[None], "tensor", 2)
    square_nodes = over_nodes(tie(square_stream, grad_input))
    self_stream = halve(self_core, "stream", 0)
    keep_keys, send_keys, keep_values, send_values = call(
        image_backward,
        halves_of(image_per) + halves_of(image_per, nodes, streams),
        [SMEM] + [VMEM] * 6,
        [pltpu.VMEM((blocks, image_per, width), BF)] * 2 + [dma((2, 2, nodes * streams))],
        5,
        after=(self_stream[0], square_nodes[0], up_half[0]),
        out_specs=[ANY] * 4,
        name="image_backward",
    )(info, x, x_last, grad_keys, grad_keys_last, grad_values, grad_values_last)

    ended = up_half[1], grad_1, square_nodes[1], self_stream[1]
    keys_stream = halve((keep_keys, swap(tie(send_keys, *ended), "core")), "stream", 0)
    values_nodes = over_nodes((keep_values, swap(tie(send_values, *ended), "core")))
    step = values_nodes[0]
    grad_2 = tensor_order(tie(grad_input[None], step), grad_1, 2)
    grad_3 = swap(grad_2, "tensor", 1)
    down_quarter = tensor_step(tie(down_half, step), 2)
    self_nodes = over_nodes(tie(self_stream, step, keys_stream[0]))
    square_half = split_rows(tie(square_nodes, step))
    keys_nodes = over_nodes(keys_stream)
    values_stream = halve(values_nodes, "stream", 0)
    step = values_stream[0]
    image_half = split_rows(keys_nodes, values_stream)
    self_half = split_rows(tie(self_nodes, step))
    up_quarter = tensor_step(tie(up_half, step), 2)
    step = image_half[0]
    square_quarter = tensor_step(tie(square_half, step), 2)
    output_4 = tensor_order(tie(output_2, step), output_3, 1)
    down_sum = finish(tie(down_quarter, step))
    self_quarter = tensor_step(tie(self_half, step), 2)
    image_quarter = tensor_step(image_half, 2)
    grad_input = tensor_order(tie(grad_2, step), grad_3, 1)
    up_sum, self_q, self_k, self_v, vectors, square_q, square_o, self_o, image_k, image_v = finish_rows(
        up_quarter,
        (self_quarter, (per, per, per, tail)),
        (square_quarter, (per, per, per)),
        (image_quarter, (image_per, image_per)),
    )

    vector = lambda r, n: vectors[r, :n]
    return (
        output_4.reshape(1, rows_all, width),
        grad_input.reshape(1, rows_all, width),
        self_q,
        self_k,
        self_v,
        self_o,
        vector(0, per),
        vector(1, per),
        square_q,
        image_k,
        image_v,
        square_o,
        vector(2, per),
        vector(3, per),
        up_sum[None],
        down_sum[None],
        vector(8, wide_per)[None],
        vector(9, wide_per)[None],
    )


def solution(mesh):
    sizes = mesh.devices.shape
    fine = Mesh(mesh.devices.reshape(sizes[0] // 2, 2, *sizes[1:]), ("node", "core", "stream", "tensor"))
    weight = P(None, "tensor")
    in_specs = (
        P("stream", DP, None), P(DP), P(DP, None, None), weight, weight, weight, weight, P(), P(),
        weight, weight, weight, weight, P(), P(), P("stream", None, "tensor"), P("stream", None, "tensor"),
        P("stream", None), P("stream", None), P("stream", DP, None),
    )
    over = ("node", "core", "stream")
    square, flat = P(over, "tensor"), P(over)
    out_specs = (
        P("stream", DP, None), P("stream", DP, None), square, square, square, square, flat, flat,
        square, square, square, square, flat, flat, P("stream", DP, "tensor"), P("stream", DP, "tensor"),
        P("stream", DP), P("stream", DP),
    )
    return jax.shard_map(shards, mesh=fine, in_specs=in_specs, out_specs=out_specs, check_vma=False)
```

```python
import functools

import jax
import jax.numpy as jnp
from jax import lax
from jax.experimental import pallas as pl
from jax.experimental.pallas import tpu as pltpu
from jax.sharding import Mesh, PartitionSpec as P

HD = 64
QUAD = 256
EPSILON = 1e-06
BF = jnp.bfloat16
F32 = jnp.float32
DP = ("node", "core")
SWAP = [(0, 1), (1, 0)]
SCALE = 0.125
NEG = -1e30


def nn(a, b):
    return lax.dot_general(a, b, (((1,), (0,)), ((), ())), preferred_element_type=F32)


def nt(a, b):
    return lax.dot_general(a, b, (((1,), (1,)), ((), ())), preferred_element_type=F32)


def tn(a, b):
    return lax.dot_general(a, b, (((0,), (0,)), ((), ())), preferred_element_type=F32)


def norm_stats(v):
    center = v - jnp.mean(v, axis=-1, keepdims=True)
    inverse = lax.rsqrt(jnp.mean(center * center, axis=-1, keepdims=True) + EPSILON)
    return center * inverse, inverse


def norm_back(e, normed, inverse, gain):
    scaled = e * gain
    out = inverse * (
        scaled
        - jnp.mean(scaled, axis=-1, keepdims=True)
        - normed * jnp.mean(scaled * normed, axis=-1, keepdims=True)
    )
    return out, jnp.sum(e * normed, axis=0, keepdims=True), jnp.sum(e, axis=0, keepdims=True)


def head_masks(rows):
    lane = lax.broadcasted_iota(jnp.int32, (rows, QUAD), 1) // HD
    return [jnp.where(lane == j, 1.0, 0.0).astype(BF) for j in range(QUAD // HD)]


def spread_heads(x, masks):
    return jnp.concatenate([x * mask for mask in masks], axis=0)


def collect_heads(x):
    rows = x.shape[0] * HD // QUAD
    lane = lax.broadcasted_iota(jnp.int32, (rows, QUAD), 1) // HD
    out = x[:rows]
    for j in range(1, QUAD // HD):
        out = jnp.where(lane == j, x[j * rows : (j + 1) * rows], out)
    return out


def softmax_keys(parts):
    peak = functools.reduce(jnp.maximum, [jnp.max(p, axis=0, keepdims=True) for p in parts])
    weights = [jnp.exp(p - peak) for p in parts]
    total = sum(jnp.sum(w, axis=0, keepdims=True) for w in weights)
    inverse = 1.0 / total
    return [w * inverse for w in weights]


def score_back(probs, grads):
    total = sum(jnp.sum(p * g, axis=0, keepdims=True) for p, g in zip(probs, grads))
    return [(p * (g - total)).astype(BF) for p, g in zip(probs, grads)]


def stack_rows(ref):
    value = ref[...]
    return value.reshape(-1, value.shape[-1])


def doubling(count):
    order, bit = [0], count // 2
    while bit:
        order = order + [mask | bit for mask in order]
        bit //= 2
    return order


def fetch(info, pieces, full, sems, where, take=None):
    node, core, stream, me = info[0], info[1], info[2], info[3]
    count = pieces[0].shape[0]
    copies = []
    for b, piece in enumerate(pieces):
        n = 1 - node if b & 1 else node
        s = 1 - stream if b & 2 else stream
        c = 1 - core if b & 4 else core
        for k, mask in enumerate(doubling(count)):
            src = jnp.bitwise_xor(me, mask)
            block = piece.at[k] if take is None else piece.at[k, take]
            copies.append(pltpu.make_async_copy(block, where(full, n, c, s, src), sems.at[b, k]))
    for copy in copies:
        copy.start(priority=1)
    return copies


def place_self(full, n, c, s, t):
    return full.at[n * 2 + c, t, s]


def place_cross(full, n, c, s, t):
    return full.at[n, t, c * 2 + s]


def forward(info, spans, *refs, items, tokens, patches):
    pieces = refs[:8]
    (
        h_own, h_oth, keys_hbm, values_hbm, keys_last, values_last, gain1, bias1, gain2, bias2,
        q_own, k_own, v_own, q_oth, k_oth, v_oth, mix, first_sum, first, cross_q, cross_mix, second_sum, second,
        full, small, keys, values, sems, small_sems, image_sems,
    ) = refs[8:]
    stream = info[2]
    copies = fetch(info, pieces, full, sems, place_self, pl.ds(0, full.shape[3]))
    later = fetch(info, pieces, small, small_sems, place_cross, pl.ds(full.shape[3], small.shape[3]))
    for at, (source, target) in enumerate(((keys_hbm, keys), (values_hbm, values))):
        later.append(pltpu.make_async_copy(source, target, image_sems.at[at]))
        later[-1].start(priority=1)
    for copy in copies:
        copy.wait()
    ho, hx = h_own[...], h_oth[...]
    for at, (own, oth) in enumerate(((q_own, q_oth), (k_own, k_oth), (v_own, v_oth))):
        weight = stack_rows(full.at[at])
        own[...] = nt(ho, weight).astype(BF)
        oth[...] = nt(hx, weight).astype(BF)
    width = ho.shape[1]

    masks = head_masks(tokens)

    def item(i, carry):
        rows = pl.ds(pl.multiple_of(i * tokens, tokens), tokens)
        valid = valid_keys(spans[i], stream, tokens, 4 * tokens)
        for u in range(width // QUAD):
            lanes = slice(u * QUAD, (u + 1) * QUAD)
            near = jnp.concatenate([k_own[rows, lanes], k_oth[rows, lanes]], axis=0)
            mixed = jnp.concatenate([v_own[rows, lanes], v_oth[rows, lanes]], axis=0)
            scores = nt(near, spread_heads(q_own[rows, lanes] * BF(SCALE), masks))
            (probs,) = softmax_keys([jnp.where(valid, scores, NEG)])
            mix[rows, lanes] = collect_heads(tn(probs.astype(BF), mixed)).astype(BF)
        return carry

    lax.fori_loop(0, items, item, 0, unroll=2)
    total = ho.astype(F32) + nn(mix[...], stack_rows(full.at[3]))
    first_sum[...] = total
    normed, _ = norm_stats(total)
    base = normed * gain1[...] + bias1[...]
    first[...] = base
    for copy in later:
        copy.wait()

    @pl.when(stream != 0)
    def _():
        second[...] = base
        second_sum[...] = base

    @pl.when(stream == 0)
    def _():
        cross_q[...] = nt(base.astype(BF), stack_rows(small.at[0])).astype(BF)

        def cross_item(i, carry):
            rows = pl.ds(pl.multiple_of(i * tokens, tokens), tokens)
            patch_rows = pl.ds(pl.multiple_of(i * patches, patches), patches)
            for u in range(width // QUAD):
                lanes = slice(u * QUAD, (u + 1) * QUAD)
                queries = spread_heads(cross_q[rows, lanes] * BF(SCALE), masks)
                scores = nt(keys[patch_rows, lanes], queries)
                tail = nt(keys_last[:, lanes], queries)
                tail = jnp.where(last_row(i, tail.shape), tail, NEG)
                probs, probs_tail = softmax_keys([scores, tail])
                out = tn(probs.astype(BF), values[patch_rows, lanes]) + tn(probs_tail.astype(BF), values_last[:, lanes])
                cross_mix[rows, lanes] = collect_heads(out).astype(BF)
            return carry

        lax.fori_loop(0, items, cross_item, 0, unroll=2)
        total = base + nn(cross_mix[...], stack_rows(small.at[1]))
        second_sum[...] = total
        normed, _ = norm_stats(total)
        second[...] = normed * gain2[...] + bias2[...]


def valid_keys(span, stream, tokens, columns):
    row = lax.broadcasted_iota(jnp.int32, (2 * tokens, columns), 0)
    own_limit = jnp.where(stream == 0, tokens, span)
    oth_limit = jnp.where(stream == 0, span, tokens)
    return ((row < tokens) & (row < own_limit)) | ((row >= tokens) & (row - tokens < oth_limit))


def image_forward(info, *refs):
    pieces = refs[:8]
    x, x_last, keys, values, keys_last, values_last, full, sems = refs[8:]

    @pl.when(info[2] == 0)
    def _():
        @pl.when(pl.program_id(0) == 0)
        def _():
            copies = fetch(info, pieces, full, sems, place_cross)
            for copy in copies:
                copy.wait()
            keys_last[...] = nt(x_last[...], stack_rows(full.at[0])).astype(BF)
            values_last[...] = nt(x_last[...], stack_rows(full.at[1])).astype(BF)

        keys[...] = nt(x[...], stack_rows(full.at[0])).astype(BF)
        values[...] = nt(x[...], stack_rows(full.at[1])).astype(BF)


def last_row(i, shape):
    return lax.broadcasted_iota(jnp.int32, shape, 0) == i


def ffn_both(info, *refs, pieces):
    weights = refs[:pieces], refs[pieces : 2 * pieces]
    (
        second, cot, gain, bias, out, grad_second, vectors, keep_down, send_down, keep_up, send_up,
        full, ups, acts, stage, sems, out_sems,
    ) = refs[2 * pieces :]
    node, core, me = info[0], info[1], info[3]
    blocks, width = full.shape[0], second.shape[1]
    nodes = keep_up.shape[0]
    copies = []
    for k, mask in enumerate(doubling(blocks)):
        src = jnp.bitwise_xor(me, mask)
        group = []
        for b in range(pieces):
            if pieces == 4:
                share = (1 - node if b & 1 else node) * 2 + (1 - core if b & 2 else core)
            else:
                share = 1 - core if b & 1 else core
            group.append(pltpu.make_async_copy(weights[k // 2][b].at[k % 2], full.at[src, share], sems.at[k, b]))
        for copy in group:
            copy.start()
        copies.append(group)

    written = []

    def emit(slot, value, keep, send, t):
        stage[slot] = value.astype(BF).reshape(stage.shape[1:])
        for n in range(nodes):
            for half, target in enumerate((keep, send)):
                part = n * 2 + (1 - core if half else core)
                copy = pltpu.make_async_copy(stage.at[slot, part], target.at[n, t], out_sems.at[slot, n * 2 + half])
                copy.start()
                written.append(copy)

    x = second[...]
    low = x.astype(BF)
    total = x
    for k, mask in enumerate(doubling(blocks)):
        for copy in copies[k]:
            copy.wait()
        both = stack_rows(full.at[jnp.bitwise_xor(me, mask)])
        up = nn(low, both[:width])
        ups[k] = up
        act = (up * (0.5 * (1.0 + lax.erf(up * 0.7071067811865476)))).astype(BF)
        acts[k] = act
        total = total + nt(act, both[width:])
    normed, inverse = norm_stats(total)
    out[...] = (normed * gain[...] + bias[...]).astype(BF)
    grad_third, grad_gain, grad_bias = norm_back(cot[...].astype(F32), normed, inverse, gain[...])
    vectors[...] = jnp.zeros_like(vectors)
    vectors[0:1] = grad_gain
    vectors[1:2] = grad_bias
    third_low = grad_third.astype(BF)
    for k, mask in enumerate(doubling(blocks)):
        emit(k, tn(third_low, acts[k]), keep_down, send_down, jnp.bitwise_xor(me, mask))
    back = grad_third
    for k, mask in enumerate(doubling(blocks)):
        both = stack_rows(full.at[jnp.bitwise_xor(me, mask)])
        up = ups[k]
        slope = 0.5 * (1.0 + lax.erf(up * 0.7071067811865476)) + up * (
            jnp.exp(-0.5 * up * up) * 0.3989422804014327
        )
        grad_up = (slope * nn(third_low, both[width:])).astype(BF)
        emit(blocks + k, tn(low, grad_up), keep_up, send_up, jnp.bitwise_xor(me, mask))
        back = back + nt(grad_up, both[:width])
    grad_second[...] = back
    for copy in written:
        copy.wait()


def cross_backward(info, *refs, items, tokens, patches):
    pieces = refs[:8]
    (
        grad_second, second_sum, first, first_sum, mix, cross_q, cross_mix, keys, values, keys_last, values_last, gain2, gain1,
        grad_keys, grad_values, grad_keys_last, grad_values_last, grad_first_sum, first_grad_low, vectors, keep, send,
        full, grad_mix, grad_q, stage, sems, out_sems,
    ) = refs[8:]
    is_query = info[2] == 0
    vectors[...] = jnp.zeros_like(vectors)
    blocks = stage.shape[0]
    per = stage.shape[1] // 3

    def write(at, value):
        value = value.astype(BF)
        for b in range(blocks):
            stage[b, at * per : (at + 1) * per, :] = value[b * per : (b + 1) * per]

    def finish(grad_first):
        normed, inverse = norm_stats(first_sum[...])
        out, grad_gain, grad_bias = norm_back(grad_first, normed, inverse, gain1[...])
        vectors[0:1] = grad_gain
        vectors[1:2] = grad_bias
        grad_first_sum[...] = out
        first_grad_low[...] = out.astype(BF)
        write(2, tn(out.astype(BF), mix[...]))

    @pl.when(jnp.logical_not(is_query))
    def _():
        stage[:, : 2 * per, :] = jnp.zeros_like(stage[:, : 2 * per, :])
        finish(grad_second[...])

    @pl.when(is_query)
    def _():
        copies = fetch(info, pieces, full, sems, place_cross, pl.ds(2 * full.shape[3], full.shape[3]))
        normed, inverse = norm_stats(second_sum[...])
        grad_cross, grad_gain, grad_bias = norm_back(grad_second[...], normed, inverse, gain2[...])
        vectors[2:3] = grad_gain
        vectors[3:4] = grad_bias
        low = grad_cross.astype(BF)
        width = low.shape[1]
        write(1, tn(low, cross_mix[...]))
        for copy in copies:
            copy.wait()
        grad_mix[...] = nt(low, stack_rows(full.at[1])).astype(BF)
        grad_keys_last[...] = jnp.zeros_like(grad_keys_last)
        grad_values_last[...] = jnp.zeros_like(grad_values_last)
        masks = head_masks(tokens)

        def item(i, carry):
            rows = pl.ds(pl.multiple_of(i * tokens, tokens), tokens)
            patch_rows = pl.ds(pl.multiple_of(i * patches, patches), patches)
            for u in range(width // QUAD):
                lanes = slice(u * QUAD, (u + 1) * QUAD)
                key, value = keys[patch_rows, lanes], values[patch_rows, lanes]
                key_last, value_last = keys_last[:, lanes], values_last[:, lanes]
                queries = spread_heads(cross_q[rows, lanes] * BF(SCALE), masks)
                pulls = spread_heads(grad_mix[rows, lanes], masks)
                scores = nt(key, queries)
                tail = nt(key_last, queries)
                is_last = last_row(i, tail.shape)
                probs = softmax_keys([scores, jnp.where(is_last, tail, NEG)])
                back, back_tail = score_back(probs, [nt(value, pulls), nt(value_last, pulls)])
                grad_keys[patch_rows, lanes] = nn(back, queries).astype(BF)
                grad_values[patch_rows, lanes] = nn(probs[0].astype(BF), pulls).astype(BF)
                grad_keys_last[:, lanes] += nn(back_tail, queries)
                grad_values_last[:, lanes] += nn(probs[1].astype(BF), pulls)
                grad_q[rows, lanes] = (collect_heads(tn(back, key) + tn(back_tail, key_last)) * SCALE).astype(BF)
            return carry

        lax.fori_loop(0, items, item, 0, unroll=2)
        grad_cross_q = grad_q[...]
        write(0, tn(first[...].astype(BF), grad_cross_q))
        finish(grad_cross + nn(grad_cross_q, stack_rows(full.at[0])))

    for copy in send_blocks(stage, keep, send, info[1], out_sems, True):
        copy.wait()


def send_blocks(stage, keep, send, core, sems, swapped):
    nodes, streams = keep.shape[:2][:: -1 if swapped else 1]
    copies = []
    for n in range(nodes):
        for s in range(streams):
            for half, target in enumerate((keep, send)):
                part = (n * 2 + (1 - core if half else core)) * streams + s
                copies.append(pltpu.make_async_copy(
                    stage.at[part], target.at[(s, n) if swapped else (n, s)], sems.at[half, n * streams + s]
                ))
    for copy in copies:
        copy.start()
    return copies


def image_backward(
    info, x, x_last, grad_keys, keys_last, grad_values, values_last,
    keep_keys, send_keys, keep_values, send_values, stage_keys, stage_values, sems,
):
    blocks, image, width = stage_keys.shape
    copies = []
    for m, (grad, last, stage, keep, send) in enumerate((
        (grad_keys, keys_last, stage_keys, keep_keys, send_keys),
        (grad_values, values_last, stage_values, keep_values, send_values),
    )):
        @pl.when(info[2] == 0)
        def _():
            for u in range(width // QUAD):
                lanes = slice(u * QUAD, (u + 1) * QUAD)
                value = (tn(x[...], grad[:, lanes]) + tn(x_last[...], last[:, lanes].astype(BF))).astype(BF)
                for b in range(blocks):
                    stage[b, :, lanes] = value[b * image : (b + 1) * image]

        @pl.when(info[2] != 0)
        def _():
            stage[...] = jnp.zeros_like(stage)

        copies += send_blocks(stage, keep, send, info[1], sems.at[m], m == 0)
    for copy in copies:
        copy.wait()


def self_backward(info, spans, *refs, items, tokens):
    pieces = refs[:8]
    (
        h_own, low_own, low_oth, q_own, k_own, v_own, q_oth, k_oth, v_oth, grad_first_sum, vectors12, vectors3,
        grad_input, keep, send, grads, full, pull_own, pull_oth, grad_q, grad_k, grad_v, sems, out_sems,
    ) = refs[8:]
    stream = info[2]
    copies = fetch(info, pieces, full, sems, place_self, pl.ds(0, full.shape[3]))
    for copy in copies:
        copy.wait()
    out_weight = stack_rows(full.at[3])
    pull_own[...] = nt(low_own[...], out_weight).astype(BF)
    pull_oth[...] = nt(low_oth[...], out_weight).astype(BF)
    width = h_own.shape[1]
    masks = head_masks(tokens)

    def item(i, carry):
        rows = pl.ds(pl.multiple_of(i * tokens, tokens), tokens)
        valid = valid_keys(spans[i], stream, tokens, 8 * tokens)
        for u in range(width // QUAD):
            lanes = slice(u * QUAD, (u + 1) * QUAD)
            keys = jnp.concatenate([k_own[rows, lanes], k_oth[rows, lanes]], axis=0)
            values = jnp.concatenate([v_own[rows, lanes], v_oth[rows, lanes]], axis=0)
            both = [spread_heads(q[rows, lanes] * BF(SCALE), masks) for q in (q_own, q_oth)]
            queries = jnp.concatenate(both, axis=0)
            pulls = jnp.concatenate([spread_heads(pull[rows, lanes], masks) for pull in (pull_own, pull_oth)], axis=0)
            scores = nt(keys, queries)
            probs = softmax_keys([jnp.where(valid, scores, NEG)])
            (back,) = score_back(probs, [nt(values, pulls)])
            own_probs = probs[0].astype(BF)
            grad_k[rows, lanes] = nn(back[:tokens], queries).astype(BF)
            grad_v[rows, lanes] = nn(own_probs[:tokens], pulls).astype(BF)
            grad_q[rows, lanes] = (collect_heads(tn(back[:, : 4 * tokens], keys)) * SCALE).astype(BF)
        return carry

    lax.fori_loop(0, items, item, 0, unroll=2)
    hidden = h_own[...]
    total = grad_first_sum[...]
    blocks, per = grads.shape[0], width // grads.shape[0]

    def write(at, value):
        value = value.astype(BF)
        for b in range(blocks):
            grads[b, at * per : (at + 1) * per, :] = value[b * per : (b + 1) * per]

    for at, ref in enumerate((grad_q, grad_k, grad_v)):
        value = ref[...]
        write(at, tn(hidden, value))
        total = total + nn(value, stack_rows(full.at[at]))
    tail = grads.shape[1] - 3 * per
    local = width // full.shape[1]
    source = lax.broadcasted_iota(jnp.int32, (width, width), 0)
    target = lax.rem(lax.broadcasted_iota(jnp.int32, (width, width), 1), local)
    lane = lax.broadcasted_iota(jnp.int32, (8, width), 1)

    def spread(vectors, size):
        value = vectors[...].astype(BF)
        parts = [jnp.where(lane // size == p, value, jnp.zeros_like(value)) for p in range(width // size)]
        chosen = jnp.where(lax.rem(source, size) == target, 1.0, 0.0).astype(BF)
        return nn(jnp.concatenate(parts, axis=0), chosen).astype(BF)

    shared, halves = spread(vectors12, per), spread(vectors3, 2 * per)
    for b in range(blocks):
        own = halves[b // 2 * 8 : b // 2 * 8 + 8]
        own = jnp.where(stream == b % 2, own, jnp.zeros_like(own))
        grads[b, 3 * per :, :] = jnp.concatenate([shared[b * 8 : b * 8 + 8], own], axis=0)
    grad_input[...] = total.astype(BF)
    for copy in send_blocks(grads, keep, send, info[1], out_sems, True):
        copy.wait()


VMEM = pl.BlockSpec(memory_space=pltpu.VMEM)
SMEM = pl.BlockSpec(memory_space=pltpu.SMEM)
ANY = pl.BlockSpec(memory_space=pl.ANY)


def shape(dims, kind):
    return jax.ShapeDtypeStruct(tuple(dims), kind)


def call(kernel, out_shapes, specs, scratch, micros, after=(), **more):
    count = len(specs)

    def body(*refs):
        kernel(*refs[:count], *refs[count + len(after) :])

    run = pl.pallas_call(
        body,
        out_shape=out_shapes,
        in_specs=specs + [ANY] * len(after),
        out_specs=more.pop("out_specs", [VMEM] * len(out_shapes)),
        scratch_shapes=scratch,
        compiler_params=pltpu.CompilerParams(vmem_limit_bytes=62 * 1024 * 1024),
        cost_estimate=pl.CostEstimate(flops=int(micros * 1.15e9), bytes_accessed=int(micros * 3.6e6), transcendentals=0),
        **more,
    )
    return lambda *operands: run(*operands, *after)


def pick(array, index, axis):
    return lax.dynamic_index_in_dim(array, index, axis, keepdims=False)


def add(a, b):
    return (a.astype(F32) + b.astype(F32)).astype(BF)


def swap(block, axis, bit=1):
    return lax.ppermute(block, axis, [(i, i ^ bit) for i in range(lax.axis_size(axis))])


def tie(value, *others):
    return jax.tree.map(lambda v: lax.optimization_barrier((v,) + others)[0], value)


def tensor_order(gathered, other, bit):
    upper = jnp.bitwise_and(lax.axis_index("tensor"), bit) != 0
    low, high = jnp.where(upper, other, gathered), jnp.where(upper, gathered, other)
    return jnp.stack([low, high], axis=1).reshape((-1,) + gathered.shape[1:])


def own_piece(pieces):
    pieces = pick(pick(pieces, lax.axis_index("core"), 1), lax.axis_index("stream"), 1)
    if lax.axis_size("node") == 2:
        return [pick(pieces, lax.axis_index("node"), 0)]
    return [pieces[0], pieces[1]]


def halve(pair, axis_name, axis, bit=1):
    keep, arrived = pair
    me = jnp.bitwise_and(lax.axis_index(axis_name) // bit, 1)
    sent = add(pick(keep, 1 - me, axis), pick(arrived, 1 - me, axis))
    kept = add(pick(keep, me, axis), pick(arrived, me, axis))
    return kept, swap(sent, axis_name, bit)


def over_nodes(pair):
    if lax.axis_size("node") == 2:
        return halve(pair, "node", 0)
    total = lax.psum_scatter(add(*pair), "node", scatter_dimension=0, tiled=False)
    return total, jnp.zeros_like(total)


def tensor_step(pair, bit):
    pair = [v.reshape((v.shape[0] // 2, 2) + v.shape[1:]) for v in pair]
    return halve(pair, "tensor", 1, bit)


def finish(pair):
    return (pair[0].astype(F32) + pair[1].astype(F32))[0]


def split_rows(*pairs):
    count, me = lax.axis_size("tensor"), lax.axis_index("tensor")
    rows, columns = sum(pair[0].shape[0] for pair in pairs), pairs[0][0].shape[1]
    half, local = rows // 2, columns // count

    def kernel(bit, *refs):
        *inputs, stays, goes = refs
        totals = [
            (kept[...].astype(F32) + arrived[...].astype(F32)).astype(BF) for kept, arrived in zip(inputs[::2], inputs[1::2])
        ]
        total = jnp.concatenate(totals, axis=0)
        upper = bit[0] == 1
        for p in range(count // 2):
            two = [
                jnp.concatenate([total[:half, t * local : (t + 1) * local], total[half:, t * local : (t + 1) * local]], axis=1)
                for t in (2 * p, 2 * p + 1)
            ]
            stays[p] = jnp.where(upper, two[1], two[0])
            goes[p] = jnp.where(upper, two[0], two[1])

    outs = [shape((count // 2, half, 2 * local), BF)] * 2
    bit = jnp.bitwise_and(me, 1).reshape(1)
    operands = [v for pair in pairs for v in pair]
    stays, goes = call(kernel, outs, [SMEM] + [VMEM] * len(operands), [], 1, name="split_rows")(bit, *operands)
    return stays, swap(goes, "tensor", 1)


def finish_rows(plain, *packs):
    local = packs[0][0][0].shape[2] // 2

    def kernel(*refs):
        inputs, outs = refs[: 2 + 2 * len(packs)], refs[2 + 2 * len(packs) :]
        outs[0][...] = inputs[0][0].astype(F32) + inputs[1][0].astype(F32)
        at = 1
        for p, (_, sizes) in enumerate(packs):
            both = inputs[2 + 2 * p][0].astype(F32) + inputs[3 + 2 * p][0].astype(F32)
            total = jnp.concatenate([both[:, :local], both[:, local:]], axis=0)
            start = 0
            for size in sizes:
                outs[at][...] = total[start : start + size]
                start += size
                at += 1

    outs = [shape(plain[0].shape[1:], F32)] + [shape((size, local), F32) for _, sizes in packs for size in sizes]
    operands = [*plain, *(v for pair, _ in packs for v in pair)]
    return call(kernel, outs, [VMEM] * len(operands), [], 1, name="finish_rows")(*operands)


def shards(
    hidden_in, lengths, image_features, self_q, self_k, self_v, self_out, ln1_gain, ln1_bias,
    cross_q, cross_k, cross_v, cross_out, ln2_gain, ln2_bias, ffn_up, ffn_down, ln3_gain, ln3_bias, cotangent,
):
    nodes, streams, count = lax.axis_size("node"), lax.axis_size("stream"), lax.axis_size("tensor")
    node, core = lax.axis_index("node"), lax.axis_index("core")
    stream, me = lax.axis_index("stream"), lax.axis_index("tensor")
    devices = nodes * 2
    rows_all, width = hidden_in.shape[1:]
    local = self_q.shape[1]
    image_tokens, image_width = image_features.shape[1:]
    patches = image_tokens - 1
    items = lengths.shape[0] // count
    rows = rows_all // count
    tokens = rows // items
    info = jnp.stack([node if nodes == 2 else jnp.int32(0), core, stream, me]).astype(jnp.int32)

    self_pieces = jnp.stack([self_q.T, self_k.T, self_v.T, self_out.T]).reshape(2, 2, 2, local // 2, width)
    small_pieces = jnp.stack([cross_q.T, cross_out.T]).reshape(2, 2, 2, local // 4, width)
    image_pieces = jnp.stack([cross_k.T, cross_v.T]).reshape(2, 2, 2, local // 4, image_width)
    h_own = lax.dynamic_slice_in_dim(hidden_in[0], me * rows, rows, 0)
    h_oth = lax.ppermute(h_own, "stream", SWAP)
    spans = lax.dynamic_slice_in_dim(lengths, me * items, items, 0)
    cot = lax.dynamic_slice_in_dim(cotangent[0], me * rows, rows, 0)
    image = lax.dynamic_slice_in_dim(image_features, me * items, items, 0)
    x = image[:, :patches].reshape(items * patches, image_width)
    x_last = image[:, patches]

    z = lambda vs, bit: [swap(v, "tensor", bit) for v in vs]
    join = lambda a, b: [jnp.concatenate([v, w]) for v, w in zip(a, b)]
    nodes_too = lambda vs: vs + [swap(vs[0], "node")] if nodes == 2 else vs
    cores_too = lambda vs: vs + [swap(v, "core") for v in vs]
    one_way = lambda v: lax.ppermute(v, "stream", [(1, 0)])
    image_0 = [v[None] for v in own_piece(image_pieces)]
    self_0 = [v[None] for v in own_piece(jnp.concatenate([self_pieces, small_pieces], axis=3))]
    ffn_share = 4 if nodes == 2 else 2
    ffn_rows = jnp.concatenate([ffn_up[0], ffn_down[0]], axis=0).reshape(ffn_share, 1, 2 * width // ffn_share, -1)
    ffn_own = pick(ffn_rows, node * 2 + core if nodes == 2 else core, 0)
    ffn_0 = [ffn_own]

    image_1 = z(image_0, 2)
    image_2 = join(tie(image_0, h_oth), image_1)
    image_3 = z(image_2, 1)
    self_1 = z(tie(self_0, *image_1), 2)
    image_4 = join(image_2, image_3)
    image_near = nodes_too(image_4)
    image_side = [one_way(image_near[0])]
    self_2 = join(tie(self_0, x, *image_4), self_1)
    self_3 = z(self_2, 1)
    ffn_1 = z(tie(ffn_0, *self_1, *image_4), 2)
    image_side.append(one_way(tie(image_near[1], image_side[0])))
    self_4 = join(self_2, self_3)
    self_near = nodes_too(tie(self_4, image_near[1], image_side[0]))
    image_full = cores_too(image_near + image_side)
    self_side = [swap(tie(self_near[0], image_side[1]), "stream")]

    act_low, act = shape((rows, width), BF), shape((rows, width), F32)
    image_kv, image_kv_last = shape((items * patches, width), BF), shape((items, width), BF)
    dma = pltpu.SemaphoreType.DMA
    self_scratch = pltpu.VMEM((4, count, 2, local // 2, width), BF)
    small_scratch = pltpu.VMEM((2, count, 4, local // 4, width), BF)
    image_scratch = pltpu.VMEM((2, count, 4, local // 4, image_width), BF)
    image_vmem = pltpu.VMEM((items * patches, width), BF)
    row = lambda v: v.reshape(1, width)

    image_keys, image_values, keys_last, values_last = call(
        image_forward,
        [image_kv] * 2 + [image_kv_last] * 2,
        [SMEM] + [ANY] * 8 + [pl.BlockSpec((patches, image_width), lambda i: (i, 0)), pl.BlockSpec((items, image_width), lambda i: (0, 0))],
        [image_scratch, dma((8, count))],
        3,
        after=(),
        grid=(items,),
        out_specs=[pl.BlockSpec((patches, width), lambda i: (i, 0))] * 2 + [pl.BlockSpec((items, width), lambda i: (0, 0))] * 2,
        name="image_forward",
    )(info, *image_full, x, x_last)

    self_side.append(swap(tie(self_near[1], image_keys, self_side[0], *ffn_1), "stream"))
    ffn_2 = join(tie(ffn_0, image_keys), ffn_1)
    ffn_3 = z(ffn_2, 1)
    ffn_near, ffn_late = nodes_too(ffn_2), nodes_too(ffn_3)
    self_full = cores_too(self_near + self_side)

    (
        q_own, k_own, v_own, q_oth, k_oth, v_oth, mix, first_sum, first, cross_queries, cross_mix, second_sum, second,
    ) = call(
        functools.partial(forward, items=items, tokens=tokens, patches=patches),
        [act_low] * 7 + [act] * 2 + [act_low] * 2 + [act] * 2,
        [SMEM, SMEM] + [ANY] * 8 + [VMEM] * 2 + [ANY] * 2 + [VMEM] * 6,
        [self_scratch, small_scratch, image_vmem, image_vmem, dma((8, count)), dma((8, count)), dma((2,))],
        5,
        after=tuple(ffn_3),
        name="forward",
    )(
        info, spans, *self_full, h_own, h_oth, image_keys, image_values, keys_last, values_last,
        row(ln1_gain), row(ln1_bias), row(ln2_gain), row(ln2_bias),
    )

    ffn_late = ffn_late[:-1] + [tie(ffn_late[-1], second)]
    ffn_full = cores_too(ffn_near) + cores_too(ffn_late)
    ffn_pieces = len(ffn_near) * 2
    half_grads = [shape((nodes, count, width // devices, width), BF)] * 2
    output, grad_second, vectors3, keep_down, send_down, keep_up, send_up = call(
        functools.partial(ffn_both, pieces=ffn_pieces),
        [act_low, act, shape((8, width), F32)] + half_grads * 2,
        [SMEM] + [ANY] * (2 * ffn_pieces) + [VMEM] * 4,
        [
            pltpu.VMEM((count, ffn_share, 2 * width // ffn_share, width), BF),
            pltpu.VMEM((count, rows, width), F32),
            pltpu.VMEM((count, rows, width), BF),
            pltpu.VMEM((2 * count, devices, width // devices, width), BF),
            dma((count, ffn_pieces)),
            dma((2 * count, 2 * nodes)),
        ],
        5,
        out_specs=[VMEM] * 3 + [ANY] * 4,
        name="ffn_both",
    )(info, *ffn_full, second, cot, ln3_gain, ln3_bias)
    down_core = keep_down, swap(send_down, "core")
    up_core = keep_up, swap(send_up, "core")
    output_1 = swap(output[None], "tensor", 2)
    down_nodes = over_nodes(down_core)
    blocks = devices * streams
    per, image_per, wide_per = width // blocks, image_width // blocks, width // devices
    tail = 16
    halves_of = lambda r, first=streams, then=nodes: [shape((first, then, r, width), BF)] * 2

    grad_keys, grad_values, grad_keys_last, grad_values_last, grad_first_sum, low_own, vectors12, keep_square, send_square = call(
        functools.partial(cross_backward, items=items, tokens=tokens, patches=patches),
        [
            image_kv, image_kv, shape((items, width), F32), shape((items, width), F32), act, act_low, shape((8, width), F32),
            *halves_of(3 * per),
        ],
        [SMEM] + [ANY] * 8 + [VMEM] * 13,
        [
            small_scratch, pltpu.VMEM((rows, width), BF), pltpu.VMEM((rows, width), BF),
            pltpu.VMEM((blocks, 3 * per, width), BF), dma((8, count)), dma((2, nodes * streams)),
        ],
        5,
        after=(down_nodes[0],),
        out_specs=[VMEM] * 7 + [ANY] * 2,
        name="cross_backward",
    )(
        info, *self_full, grad_second, second_sum, first, first_sum, mix, cross_queries, cross_mix, image_keys, image_values,
        keys_last, values_last, row(ln2_gain), row(ln1_gain),
    )
    ended = output_1, down_nodes[1], up_core[1]
    low_oth = swap(tie(low_own, *ended), "stream")
    square_core = keep_square, swap(tie(send_square, *ended), "core")
    output_2 = tensor_order(tie(output[None], low_own), output_1, 2)
    output_3 = swap(output_2, "tensor", 1)
    up_nodes = over_nodes(tie(up_core, low_own))
    down_half = tensor_step(tie(down_nodes, low_own), 1)
    square_stream = halve(tie(square_core, low_oth), "stream", 0)
    grad_input, keep_self, send_self = call(
        functools.partial(self_backward, items=items, tokens=tokens),
        [act_low] + halves_of(3 * per + tail),
        [SMEM, SMEM] + [ANY] * 8 + [VMEM] * 12,
        [pltpu.VMEM((blocks, 3 * per + tail, width), BF), self_scratch]
        + [pltpu.VMEM((rows, width), BF)] * 5
        + [dma((8, count)), dma((2, nodes * streams))],
        3,
        out_specs=[VMEM] + [ANY] * 2,
        after=(up_nodes[0], down_half[0], square_stream[0], output_2),
        name="self_backward",
    )(info, spans, *self_full, h_own, low_own, low_oth, q_own, k_own, v_own, q_oth, k_oth, v_oth, grad_first_sum, vectors12, vectors3)

    ended = up_nodes[1], down_half[1], square_stream[1], output_3
    self_core = keep_self, swap(tie(send_self, *ended), "core")
    up_half = tensor_step(tie(up_nodes, grad_input), 1)
    grad_1 = swap(grad_input[None], "tensor", 2)
    square_nodes = over_nodes(tie(square_stream, grad_input))
    self_stream = halve(self_core, "stream", 0)
    keep_keys, send_keys, keep_values, send_values = call(
        image_backward,
        halves_of(image_per) + halves_of(image_per, nodes, streams),
        [SMEM] + [VMEM] * 6,
        [pltpu.VMEM((blocks, image_per, width), BF)] * 2 + [dma((2, 2, nodes * streams))],
        5,
        after=(self_stream[0], square_nodes[0], up_half[0]),
        out_specs=[ANY] * 4,
        name="image_backward",
    )(info, x, x_last, grad_keys, grad_keys_last, grad_values, grad_values_last)

    ended = up_half[1], grad_1, square_nodes[1], self_stream[1]
    keys_stream = halve((keep_keys, swap(tie(send_keys, *ended), "core")), "stream", 0)
    values_nodes = over_nodes((keep_values, swap(tie(send_values, *ended), "core")))
    step = values_nodes[0]
    grad_2 = tensor_order(tie(grad_input[None], step), grad_1, 2)
    grad_3 = swap(grad_2, "tensor", 1)
    down_quarter = tensor_step(tie(down_half, step), 2)
    self_nodes = over_nodes(tie(self_stream, step, keys_stream[0]))
    square_half = split_rows(tie(square_nodes, step))
    keys_nodes = over_nodes(keys_stream)
    values_stream = halve(values_nodes, "stream", 0)
    step = values_stream[0]
    image_half = split_rows(keys_nodes, values_stream)
    self_half = split_rows(tie(self_nodes, step))
    up_quarter = tensor_step(tie(up_half, step), 2)
    step = image_half[0]
    square_quarter = tensor_step(tie(square_half, step), 2)
    output_4 = tensor_order(tie(output_2, step), output_3, 1)
    down_sum = finish(tie(down_quarter, step))
    self_quarter = tensor_step(tie(self_half, step), 2)
    image_quarter = tensor_step(image_half, 2)
    grad_input = tensor_order(tie(grad_2, step), grad_3, 1)
    up_sum, self_q, self_k, self_v, vectors, square_q, square_o, self_o, image_k, image_v = finish_rows(
        up_quarter,
        (self_quarter, (per, per, per, tail)),
        (square_quarter, (per, per, per)),
        (image_quarter, (image_per, image_per)),
    )

    vector = lambda r, n: vectors[r, :n]
    return (
        output_4.reshape(1, rows_all, width),
        grad_input.reshape(1, rows_all, width),
        self_q,
        self_k,
        self_v,
        self_o,
        vector(0, per),
        vector(1, per),
        square_q,
        image_k,
        image_v,
        square_o,
        vector(2, per),
        vector(3, per),
        up_sum[None],
        down_sum[None],
        vector(8, wide_per)[None],
        vector(9, wide_per)[None],
    )


def solution(mesh):
    sizes = mesh.devices.shape
    fine = Mesh(mesh.devices.reshape(sizes[0] // 2, 2, *sizes[1:]), ("node", "core", "stream", "tensor"))
    weight = P(None, "tensor")
    in_specs = (
        P("stream", DP, None), P(DP), P(DP, None, None), weight, weight, weight, weight, P(), P(),
        weight, weight, weight, weight, P(), P(), P("stream", None, "tensor"), P("stream", None, "tensor"),
        P("stream", None), P("stream", None), P("stream", DP, None),
    )
    over = ("node", "core", "stream")
    square, flat = P(over, "tensor"), P(over)
    out_specs = (
        P("stream", DP, None), P("stream", DP, None), square, square, square, square, flat, flat,
        square, square, square, square, flat, flat, P("stream", DP, "tensor"), P("stream", DP, "tensor"),
        P("stream", DP), P("stream", DP),
    )
    return jax.shard_map(shards, mesh=fine, in_specs=in_specs, out_specs=out_specs, check_vma=False)
```

```python
import functools

import jax
import jax.numpy as jnp
from jax import lax
from jax.experimental import pallas as pl
from jax.experimental.pallas import tpu as pltpu
from jax.sharding import Mesh, PartitionSpec as P

HD = 64
QUAD = 256
EPSILON = 1e-06
BF = jnp.bfloat16
F32 = jnp.float32
DP = ("node", "core")
SWAP = [(0, 1), (1, 0)]
SCALE = 0.125
NEG = -1e30


def nn(a, b):
    return lax.dot_general(a, b, (((1,), (0,)), ((), ())), preferred_element_type=F32)


def nt(a, b):
    return lax.dot_general(a, b, (((1,), (1,)), ((), ())), preferred_element_type=F32)


def tn(a, b):
    return lax.dot_general(a, b, (((0,), (0,)), ((), ())), preferred_element_type=F32)


def norm_stats(v):
    center = v - jnp.mean(v, axis=-1, keepdims=True)
    inverse = lax.rsqrt(jnp.mean(center * center, axis=-1, keepdims=True) + EPSILON)
    return center * inverse, inverse


def norm_back(e, normed, inverse, gain):
    scaled = e * gain
    out = inverse * (
        scaled
        - jnp.mean(scaled, axis=-1, keepdims=True)
        - normed * jnp.mean(scaled * normed, axis=-1, keepdims=True)
    )
    return out, jnp.sum(e * normed, axis=0, keepdims=True), jnp.sum(e, axis=0, keepdims=True)


def head_masks(rows):
    lane = lax.broadcasted_iota(jnp.int32, (rows, QUAD), 1) // HD
    return [jnp.where(lane == j, 1.0, 0.0).astype(BF) for j in range(QUAD // HD)]


def spread_heads(x, masks):
    return jnp.concatenate([x * mask for mask in masks], axis=0)


def collect_heads(x):
    rows = x.shape[0] * HD // QUAD
    lane = lax.broadcasted_iota(jnp.int32, (rows, QUAD), 1) // HD
    out = x[:rows]
    for j in range(1, QUAD // HD):
        out = jnp.where(lane == j, x[j * rows : (j + 1) * rows], out)
    return out


def softmax_keys(parts):
    peak = functools.reduce(jnp.maximum, [jnp.max(p, axis=0, keepdims=True) for p in parts])
    weights = [jnp.exp(p - peak) for p in parts]
    total = sum(jnp.sum(w, axis=0, keepdims=True) for w in weights)
    inverse = 1.0 / total
    return [w * inverse for w in weights]


def score_back(probs, grads):
    total = sum(jnp.sum(p * g, axis=0, keepdims=True) for p, g in zip(probs, grads))
    return [(p * (g - total)).astype(BF) for p, g in zip(probs, grads)]


def stack_rows(ref):
    value = ref[...]
    return value.reshape(-1, value.shape[-1])


def doubling(count):
    order, bit = [0], count // 2
    while bit:
        order = order + [mask | bit for mask in order]
        bit //= 2
    return order


def fetch(info, pieces, full, sems, where, take=None):
    node, core, stream, me = info[0], info[1], info[2], info[3]
    count = pieces[0].shape[0]
    copies = []
    for b, piece in enumerate(pieces):
        n = 1 - node if b & 1 else node
        s = 1 - stream if b & 2 else stream
        c = 1 - core if b & 4 else core
        for k, mask in enumerate(doubling(count)):
            src = jnp.bitwise_xor(me, mask)
            block = piece.at[k] if take is None else piece.at[k, take]
            copies.append(pltpu.make_async_copy(block, where(full, n, c, s, src), sems.at[b, k]))
    for copy in copies:
        copy.start(priority=1)
    return copies


def place_self(full, n, c, s, t):
    return full.at[n * 2 + c, t, s]


def place_cross(full, n, c, s, t):
    return full.at[n, t, c * 2 + s]


def forward(info, spans, *refs, items, tokens, patches):
    pieces = refs[:8]
    (
        h_own, h_oth, keys_hbm, values_hbm, keys_last, values_last, gain1, bias1, gain2, bias2,
        q_own, k_own, v_own, q_oth, k_oth, v_oth, mix, first_sum, first, cross_q, cross_mix, second_sum, second,
        full, small, keys, values, sems, small_sems, image_sems,
    ) = refs[8:]
    stream = info[2]
    copies = fetch(info, pieces, full, sems, place_self, pl.ds(0, full.shape[3]))
    later = fetch(info, pieces, small, small_sems, place_cross, pl.ds(full.shape[3], small.shape[3]))
    for at, (source, target) in enumerate(((keys_hbm, keys), (values_hbm, values))):
        later.append(pltpu.make_async_copy(source, target, image_sems.at[at]))
        later[-1].start(priority=1)
    for copy in copies:
        copy.wait()
    ho, hx = h_own[...], h_oth[...]
    for at, (own, oth) in enumerate(((q_own, q_oth), (k_own, k_oth), (v_own, v_oth))):
        weight = stack_rows(full.at[at])
        own[...] = nt(ho, weight).astype(BF)
        oth[...] = nt(hx, weight).astype(BF)
    width = ho.shape[1]

    masks = head_masks(tokens)

    def item(i, carry):
        rows = pl.ds(pl.multiple_of(i * tokens, tokens), tokens)
        valid = valid_keys(spans[i], stream, tokens, 4 * tokens)
        for u in range(width // QUAD):
            lanes = slice(u * QUAD, (u + 1) * QUAD)
            near = jnp.concatenate([k_own[rows, lanes], k_oth[rows, lanes]], axis=0)
            mixed = jnp.concatenate([v_own[rows, lanes], v_oth[rows, lanes]], axis=0)
            scores = nt(near, spread_heads(q_own[rows, lanes] * BF(SCALE), masks))
            (probs,) = softmax_keys([jnp.where(valid, scores, NEG)])
            mix[rows, lanes] = collect_heads(tn(probs.astype(BF), mixed)).astype(BF)
        return carry

    lax.fori_loop(0, items, item, 0, unroll=4)
    total = ho.astype(F32) + nn(mix[...], stack_rows(full.at[3]))
    first_sum[...] = total
    normed, _ = norm_stats(total)
    base = normed * gain1[...] + bias1[...]
    first[...] = base
    for copy in later:
        copy.wait()

    @pl.when(stream != 0)
    def _():
        second[...] = base
        second_sum[...] = base

    @pl.when(stream == 0)
    def _():
        cross_q[...] = nt(base.astype(BF), stack_rows(small.at[0])).astype(BF)

        def cross_item(i, carry):
            rows = pl.ds(pl.multiple_of(i * tokens, tokens), tokens)
            patch_rows = pl.ds(pl.multiple_of(i * patches, patches), patches)
            for u in range(width // QUAD):
                lanes = slice(u * QUAD, (u + 1) * QUAD)
                queries = spread_heads(cross_q[rows, lanes] * BF(SCALE), masks)
                scores = nt(keys[patch_rows, lanes], queries)
                tail = nt(keys_last[:, lanes], queries)
                tail = jnp.where(last_row(i, tail.shape), tail, NEG)
                probs, probs_tail = softmax_keys([scores, tail])
                out = tn(probs.astype(BF), values[patch_rows, lanes]) + tn(probs_tail.astype(BF), values_last[:, lanes])
                cross_mix[rows, lanes] = collect_heads(out).astype(BF)
            return carry

        lax.fori_loop(0, items, cross_item, 0, unroll=4)
        total = base + nn(cross_mix[...], stack_rows(small.at[1]))
        second_sum[...] = total
        normed, _ = norm_stats(total)
        second[...] = normed * gain2[...] + bias2[...]


def valid_keys(span, stream, tokens, columns):
    row = lax.broadcasted_iota(jnp.int32, (2 * tokens, columns), 0)
    own_limit = jnp.where(stream == 0, tokens, span)
    oth_limit = jnp.where(stream == 0, span, tokens)
    return ((row < tokens) & (row < own_limit)) | ((row >= tokens) & (row - tokens < oth_limit))


def image_forward(info, *refs):
    pieces = refs[:8]
    x, x_last, keys, values, keys_last, values_last, full, sems = refs[8:]

    @pl.when(info[2] == 0)
    def _():
        @pl.when(pl.program_id(0) == 0)
        def _():
            copies = fetch(info, pieces, full, sems, place_cross)
            for copy in copies:
                copy.wait()
            keys_last[...] = nt(x_last[...], stack_rows(full.at[0])).astype(BF)
            values_last[...] = nt(x_last[...], stack_rows(full.at[1])).astype(BF)

        keys[...] = nt(x[...], stack_rows(full.at[0])).astype(BF)
        values[...] = nt(x[...], stack_rows(full.at[1])).astype(BF)


def last_row(i, shape):
    return lax.broadcasted_iota(jnp.int32, shape, 0) == i


def ffn_both(info, *refs, pieces):
    weights = refs[:pieces], refs[pieces : 2 * pieces]
    (
        second, cot, gain, bias, out, grad_second, vectors, keep_down, send_down, keep_up, send_up,
        full, ups, acts, stage, sems, out_sems,
    ) = refs[2 * pieces :]
    node, core, me = info[0], info[1], info[3]
    blocks, width = full.shape[0], second.shape[1]
    nodes = keep_up.shape[0]
    copies = []
    for k, mask in enumerate(doubling(blocks)):
        src = jnp.bitwise_xor(me, mask)
        group = []
        for b in range(pieces):
            if pieces == 4:
                share = (1 - node if b & 1 else node) * 2 + (1 - core if b & 2 else core)
            else:
                share = 1 - core if b & 1 else core
            group.append(pltpu.make_async_copy(weights[k // 2][b].at[k % 2], full.at[src, share], sems.at[k, b]))
        for copy in group:
            copy.start()
        copies.append(group)

    written = []

    def emit(slot, value, keep, send, t):
        stage[slot] = value.astype(BF).reshape(stage.shape[1:])
        for n in range(nodes):
            for half, target in enumerate((keep, send)):
                part = n * 2 + (1 - core if half else core)
                copy = pltpu.make_async_copy(stage.at[slot, part], target.at[n, t], out_sems.at[slot, n * 2 + half])
                copy.start()
                written.append(copy)

    x = second[...]
    low = x.astype(BF)
    total = x
    for k, mask in enumerate(doubling(blocks)):
        for copy in copies[k]:
            copy.wait()
        both = stack_rows(full.at[jnp.bitwise_xor(me, mask)])
        up = nn(low, both[:width])
        ups[k] = up
        act = (up * (0.5 * (1.0 + lax.erf(up * 0.7071067811865476)))).astype(BF)
        acts[k] = act
        total = total + nt(act, both[width:])
    normed, inverse = norm_stats(total)
    out[...] = (normed * gain[...] + bias[...]).astype(BF)
    grad_third, grad_gain, grad_bias = norm_back(cot[...].astype(F32), normed, inverse, gain[...])
    vectors[...] = jnp.zeros_like(vectors)
    vectors[0:1] = grad_gain
    vectors[1:2] = grad_bias
    third_low = grad_third.astype(BF)
    for k, mask in enumerate(doubling(blocks)):
        emit(k, tn(third_low, acts[k]), keep_down, send_down, jnp.bitwise_xor(me, mask))
    back = grad_third
    for k, mask in enumerate(doubling(blocks)):
        both = stack_rows(full.at[jnp.bitwise_xor(me, mask)])
        up = ups[k]
        slope = 0.5 * (1.0 + lax.erf(up * 0.7071067811865476)) + up * (
            jnp.exp(-0.5 * up * up) * 0.3989422804014327
        )
        grad_up = (slope * nn(third_low, both[width:])).astype(BF)
        emit(blocks + k, tn(low, grad_up), keep_up, send_up, jnp.bitwise_xor(me, mask))
        back = back + nt(grad_up, both[:width])
    grad_second[...] = back
    for copy in written:
        copy.wait()


def cross_backward(info, *refs, items, tokens, patches):
    pieces = refs[:8]
    (
        grad_second, second_sum, first, first_sum, mix, cross_q, cross_mix, keys, values, keys_last, values_last, gain2, gain1,
        grad_keys, grad_values, grad_keys_last, grad_values_last, grad_first_sum, first_grad_low, vectors, keep, send,
        full, grad_mix, grad_q, stage, sems, out_sems,
    ) = refs[8:]
    is_query = info[2] == 0
    vectors[...] = jnp.zeros_like(vectors)
    blocks = stage.shape[0]
    per = stage.shape[1] // 3

    def write(at, value):
        value = value.astype(BF)
        for b in range(blocks):
            stage[b, at * per : (at + 1) * per, :] = value[b * per : (b + 1) * per]

    def finish(grad_first):
        normed, inverse = norm_stats(first_sum[...])
        out, grad_gain, grad_bias = norm_back(grad_first, normed, inverse, gain1[...])
        vectors[0:1] = grad_gain
        vectors[1:2] = grad_bias
        grad_first_sum[...] = out
        first_grad_low[...] = out.astype(BF)
        write(2, tn(out.astype(BF), mix[...]))

    @pl.when(jnp.logical_not(is_query))
    def _():
        stage[:, : 2 * per, :] = jnp.zeros_like(stage[:, : 2 * per, :])
        finish(grad_second[...])

    @pl.when(is_query)
    def _():
        copies = fetch(info, pieces, full, sems, place_cross, pl.ds(2 * full.shape[3], full.shape[3]))
        normed, inverse = norm_stats(second_sum[...])
        grad_cross, grad_gain, grad_bias = norm_back(grad_second[...], normed, inverse, gain2[...])
        vectors[2:3] = grad_gain
        vectors[3:4] = grad_bias
        low = grad_cross.astype(BF)
        width = low.shape[1]
        write(1, tn(low, cross_mix[...]))
        for copy in copies:
            copy.wait()
        grad_mix[...] = nt(low, stack_rows(full.at[1])).astype(BF)
        grad_keys_last[...] = jnp.zeros_like(grad_keys_last)
        grad_values_last[...] = jnp.zeros_like(grad_values_last)
        masks = head_masks(tokens)

        def item(i, carry):
            rows = pl.ds(pl.multiple_of(i * tokens, tokens), tokens)
            patch_rows = pl.ds(pl.multiple_of(i * patches, patches), patches)
            for u in range(width // QUAD):
                lanes = slice(u * QUAD, (u + 1) * QUAD)
                key, value = keys[patch_rows, lanes], values[patch_rows, lanes]
                key_last, value_last = keys_last[:, lanes], values_last[:, lanes]
                queries = spread_heads(cross_q[rows, lanes] * BF(SCALE), masks)
                pulls = spread_heads(grad_mix[rows, lanes], masks)
                scores = nt(key, queries)
                tail = nt(key_last, queries)
                is_last = last_row(i, tail.shape)
                probs = softmax_keys([scores, jnp.where(is_last, tail, NEG)])
                back, back_tail = score_back(probs, [nt(value, pulls), nt(value_last, pulls)])
                grad_keys[patch_rows, lanes] = nn(back, queries).astype(BF)
                grad_values[patch_rows, lanes] = nn(probs[0].astype(BF), pulls).astype(BF)
                grad_keys_last[:, lanes] += nn(back_tail, queries)
                grad_values_last[:, lanes] += nn(probs[1].astype(BF), pulls)
                grad_q[rows, lanes] = (collect_heads(tn(back, key) + tn(back_tail, key_last)) * SCALE).astype(BF)
            return carry

        lax.fori_loop(0, items, item, 0, unroll=2)
        grad_cross_q = grad_q[...]
        write(0, tn(first[...].astype(BF), grad_cross_q))
        finish(grad_cross + nn(grad_cross_q, stack_rows(full.at[0])))

    for copy in send_blocks(stage, keep, send, info[1], out_sems, True):
        copy.wait()


def send_blocks(stage, keep, send, core, sems, swapped):
    nodes, streams = keep.shape[:2][:: -1 if swapped else 1]
    copies = []
    for n in range(nodes):
        for s in range(streams):
            for half, target in enumerate((keep, send)):
                part = (n * 2 + (1 - core if half else core)) * streams + s
                copies.append(pltpu.make_async_copy(
                    stage.at[part], target.at[(s, n) if swapped else (n, s)], sems.at[half, n * streams + s]
                ))
    for copy in copies:
        copy.start()
    return copies


def image_backward(
    info, x, x_last, grad_keys, keys_last, grad_values, values_last,
    keep_keys, send_keys, keep_values, send_values, stage_keys, stage_values, sems,
):
    blocks, image, width = stage_keys.shape
    copies = []
    for m, (grad, last, stage, keep, send) in enumerate((
        (grad_keys, keys_last, stage_keys, keep_keys, send_keys),
        (grad_values, values_last, stage_values, keep_values, send_values),
    )):
        @pl.when(info[2] == 0)
        def _():
            for u in range(width // QUAD):
                lanes = slice(u * QUAD, (u + 1) * QUAD)
                value = (tn(x[...], grad[:, lanes]) + tn(x_last[...], last[:, lanes].astype(BF))).astype(BF)
                for b in range(blocks):
                    stage[b, :, lanes] = value[b * image : (b + 1) * image]

        @pl.when(info[2] != 0)
        def _():
            stage[...] = jnp.zeros_like(stage)

        copies += send_blocks(stage, keep, send, info[1], sems.at[m], m == 0)
    for copy in copies:
        copy.wait()


def self_backward(info, spans, *refs, items, tokens):
    pieces = refs[:8]
    (
        h_own, low_own, low_oth, q_own, k_own, v_own, q_oth, k_oth, v_oth, grad_first_sum, vectors12, vectors3,
        grad_input, keep, send, grads, full, pull_own, pull_oth, grad_q, grad_k, grad_v, sems, out_sems,
    ) = refs[8:]
    stream = info[2]
    copies = fetch(info, pieces, full, sems, place_self, pl.ds(0, full.shape[3]))
    for copy in copies:
        copy.wait()
    out_weight = stack_rows(full.at[3])
    pull_own[...] = nt(low_own[...], out_weight).astype(BF)
    pull_oth[...] = nt(low_oth[...], out_weight).astype(BF)
    width = h_own.shape[1]
    masks = head_masks(tokens)

    def item(i, carry):
        rows = pl.ds(pl.multiple_of(i * tokens, tokens), tokens)
        valid = valid_keys(spans[i], stream, tokens, 8 * tokens)
        for u in range(width // QUAD):
            lanes = slice(u * QUAD, (u + 1) * QUAD)
            keys = jnp.concatenate([k_own[rows, lanes], k_oth[rows, lanes]], axis=0)
            values = jnp.concatenate([v_own[rows, lanes], v_oth[rows, lanes]], axis=0)
            both = [spread_heads(q[rows, lanes] * BF(SCALE), masks) for q in (q_own, q_oth)]
            queries = jnp.concatenate(both, axis=0)
            pulls = jnp.concatenate([spread_heads(pull[rows, lanes], masks) for pull in (pull_own, pull_oth)], axis=0)
            scores = nt(keys, queries)
            probs = softmax_keys([jnp.where(valid, scores, NEG)])
            (back,) = score_back(probs, [nt(values, pulls)])
            own_probs = probs[0].astype(BF)
            grad_k[rows, lanes] = nn(back[:tokens], queries).astype(BF)
            grad_v[rows, lanes] = nn(own_probs[:tokens], pulls).astype(BF)
            grad_q[rows, lanes] = (collect_heads(tn(back[:, : 4 * tokens], keys)) * SCALE).astype(BF)
        return carry

    lax.fori_loop(0, items, item, 0, unroll=2)
    hidden = h_own[...]
    total = grad_first_sum[...]
    blocks, per = grads.shape[0], width // grads.shape[0]

    def write(at, value):
        value = value.astype(BF)
        for b in range(blocks):
            grads[b, at * per : (at + 1) * per, :] = value[b * per : (b + 1) * per]

    for at, ref in enumerate((grad_q, grad_k, grad_v)):
        value = ref[...]
        write(at, tn(hidden, value))
        total = total + nn(value, stack_rows(full.at[at]))
    tail = grads.shape[1] - 3 * per
    local = width // full.shape[1]
    source = lax.broadcasted_iota(jnp.int32, (width, width), 0)
    target = lax.rem(lax.broadcasted_iota(jnp.int32, (width, width), 1), local)
    lane = lax.broadcasted_iota(jnp.int32, (8, width), 1)

    def spread(vectors, size):
        value = vectors[...].astype(BF)
        parts = [jnp.where(lane // size == p, value, jnp.zeros_like(value)) for p in range(width // size)]
        chosen = jnp.where(lax.rem(source, size) == target, 1.0, 0.0).astype(BF)
        return nn(jnp.concatenate(parts, axis=0), chosen).astype(BF)

    shared, halves = spread(vectors12, per), spread(vectors3, 2 * per)
    for b in range(blocks):
        own = halves[b // 2 * 8 : b // 2 * 8 + 8]
        own = jnp.where(stream == b % 2, own, jnp.zeros_like(own))
        grads[b, 3 * per :, :] = jnp.concatenate([shared[b * 8 : b * 8 + 8], own], axis=0)
    grad_input[...] = total.astype(BF)
    for copy in send_blocks(grads, keep, send, info[1], out_sems, True):
        copy.wait()


VMEM = pl.BlockSpec(memory_space=pltpu.VMEM)
SMEM = pl.BlockSpec(memory_space=pltpu.SMEM)
ANY = pl.BlockSpec(memory_space=pl.ANY)


def shape(dims, kind):
    return jax.ShapeDtypeStruct(tuple(dims), kind)


def call(kernel, out_shapes, specs, scratch, micros, after=(), **more):
    count = len(specs)

    def body(*refs):
        kernel(*refs[:count], *refs[count + len(after) :])

    run = pl.pallas_call(
        body,
        out_shape=out_shapes,
        in_specs=specs + [ANY] * len(after),
        out_specs=more.pop("out_specs", [VMEM] * len(out_shapes)),
        scratch_shapes=scratch,
        compiler_params=pltpu.CompilerParams(vmem_limit_bytes=62 * 1024 * 1024),
        cost_estimate=pl.CostEstimate(flops=int(micros * 1.15e9), bytes_accessed=int(micros * 3.6e6), transcendentals=0),
        **more,
    )
    return lambda *operands: run(*operands, *after)


def pick(array, index, axis):
    return lax.dynamic_index_in_dim(array, index, axis, keepdims=False)


def add(a, b):
    return (a.astype(F32) + b.astype(F32)).astype(BF)


def swap(block, axis, bit=1):
    return lax.ppermute(block, axis, [(i, i ^ bit) for i in range(lax.axis_size(axis))])


def tie(value, *others):
    return jax.tree.map(lambda v: lax.optimization_barrier((v,) + others)[0], value)


def tensor_order(gathered, other, bit):
    upper = jnp.bitwise_and(lax.axis_index("tensor"), bit) != 0
    low, high = jnp.where(upper, other, gathered), jnp.where(upper, gathered, other)
    return jnp.stack([low, high], axis=1).reshape((-1,) + gathered.shape[1:])


def own_piece(pieces):
    pieces = pick(pick(pieces, lax.axis_index("core"), 1), lax.axis_index("stream"), 1)
    if lax.axis_size("node") == 2:
        return [pick(pieces, lax.axis_index("node"), 0)]
    return [pieces[0], pieces[1]]


def halve(pair, axis_name, axis, bit=1):
    keep, arrived = pair
    me = jnp.bitwise_and(lax.axis_index(axis_name) // bit, 1)
    sent = add(pick(keep, 1 - me, axis), pick(arrived, 1 - me, axis))
    kept = add(pick(keep, me, axis), pick(arrived, me, axis))
    return kept, swap(sent, axis_name, bit)


def over_nodes(pair):
    if lax.axis_size("node") == 2:
        return halve(pair, "node", 0)
    total = lax.psum_scatter(add(*pair), "node", scatter_dimension=0, tiled=False)
    return total, jnp.zeros_like(total)


def tensor_step(pair, bit):
    pair = [v.reshape((v.shape[0] // 2, 2) + v.shape[1:]) for v in pair]
    return halve(pair, "tensor", 1, bit)


def finish(pair):
    return (pair[0].astype(F32) + pair[1].astype(F32))[0]


def split_rows(*pairs):
    count, me = lax.axis_size("tensor"), lax.axis_index("tensor")
    rows, columns = sum(pair[0].shape[0] for pair in pairs), pairs[0][0].shape[1]
    half, local = rows // 2, columns // count

    def kernel(bit, *refs):
        *inputs, stays, goes = refs
        totals = [
            (kept[...].astype(F32) + arrived[...].astype(F32)).astype(BF) for kept, arrived in zip(inputs[::2], inputs[1::2])
        ]
        total = jnp.concatenate(totals, axis=0)
        upper = bit[0] == 1
        for p in range(count // 2):
            two = [
                jnp.concatenate([total[:half, t * local : (t + 1) * local], total[half:, t * local : (t + 1) * local]], axis=1)
                for t in (2 * p, 2 * p + 1)
            ]
            stays[p] = jnp.where(upper, two[1], two[0])
            goes[p] = jnp.where(upper, two[0], two[1])

    outs = [shape((count // 2, half, 2 * local), BF)] * 2
    bit = jnp.bitwise_and(me, 1).reshape(1)
    operands = [v for pair in pairs for v in pair]
    stays, goes = call(kernel, outs, [SMEM] + [VMEM] * len(operands), [], 1, name="split_rows")(bit, *operands)
    return stays, swap(goes, "tensor", 1)


def finish_rows(plain, *packs):
    local = packs[0][0][0].shape[2] // 2

    def kernel(*refs):
        inputs, outs = refs[: 2 + 2 * len(packs)], refs[2 + 2 * len(packs) :]
        outs[0][...] = inputs[0][0].astype(F32) + inputs[1][0].astype(F32)
        at = 1
        for p, (_, sizes) in enumerate(packs):
            both = inputs[2 + 2 * p][0].astype(F32) + inputs[3 + 2 * p][0].astype(F32)
            total = jnp.concatenate([both[:, :local], both[:, local:]], axis=0)
            start = 0
            for size in sizes:
                outs[at][...] = total[start : start + size]
                start += size
                at += 1

    outs = [shape(plain[0].shape[1:], F32)] + [shape((size, local), F32) for _, sizes in packs for size in sizes]
    operands = [*plain, *(v for pair, _ in packs for v in pair)]
    return call(kernel, outs, [VMEM] * len(operands), [], 1, name="finish_rows")(*operands)


def shards(
    hidden_in, lengths, image_features, self_q, self_k, self_v, self_out, ln1_gain, ln1_bias,
    cross_q, cross_k, cross_v, cross_out, ln2_gain, ln2_bias, ffn_up, ffn_down, ln3_gain, ln3_bias, cotangent,
):
    nodes, streams, count = lax.axis_size("node"), lax.axis_size("stream"), lax.axis_size("tensor")
    node, core = lax.axis_index("node"), lax.axis_index("core")
    stream, me = lax.axis_index("stream"), lax.axis_index("tensor")
    devices = nodes * 2
    rows_all, width = hidden_in.shape[1:]
    local = self_q.shape[1]
    image_tokens, image_width = image_features.shape[1:]
    patches = image_tokens - 1
    items = lengths.shape[0] // count
    rows = rows_all // count
    tokens = rows // items
    info = jnp.stack([node if nodes == 2 else jnp.int32(0), core, stream, me]).astype(jnp.int32)

    self_pieces = jnp.stack([self_q.T, self_k.T, self_v.T, self_out.T]).reshape(2, 2, 2, local // 2, width)
    small_pieces = jnp.stack([cross_q.T, cross_out.T]).reshape(2, 2, 2, local // 4, width)
    image_pieces = jnp.stack([cross_k.T, cross_v.T]).reshape(2, 2, 2, local // 4, image_width)
    h_own = lax.dynamic_slice_in_dim(hidden_in[0], me * rows, rows, 0)
    h_oth = lax.ppermute(h_own, "stream", SWAP)
    spans = lax.dynamic_slice_in_dim(lengths, me * items, items, 0)
    cot = lax.dynamic_slice_in_dim(cotangent[0], me * rows, rows, 0)
    image = lax.dynamic_slice_in_dim(image_features, me * items, items, 0)
    x = image[:, :patches].reshape(items * patches, image_width)
    x_last = image[:, patches]

    z = lambda vs, bit: [swap(v, "tensor", bit) for v in vs]
    join = lambda a, b: [jnp.concatenate([v, w]) for v, w in zip(a, b)]
    nodes_too = lambda vs: vs + [swap(vs[0], "node")] if nodes == 2 else vs
    cores_too = lambda vs: vs + [swap(v, "core") for v in vs]
    one_way = lambda v: lax.ppermute(v, "stream", [(1, 0)])
    image_0 = [v[None] for v in own_piece(image_pieces)]
    self_0 = [v[None] for v in own_piece(jnp.concatenate([self_pieces, small_pieces], axis=3))]
    ffn_share = 4 if nodes == 2 else 2
    ffn_rows = jnp.concatenate([ffn_up[0], ffn_down[0]], axis=0).reshape(ffn_share, 1, 2 * width // ffn_share, -1)
    ffn_own = pick(ffn_rows, node * 2 + core if nodes == 2 else core, 0)
    ffn_0 = [ffn_own]

    image_1 = z(image_0, 2)
    image_2 = join(tie(image_0, h_oth), image_1)
    image_3 = z(image_2, 1)
    self_1 = z(tie(self_0, *image_1), 2)
    image_4 = join(image_2, image_3)
    image_near = nodes_too(image_4)
    image_side = [one_way(image_near[0])]
    self_2 = join(tie(self_0, x, *image_4), self_1)
    self_3 = z(self_2, 1)
    ffn_1 = z(tie(ffn_0, *self_1, *image_4), 2)
    image_side.append(one_way(tie(image_near[1], image_side[0])))
    self_4 = join(self_2, self_3)
    self_near = nodes_too(tie(self_4, image_near[1], image_side[0]))
    image_full = cores_too(image_near + image_side)
    self_side = [swap(tie(self_near[0], image_side[1]), "stream")]

    act_low, act = shape((rows, width), BF), shape((rows, width), F32)
    image_kv, image_kv_last = shape((items * patches, width), BF), shape((items, width), BF)
    dma = pltpu.SemaphoreType.DMA
    self_scratch = pltpu.VMEM((4, count, 2, local // 2, width), BF)
    small_scratch = pltpu.VMEM((2, count, 4, local // 4, width), BF)
    image_scratch = pltpu.VMEM((2, count, 4, local // 4, image_width), BF)
    image_vmem = pltpu.VMEM((items * patches, width), BF)
    row = lambda v: v.reshape(1, width)

    image_keys, image_values, keys_last, values_last = call(
        image_forward,
        [image_kv] * 2 + [image_kv_last] * 2,
        [SMEM] + [ANY] * 8 + [pl.BlockSpec((patches, image_width), lambda i: (i, 0)), pl.BlockSpec((items, image_width), lambda i: (0, 0))],
        [image_scratch, dma((8, count))],
        3,
        after=(),
        grid=(items,),
        out_specs=[pl.BlockSpec((patches, width), lambda i: (i, 0))] * 2 + [pl.BlockSpec((items, width), lambda i: (0, 0))] * 2,
        name="image_forward",
    )(info, *image_full, x, x_last)

    self_side.append(swap(tie(self_near[1], image_keys, self_side[0], *ffn_1), "stream"))
    ffn_2 = join(tie(ffn_0, image_keys), ffn_1)
    ffn_3 = z(ffn_2, 1)
    ffn_near, ffn_late = nodes_too(ffn_2), nodes_too(ffn_3)
    self_full = cores_too(self_near + self_side)

    (
        q_own, k_own, v_own, q_oth, k_oth, v_oth, mix, first_sum, first, cross_queries, cross_mix, second_sum, second,
    ) = call(
        functools.partial(forward, items=items, tokens=tokens, patches=patches),
        [act_low] * 7 + [act] * 2 + [act_low] * 2 + [act] * 2,
        [SMEM, SMEM] + [ANY] * 8 + [VMEM] * 2 + [ANY] * 2 + [VMEM] * 6,
        [self_scratch, small_scratch, image_vmem, image_vmem, dma((8, count)), dma((8, count)), dma((2,))],
        5,
        after=tuple(ffn_3),
        name="forward",
    )(
        info, spans, *self_full, h_own, h_oth, image_keys, image_values, keys_last, values_last,
        row(ln1_gain), row(ln1_bias), row(ln2_gain), row(ln2_bias),
    )

    ffn_late = ffn_late[:-1] + [tie(ffn_late[-1], second)]
    ffn_full = cores_too(ffn_near) + cores_too(ffn_late)
    ffn_pieces = len(ffn_near) * 2
    half_grads = [shape((nodes, count, width // devices, width), BF)] * 2
    output, grad_second, vectors3, keep_down, send_down, keep_up, send_up = call(
        functools.partial(ffn_both, pieces=ffn_pieces),
        [act_low, act, shape((8, width), F32)] + half_grads * 2,
        [SMEM] + [ANY] * (2 * ffn_pieces) + [VMEM] * 4,
        [
            pltpu.VMEM((count, ffn_share, 2 * width // ffn_share, width), BF),
            pltpu.VMEM((count, rows, width), F32),
            pltpu.VMEM((count, rows, width), BF),
            pltpu.VMEM((2 * count, devices, width // devices, width), BF),
            dma((count, ffn_pieces)),
            dma((2 * count, 2 * nodes)),
        ],
        5,
        out_specs=[VMEM] * 3 + [ANY] * 4,
        name="ffn_both",
    )(info, *ffn_full, second, cot, ln3_gain, ln3_bias)
    down_core = keep_down, swap(send_down, "core")
    up_core = keep_up, swap(send_up, "core")
    output_1 = swap(output[None], "tensor", 2)
    down_nodes = over_nodes(down_core)
    blocks = devices * streams
    per, image_per, wide_per = width // blocks, image_width // blocks, width // devices
    tail = 16
    halves_of = lambda r, first=streams, then=nodes: [shape((first, then, r, width), BF)] * 2

    grad_keys, grad_values, grad_keys_last, grad_values_last, grad_first_sum, low_own, vectors12, keep_square, send_square = call(
        functools.partial(cross_backward, items=items, tokens=tokens, patches=patches),
        [
            image_kv, image_kv, shape((items, width), F32), shape((items, width), F32), act, act_low, shape((8, width), F32),
            *halves_of(3 * per),
        ],
        [SMEM] + [ANY] * 8 + [VMEM] * 13,
        [
            small_scratch, pltpu.VMEM((rows, width), BF), pltpu.VMEM((rows, width), BF),
            pltpu.VMEM((blocks, 3 * per, width), BF), dma((8, count)), dma((2, nodes * streams)),
        ],
        5,
        after=(down_nodes[0],),
        out_specs=[VMEM] * 7 + [ANY] * 2,
        name="cross_backward",
    )(
        info, *self_full, grad_second, second_sum, first, first_sum, mix, cross_queries, cross_mix, image_keys, image_values,
        keys_last, values_last, row(ln2_gain), row(ln1_gain),
    )
    ended = output_1, down_nodes[1], up_core[1]
    low_oth = swap(tie(low_own, *ended), "stream")
    square_core = keep_square, swap(tie(send_square, *ended), "core")
    output_2 = tensor_order(tie(output[None], low_own), output_1, 2)
    output_3 = swap(output_2, "tensor", 1)
    up_nodes = over_nodes(tie(up_core, low_own))
    down_half = tensor_step(tie(down_nodes, low_own), 1)
    square_stream = halve(tie(square_core, low_oth), "stream", 0)
    grad_input, keep_self, send_self = call(
        functools.partial(self_backward, items=items, tokens=tokens),
        [act_low] + halves_of(3 * per + tail),
        [SMEM, SMEM] + [ANY] * 8 + [VMEM] * 12,
        [pltpu.VMEM((blocks, 3 * per + tail, width), BF), self_scratch]
        + [pltpu.VMEM((rows, width), BF)] * 5
        + [dma((8, count)), dma((2, nodes * streams))],
        3,
        out_specs=[VMEM] + [ANY] * 2,
        after=(up_nodes[0], down_half[0], square_stream[0], output_2),
        name="self_backward",
    )(info, spans, *self_full, h_own, low_own, low_oth, q_own, k_own, v_own, q_oth, k_oth, v_oth, grad_first_sum, vectors12, vectors3)

    ended = up_nodes[1], down_half[1], square_stream[1], output_3
    self_core = keep_self, swap(tie(send_self, *ended), "core")
    up_half = tensor_step(tie(up_nodes, grad_input), 1)
    grad_1 = swap(grad_input[None], "tensor", 2)
    square_nodes = over_nodes(tie(square_stream, grad_input))
    self_stream = halve(self_core, "stream", 0)
    keep_keys, send_keys, keep_values, send_values = call(
        image_backward,
        halves_of(image_per) + halves_of(image_per, nodes, streams),
        [SMEM] + [VMEM] * 6,
        [pltpu.VMEM((blocks, image_per, width), BF)] * 2 + [dma((2, 2, nodes * streams))],
        5,
        after=(self_stream[0], square_nodes[0], up_half[0]),
        out_specs=[ANY] * 4,
        name="image_backward",
    )(info, x, x_last, grad_keys, grad_keys_last, grad_values, grad_values_last)

    ended = up_half[1], grad_1, square_nodes[1], self_stream[1]
    keys_stream = halve((keep_keys, swap(tie(send_keys, *ended), "core")), "stream", 0)
    values_nodes = over_nodes((keep_values, swap(tie(send_values, *ended), "core")))
    step = values_nodes[0]
    grad_2 = tensor_order(tie(grad_input[None], step), grad_1, 2)
    grad_3 = swap(grad_2, "tensor", 1)
    down_quarter = tensor_step(tie(down_half, step), 2)
    self_nodes = over_nodes(tie(self_stream, step, keys_stream[0]))
    square_half = split_rows(tie(square_nodes, step))
    keys_nodes = over_nodes(keys_stream)
    values_stream = halve(values_nodes, "stream", 0)
    step = values_stream[0]
    image_half = split_rows(keys_nodes, values_stream)
    self_half = split_rows(tie(self_nodes, step))
    up_quarter = tensor_step(tie(up_half, step), 2)
    step = image_half[0]
    square_quarter = tensor_step(tie(square_half, step), 2)
    output_4 = tensor_order(tie(output_2, step), output_3, 1)
    down_sum = finish(tie(down_quarter, step))
    self_quarter = tensor_step(tie(self_half, step), 2)
    image_quarter = tensor_step(image_half, 2)
    grad_input = tensor_order(tie(grad_2, step), grad_3, 1)
    up_sum, self_q, self_k, self_v, vectors, square_q, square_o, self_o, image_k, image_v = finish_rows(
        up_quarter,
        (self_quarter, (per, per, per, tail)),
        (square_quarter, (per, per, per)),
        (image_quarter, (image_per, image_per)),
    )

    vector = lambda r, n: vectors[r, :n]
    return (
        output_4.reshape(1, rows_all, width),
        grad_input.reshape(1, rows_all, width),
        self_q,
        self_k,
        self_v,
        self_o,
        vector(0, per),
        vector(1, per),
        square_q,
        image_k,
        image_v,
        square_o,
        vector(2, per),
        vector(3, per),
        up_sum[None],
        down_sum[None],
        vector(8, wide_per)[None],
        vector(9, wide_per)[None],
    )


def solution(mesh):
    sizes = mesh.devices.shape
    fine = Mesh(mesh.devices.reshape(sizes[0] // 2, 2, *sizes[1:]), ("node", "core", "stream", "tensor"))
    weight = P(None, "tensor")
    in_specs = (
        P("stream", DP, None), P(DP), P(DP, None, None), weight, weight, weight, weight, P(), P(),
        weight, weight, weight, weight, P(), P(), P("stream", None, "tensor"), P("stream", None, "tensor"),
        P("stream", None), P("stream", None), P("stream", DP, None),
    )
    over = ("node", "core", "stream")
    square, flat = P(over, "tensor"), P(over)
    out_specs = (
        P("stream", DP, None), P("stream", DP, None), square, square, square, square, flat, flat,
        square, square, square, square, flat, flat, P("stream", DP, "tensor"), P("stream", DP, "tensor"),
        P("stream", DP), P("stream", DP),
    )
    return jax.shard_map(shards, mesh=fine, in_specs=in_specs, out_specs=out_specs, check_vma=False)
```
